32 devices in a mesh: dp: 8 (over z, x), tensor: 4 (over y, core).
Axes of the slice: x: 2, y: 2, z: 4, core: 2. Of those that a mesh axis runs over, the one named last changes fastest.
Arguments:
- token_ids: int32 [16, 1024], P('dp', 'tensor'), may hold values from 0 to 32
- mask_pos: int32 [16, 160], P('dp'), may hold values from 0 to 1023, as said below
- mask_target: int32 [16, 160], P('dp'), may hold values from 0 to 32
- mask_count: int32 [16], P('dp'), may hold values from 1 to 160, as said below
- weight_in: float32 [2, 480, 1440], P(None, 'dp', 'tensor'), may hold values from -0.25 to 0.25
- weight_out: float32 [2, 480, 480], P(None, 'tensor', 'dp'), may hold values from -6 to 6
- weight_up: float32 [2, 480, 1920], P(None, 'dp', 'tensor'), may hold values from -0.25 to 0.25
- weight_down: float32 [2, 1920, 480], P(None, 'tensor', 'dp'), may hold values from -0.125 to 0.125
- norm_params: float32 [10, 480], replicated, may hold values from -2 to 2, as said below
- vocab_table: float32 [33, 480], replicated, may hold values from -0.6 to 0.6
- first_in: float32 [2, 480, 1440], P(None, 'dp', 'tensor'), may hold values from -0.0078125 to 0.0078125
- first_out: float32 [2, 480, 480], P(None, 'tensor', 'dp'), may hold values from -0.0078125 to 0.0078125
- first_up: float32 [2, 480, 1920], P(None, 'dp', 'tensor'), may hold values from -0.0078125 to 0.0078125
- first_down: float32 [2, 1920, 480], P(None, 'tensor', 'dp'), may hold values from -0.0078125 to 0.0078125
- first_norm: float32 [10, 480], replicated, may hold values from -0.25 to 0.25
- first_vocab: float32 [33, 480], replicated, may hold values from -0.25 to 0.25
- second_in: float32 [2, 480, 1440], P(None, 'dp', 'tensor'), may hold values from 1.9929846e-06 to 7.971938e-06
- second_out: float32 [2, 480, 480], P(None, 'tensor', 'dp'), may hold values from 1.9929846e-06 to 7.971938e-06
- second_up: float32 [2, 480, 1920], P(None, 'dp', 'tensor'), may hold values from 1.9929846e-06 to 7.971938e-06
- second_down: float32 [2, 1920, 480], P(None, 'tensor', 'dp'), may hold values from 1.9929846e-06 to 7.971938e-06
- second_norm: float32 [10, 480], replicated, may hold values from 0.00390625 to 0.015625
- second_vocab: float32 [33, 480], replicated, may hold values from 0.00390625 to 0.015625
Outputs:
- loss_total: float32 [], replicated
- mask_total: float32 [], replicated
- master_in: float32 [2, 480, 1440], P(None, 'dp', 'tensor')
- master_out: float32 [2, 480, 480], P(None, 'tensor', 'dp')
- master_up: float32 [2, 480, 1920], P(None, 'dp', 'tensor')
- master_down: float32 [2, 1920, 480], P(None, 'tensor', 'dp')
- master_norm: float32 [10, 480], replicated
- master_vocab: float32 [33, 480], replicated
- mean_in: float32 [2, 480, 1440], P(None, 'dp', 'tensor')
- mean_out: float32 [2, 480, 480], P(None, 'tensor', 'dp')
- mean_up: float32 [2, 480, 1920], P(None, 'dp', 'tensor')
- mean_down: float32 [2, 1920, 480], P(None, 'tensor', 'dp')
- mean_norm: float32 [10, 480], replicated
- mean_vocab: float32 [33, 480], replicated
- square_in: float32 [2, 480, 1440], P(None, 'dp', 'tensor')
- square_out: float32 [2, 480, 480], P(None, 'tensor', 'dp')
- square_up: float32 [2, 480, 1920], P(None, 'dp', 'tensor')
- square_down: float32 [2, 1920, 480], P(None, 'tensor', 'dp')
- square_norm: float32 [10, 480], replicated
- square_vocab: float32 [33, 480], replicated
- copy_in: bfloat16 [2, 480, 1440], P(None, 'dp', 'tensor')
- copy_out: bfloat16 [2, 480, 480], P(None, 'tensor', 'dp')
- copy_up: bfloat16 [2, 480, 1920], P(None, 'dp', 'tensor')
- copy_down: bfloat16 [2, 1920, 480], P(None, 'tensor', 'dp')
- copy_vocab: bfloat16 [33, 480], replicated
The draws below stay inside these ranges and needn't reach their ends.
Inputs may be any that keep to these rules, and one draw needn't show every extreme that they name: `mask_pos`: positions within one sequence; the 160 slots of a sequence name distinct positions. `mask_count`: slots below a sequence's count are live, the others are ignored; the last sequence has all 160 live. `norm_params`: even rows near one, odd rows of both signs.
All inputs are finite; a program needn't handle non-finite values.
Results may differ from the reference program's by a relative error of at most 0.0016.
The reference program's roundings to bfloat16 on the way count: a program that leaves them out, or rounds other values in their place, can miss the bound.
Values may be sent and summed in bfloat16 or wider, within the bound.
No kernel may reach another device: no remote copies, remote signals or barrier semaphores. Data moves between devices by JAX's collectives and lax.ppermute only.
A program may use at most 320 MiB of HBM per device.

```python
import math
import jax
import jax.numpy as jnp
from jax import lax

D = 480
HEADS = 20
HEAD = 24
FF = 1920
VOCAB = 33
LAYERS = 2
LENGTH = 1024
MSLOT = 160
STEP = 5
SEQS = 16
NORMS = 10
N_TENSOR = 4


def draw_mask_pos(key, part):
    key = jax.random.fold_in(key, 3)
    quarter = LENGTH // N_TENSOR
    triangle = N_TENSOR * (N_TENSOR + 1) // 2

    def lone_token_entry(row_key):
        pieces = []
        placed = 0
        for segment in range(N_TENSOR):
            if segment < N_TENSOR - 1:
                amount = max(MSLOT * (segment + 1) // triangle, 1)
            else:
                amount = MSLOT - placed
            placed = placed + amount
            order = jax.random.permutation(jax.random.fold_in(row_key, segment), quarter)
            pieces.append(order[:amount].astype(jnp.int32) + segment * quarter)
        concatenated_parts = jnp.concatenate(pieces)
        shuffle = jax.random.permutation(jax.random.fold_in(row_key, 977), MSLOT)
        return concatenated_parts[shuffle]
    row_keys = jax.random.split(key, SEQS)
    return jax.vmap(lone_token_entry)(row_keys).astype(jnp.int32)


def draw_mask_count(key, part):
    key = jax.random.fold_in(key, 5)
    rows = jnp.arange(SEQS, dtype=jnp.int32)
    lowest = MSLOT // 3
    base = lowest + (MSLOT - lowest) * rows // max(SEQS - 1, 1)
    jitter = jax.random.randint(key, (SEQS,), 0, MSLOT // 8 + 1)
    counts = jnp.maximum(base - jitter, 1)
    return jnp.where(rows == SEQS - 1, MSLOT, counts).astype(jnp.int32)


def draw_norm_params(key, part):
    key = jax.random.fold_in(key, 7)
    parity = jnp.arange(NORMS)[:, None] % 2
    gains = 1.0 + 0.3 * jax.random.uniform(key, (NORMS, D), jnp.float32, -1.0, 1.0)
    shifts = jnp.clip(0.3 * jax.random.normal(jax.random.fold_in(key, 1), (NORMS, D), jnp.float32), -1.5, 1.5)
    return jnp.where(parity == 0, gains, shifts).astype(jnp.float32)


def touch_ends(drawn, stream_key, smallest, high):
    place = [jax.random.randint(jax.random.fold_in(stream_key, axis), (), 0, length) for axis, length in enumerate(drawn.shape)]
    widest = drawn.shape.index(max(drawn.shape))
    next_to = place[:widest] + [(place[widest] + 1) % drawn.shape[widest]] + place[widest + 1:]
    return drawn.at[tuple(place)].set(smallest).at[tuple(next_to)].set(high)


def levels(rng, extent, shards, least, top_value):
    level = 1.0
    for axis_at, shards_of in shards:
        draws = jax.random.uniform(jax.random.fold_in(jax.random.fold_in(rng, 6), axis_at), (shards_of,), jnp.float32, least / len(shards), top_value / len(shards))
        level = level * jnp.repeat(jnp.exp(draws), extent[axis_at] // shards_of).reshape((-1,) + (1,) * (len(extent) - 1 - axis_at))
    return level


def normal_values(stream_key, shape, width, reach, cuts=(), held_as=jnp.bfloat16):
    array = width * jax.random.normal(stream_key, shape, jnp.float32)
    if cuts:
        array = array * levels(stream_key, shape, cuts, -0.22, 0.18)
    return jnp.clip(array, -reach, reach).astype(held_as)


def setup_inputs(seed: int = 0) -> dict:
    streams_of = jax.random.split(jax.random.key(seed), 23)
    return {
        "token_ids": touch_ends(jax.random.randint(streams_of[0], (SEQS, LENGTH), 0, VOCAB), jax.random.fold_in(streams_of[0], 1), 0, VOCAB - 1).astype(jnp.int32),
        "mask_pos": draw_mask_pos(jax.random.fold_in(streams_of[22], 71), 0),
        "mask_target": touch_ends(jax.random.randint(streams_of[2], (SEQS, MSLOT), 0, VOCAB), jax.random.fold_in(streams_of[2], 1), 0, VOCAB - 1).astype(jnp.int32),
        "mask_count": draw_mask_count(jax.random.fold_in(streams_of[22], 71), 0),
        "weight_in": normal_values(streams_of[4], (LAYERS, D, 3 * D), D ** -0.5, 0.25, ((1, 8), (2, 4)), jnp.float32),
        "weight_out": normal_values(streams_of[5], (LAYERS, D, D), (max(D // 256, 1)) ** -0.5, 6.0, ((1, 4), (2, 8)), jnp.float32),
        "weight_up": normal_values(streams_of[6], (LAYERS, D, FF), D ** -0.5, 0.25, ((1, 8), (2, 4)), jnp.float32),
        "weight_down": normal_values(streams_of[7], (LAYERS, FF, D), FF ** -0.5, 0.125, ((1, 4), (2, 8)), jnp.float32),
        "norm_params": draw_norm_params(jax.random.fold_in(streams_of[22], 71), 0),
        "vocab_table": normal_values(streams_of[9], (VOCAB, D), 0.1, 0.6, (), jnp.float32),
        "first_in": normal_values(streams_of[10], (LAYERS, D, 3 * D), ((196 * MSLOT * SEQS) ** -0.5), 0.0078125, ((1, 8), (2, 4)), jnp.float32),
        "first_out": normal_values(streams_of[11], (LAYERS, D, D), ((196 * MSLOT * SEQS) ** -0.5), 0.0078125, ((1, 4), (2, 8)), jnp.float32),
        "first_up": normal_values(streams_of[12], (LAYERS, D, FF), ((196 * MSLOT * SEQS) ** -0.5), 0.0078125, ((1, 8), (2, 4)), jnp.float32),
        "first_down": normal_values(streams_of[13], (LAYERS, FF, D), ((196 * MSLOT * SEQS) ** -0.5), 0.0078125, ((1, 4), (2, 8)), jnp.float32),
        "first_norm": normal_values(streams_of[14], (NORMS, D), ((0.2 * MSLOT * SEQS) ** -0.5), 0.25, (), jnp.float32),
        "first_vocab": normal_values(streams_of[15], (VOCAB, D), ((0.2 * MSLOT * SEQS) ** -0.5), 0.25, (), jnp.float32),
        "second_in": jnp.clip(jnp.exp(math.log(7.97193843027344e-06) - 1.3862944 * jax.random.uniform(streams_of[16], (LAYERS, D, 3 * D), jnp.float32) ** levels(streams_of[16], (LAYERS, D, 3 * D), ((1, 8), (2, 4)), -0.2, 0.2)), 1.99298460756836e-06, 7.97193843027344e-06),
        "second_out": jnp.clip(jnp.exp(math.log(7.97193843027344e-06) - 1.3862944 * jax.random.uniform(streams_of[17], (LAYERS, D, D), jnp.float32) ** levels(streams_of[17], (LAYERS, D, D), ((1, 4), (2, 8)), -0.2, 0.2)), 1.99298460756836e-06, 7.97193843027344e-06),
        "second_up": jnp.clip(jnp.exp(math.log(7.97193843027344e-06) - 1.3862944 * jax.random.uniform(streams_of[18], (LAYERS, D, FF), jnp.float32) ** levels(streams_of[18], (LAYERS, D, FF), ((1, 8), (2, 4)), -0.2, 0.2)), 1.99298460756836e-06, 7.97193843027344e-06),
        "second_down": jnp.clip(jnp.exp(math.log(7.97193843027344e-06) - 1.3862944 * jax.random.uniform(streams_of[19], (LAYERS, FF, D), jnp.float32) ** levels(streams_of[19], (LAYERS, FF, D), ((1, 4), (2, 8)), -0.2, 0.2)), 1.99298460756836e-06, 7.97193843027344e-06),
        "second_norm": jnp.clip(jnp.exp(jax.random.uniform(streams_of[20], (NORMS, D), jnp.float32, math.log(0.00390625), math.log(0.015625))), 0.00390625, 0.015625),
        "second_vocab": jnp.clip(jnp.exp(jax.random.uniform(streams_of[21], (VOCAB, D), jnp.float32, math.log(0.00390625), math.log(0.015625))), 0.00390625, 0.015625),
    }


@jax.custom_vjp
def low(v):
    return lax.optimization_barrier(v.astype(jnp.bfloat16)).astype(jnp.float32)

@jax.custom_vjp
def low_back(v):
    return v

def low_keep(v):
    return (low(v), None)

def low_pass(kept, grad):
    return (grad,)

def back_keep(v):
    return (v, None)

def back_low(kept, grad):
    return (low(grad),)
low.defvjp(low_keep, low_pass)
low_back.defvjp(back_keep, back_low)
norm_eps = 1e-05
step_rates = (0.02, 0.3, 0.02, 0.02, 0.3, 0.05)
beta_first = 0.5
beta_second = 0.5
adam_eps = 1e-08
weight_decay = 0.01
highest = lax.Precision.HIGHEST

def normalize_features(resid, gain, shift):
    centre = resid - lax.optimization_barrier(jnp.mean(resid, -1, keepdims=True))
    spread = lax.optimization_barrier(jnp.mean(centre * centre, -1, keepdims=True))
    return centre * lax.rsqrt(spread + norm_eps) * gain + shift

def rotary_tables(length, size):
    half_size = size // 2
    freqs = 10000.0 ** (-jnp.arange(half_size, dtype=jnp.float32) * 2.0 / size)
    angles = jnp.arange(length, dtype=jnp.float32)[:, None] * freqs[None, :]
    return (jnp.cos(angles), jnp.sin(angles))

def rotate(values, cosine, sine):
    half_size = values.shape[-1] // 2
    first, second = (values[..., :half_size], values[..., half_size:])
    return jnp.concatenate([first * cosine - second * sine, second * cosine + first * sine], -1)

def sequence_loss(rounded, tokens_row, pos_row, target_row, live_row):
    input_matrix, projection_result, up_matrix, down_matrix, norms, table = rounded
    token_hot = (tokens_row[:, None] == jnp.arange(VOCAB)[None, :]).astype(jnp.float32)
    resid = jnp.dot(token_hot, table, precision=highest)
    cosine, sine = rotary_tables(LENGTH, HEAD)
    cosine, sine = (cosine[:, None, :], sine[:, None, :])
    for layer_at in range(LAYERS):
        normed = low(normalize_features(resid, norms[4 * layer_at], norms[4 * layer_at + 1]))
        packed_rows = low_back(jnp.dot(normed, input_matrix[layer_at], precision=highest)).reshape(LENGTH, HEADS, 3, HEAD)
        query = low(rotate(packed_rows[:, :, 0], cosine, sine))
        keys = low(rotate(packed_rows[:, :, 1], cosine, sine))
        values = low(packed_rows[:, :, 2])
        scores = low_back(jnp.einsum('qhe,khe->hqk', query, keys, precision=highest) * HEAD ** (-0.5))
        probs = jax.nn.softmax(scores, -1)
        blended_tokens = jnp.einsum('hqk,khe->qhe', low(probs), values, precision=highest)
        blended_tokens = low(low_back(blended_tokens.reshape(LENGTH, D)))
        resid = resid + low_back(jnp.dot(blended_tokens, projection_result[layer_at], precision=highest))
        normed = low(normalize_features(resid, norms[4 * layer_at + 2], norms[4 * layer_at + 3]))
        hidden_state = low_back(jnp.dot(normed, up_matrix[layer_at], precision=highest))
        active_rows = low(jax.nn.gelu(hidden_state, approximate=False))
        resid = resid + low_back(jnp.dot(active_rows, down_matrix[layer_at], precision=highest))
    final = low(normalize_features(resid, norms[4 * LAYERS], norms[4 * LAYERS + 1]))
    picked = final[pos_row]
    logits = low_back(jnp.dot(picked, table.T, precision=highest))
    peak = lax.optimization_barrier(jnp.max(logits, -1, keepdims=True))
    logsum = peak[:, 0] + jnp.log(lax.optimization_barrier(jnp.sum(jnp.exp(logits - peak), -1)))
    target_hot = (target_row[:, None] == jnp.arange(VOCAB)[None, :]).astype(jnp.float32)
    target_logit = lax.optimization_barrier(jnp.sum(logits * target_hot, -1))
    return jnp.sum((logsum - target_logit) * live_row)

def adamw(master, first, second, grad, step_rate):
    mean = beta_first * first + (1.0 - beta_first) * grad
    square = beta_second * second + (1.0 - beta_second) * grad * grad
    corrected = mean / (1.0 - beta_first ** STEP)
    rescaled_values = square / (1.0 - beta_second ** STEP)
    fresh = master - step_rate * (corrected / (jnp.sqrt(rescaled_values) + adam_eps) + weight_decay * master)
    return (fresh, mean, square)

def reference(token_ids, mask_pos, mask_target, mask_count, weight_in, weight_out, weight_up, weight_down, norm_params, vocab_table, first_in, first_out, first_up, first_down, first_norm, first_vocab, second_in, second_out, second_up, second_down, second_norm, second_vocab):
    live = (jnp.arange(MSLOT)[None, :] < mask_count[:, None]).astype(jnp.float32)
    count_total = jnp.sum(mask_count).astype(jnp.float32)
    masters = (weight_in, weight_out, weight_up, weight_down, norm_params, vocab_table)
    per_sequence = jax.checkpoint(sequence_loss)

    def total_loss(params):
        rounded = (low(params[0]), low(params[1]), low(params[2]), low(params[3]), params[4], low(params[5]))

        def accumulate(carry, row):
            return (carry + per_sequence(rounded, row[0], row[1], row[2], row[3]), None)
        summed, _ = lax.scan(accumulate, jnp.zeros((), jnp.float32), (token_ids, mask_pos, mask_target, live))
        return summed
    loss_total, pullback = jax.vjp(total_loss, masters)
    grads = pullback(1.0 / count_total)[0]
    firsts = (first_in, first_out, first_up, first_down, first_norm, first_vocab)
    elapsed_time = (second_in, second_out, second_up, second_down, second_norm, second_vocab)
    results = [adamw(masters[which], firsts[which], elapsed_time[which], grads[which], step_rates[which]) for which in range(6)]
    news = [entry[0] for entry in results]
    means = [entry[1] for entry in results]
    squares = [entry[2] for entry in results]
    copies = [news[which].astype(jnp.bfloat16) for which in (0, 1, 2, 3, 5)]
    return (loss_total, count_total, news[0], news[1], news[2], news[3], news[4], news[5], means[0], means[1], means[2], means[3], means[4], means[5], squares[0], squares[1], squares[2], squares[3], squares[4], squares[5], copies[0], copies[1], copies[2], copies[3], copies[4])
```

```python
import functools
import math

import jax
import jax.numpy as jnp
from jax import lax
from jax.experimental import pallas as pl
from jax.experimental.pallas import tpu as pltpu
from jax.sharding import PartitionSpec as P

HEAD = 24
STEP = 5
LANES = 128
TABLE_ROWS = 40
LOSS_ROW = 10
VMEM_BYTES = 60 * 1024 * 1024

norm_eps = 1e-05
step_rates = (0.02, 0.3, 0.02, 0.02, 0.3, 0.05)
beta_first = 0.5
beta_second = 0.5
adam_eps = 1e-08
weight_decay = 0.01
highest = lax.Precision.HIGHEST
brain = jnp.bfloat16
single = jnp.float32
scale = HEAD ** (-0.5)
scale_two = scale * math.log2(math.e)

params = functools.partial(pltpu.CompilerParams, vmem_limit_bytes=VMEM_BYTES)


def cost(micros):
    return pl.CostEstimate(flops=int(micros * 1.1e9), bytes_accessed=0, transcendentals=0)


class Cube:
    def __init__(self, groups, tensors):
        self.groups = groups
        self.tensors = tensors
        self.devices = groups * tensors
        self.size = self.devices.bit_length() - 1
        self.masks = [1 << at for at in range(self.size)]
        self.folded = groups >= 4
        if self.folded:
            self.masks[-1] |= self.masks[-2]

    def swap(self, x, at):
        mask = self.masks[at]
        pairs = [(device, device ^ mask) for device in range(self.devices)]
        return lax.ppermute(x, ("dp", "tensor"), pairs)

    def outer(self, turn):
        rest = list(range(1, self.size))
        rest = rest[1:2] + rest[:1] + rest[2:]
        turn = turn % len(rest)
        return rest[turn:] + rest[:turn]

    def steps(self, offset):
        bits = [(offset >> at) & 1 for at in range(self.size)]
        if self.folded:
            bits[-2] = bits[-2] ^ bits[-1]
        return bits

    def gather(self, x, order):
        held = x[None]
        for at in order:
            held = jnp.concatenate([held, self.swap(held, at)], 0)
        return held

    def slot(self, offset, order):
        bits = self.steps(offset)
        place = 0
        for rank, at in enumerate(order):
            place = place + (bits[at] << rank)
        return place


def dot(left, right, left_dim=1, right_dim=0):
    return lax.dot_general(
        left, right, (((left_dim,), (right_dim,)), ((), ())), preferred_element_type=single
    )


def split_three(x):
    high = x.astype(brain)
    rest = x - high.astype(single)
    middle = rest.astype(brain)
    return high, middle, (rest - middle.astype(single)).astype(brain)


def dot_exact(hot, x, left_dim=1, right_dim=0):
    high, middle, low = split_three(x)
    tail = dot(hot, middle, left_dim, right_dim) + dot(hot, low, left_dim, right_dim)
    return dot(hot, high, left_dim, right_dim) + tail


def fold_rows(x, op, parts=8):
    size = x.shape[0] // parts
    pieces = [x[at * size : (at + 1) * size] for at in range(parts)]
    while len(pieces) > 1:
        pieces = [op(pieces[at], pieces[at + 1]) for at in range(0, len(pieces), 2)]
    return pieces[0]


def column_max(x):
    return jnp.max(fold_rows(x, jnp.maximum), 0, keepdims=True)


def column_sum(x):
    return jnp.sum(fold_rows(x, jnp.add), 0, keepdims=True)


erf_top = (
    -2.72614225801306e-10,
    2.77068142495902e-08,
    -2.10102402082508e-06,
    -5.69250639462346e-05,
    -7.34990630326855e-04,
    -2.95459980854025e-03,
    -1.60960333262415e-02,
)
erf_bottom = (
    -1.45660718464996e-05,
    -2.13374055278905e-04,
    -1.68282697438203e-03,
    -7.37332916720468e-03,
    -1.42647390514189e-02,
)


def erf(x):
    x = jnp.clip(x, -4.0, 4.0)
    square = x * x
    top = jnp.full_like(x, erf_top[0])
    for term in erf_top[1:]:
        top = top * square + term
    bottom = jnp.full_like(x, erf_bottom[0])
    for term in erf_bottom[1:]:
        bottom = bottom * square + term
    return x * top / bottom


def normal_share(x):
    return 0.5 + 0.5 * erf(x * math.sqrt(0.5))


def gelu(x):
    return x * normal_share(x)


def gelu_slope(x, share):
    return share + x * jnp.exp(-0.5 * x * x) * (1.0 / math.sqrt(2.0 * math.pi))


def rotary_partner(x):
    lane = lax.broadcasted_iota(jnp.int32, x.shape, 1) % HEAD
    return jnp.where(
        lane < HEAD // 2,
        pltpu.roll(x, LANES - HEAD // 2, 1),
        pltpu.roll(x, HEAD // 2, 1),
    )


def rotate(x, cosine, sine):
    return x * cosine + rotary_partner(x) * sine


def unrotate(x, cosine, sine):
    return x * cosine - rotary_partner(x) * sine


class Features:
    def __init__(self, width, groups):
        self.width = width
        self.groups = groups
        self.block = width // groups
        self.padded = -(-self.block // 16) * 16
        self.total = self.padded * groups

    def pad(self, x):
        rows = x.shape[0]
        x = x.reshape(rows, self.groups, self.block)
        x = jnp.pad(x, ((0, 0), (0, 0), (0, self.padded - self.block)))
        return x.reshape(rows, self.total)

    def unpad(self, x):
        rows = x.shape[0]
        x = x.reshape(rows, self.groups, self.padded)[:, :, : self.block]
        return x.reshape(rows, self.width)

    def live(self, shape):
        lane = lax.broadcasted_iota(jnp.int32, shape, 1) % self.padded
        return lane < self.block

    def centred(self, x):
        mean = jnp.sum(x, 1, keepdims=True) * (1.0 / self.width)
        centre = jnp.where(self.live(x.shape), x - mean, 0.0)
        spread = jnp.sum(centre * centre, 1, keepdims=True) * (1.0 / self.width)
        inverse = lax.rsqrt(spread + norm_eps)
        return centre * inverse, inverse

    def norm(self, x, gain, shift):
        unit, _ = self.centred(x)
        return (unit * gain + shift).astype(brain)

    def norm_back(self, unit, inverse, gain, grad):
        scaled = grad * gain
        mean = jnp.sum(scaled, 1, keepdims=True) * (1.0 / self.width)
        along = jnp.sum(scaled * unit, 1, keepdims=True) * (1.0 / self.width)
        back = inverse * (scaled - mean - unit * along)
        return jnp.where(self.live(back.shape), back, 0.0)


class Gathered:
    def __init__(self, ref):
        self.ref = ref

    def block(self, tile, start, stop):
        groups, _, rows, _ = self.ref.shape
        return self.ref[:, tile, :, start:stop].reshape(groups * rows, stop - start)


class Relative:
    def __init__(self, cube, me, refs, cuts, orders):
        self.cube = cube
        self.me = me
        self.refs = refs
        self.cuts = cuts
        self.orders = orders

    def block(self, tile, start, stop):
        pieces = []
        for ref, low, high, order in zip(self.refs, self.cuts[:-1], self.cuts[1:], self.orders):
            first = max(start, low) - low
            last = min(stop, high) - low
            if first >= last:
                continue
            rows = []
            for group in range(self.cube.groups):
                offset = (group * self.cube.tensors + tile) ^ self.me
                rows.append(ref[self.cube.slot(offset, order), :, first:last])
            pieces.append(jnp.concatenate(rows, 0))
        return pieces[0] if len(pieces) == 1 else jnp.concatenate(pieces, 1)


class Scattered:
    def __init__(self, cube, me, keep_ref, send_ref, orders):
        self.cube = cube
        self.me = me
        self.refs = (keep_ref, send_ref)
        self.orders = orders

    def store(self, tile, turn, start, value):
        rows, wide = self.refs[0].shape[2:]
        ref = self.refs[turn & 1]
        width = value.shape[1]
        for group in range(self.cube.groups):
            offset = (group * self.cube.tensors + tile) ^ self.me
            done = 0
            while done < width:
                part, place = divmod(start + done, wide)
                count = min(width - done, wide - place)
                slot = self.cube.slot(offset, self.orders[part][::-1])
                ref[part, slot, :, place : place + count] = value[
                    group * rows : (group + 1) * rows, done : done + count
                ]
                done += count


class Whole:
    def __init__(self, ref):
        self.ref = ref

    def store(self, tile, turn, start, value):
        groups, _, rows, _ = self.ref.shape
        wide = value.shape[1]
        self.ref[:, tile, :, start : start + wide] = value.reshape(groups, rows, wide)


class Layer:
    def __init__(self, weights, base, hidden):
        self.weights = weights
        self.base = base
        self.hidden = hidden

    def out(self, tile):
        return self.weights.block(tile, self.base, self.base + LANES)

    def up(self, tile):
        start = self.base + LANES
        return self.weights.block(tile, start, start + self.hidden)

    def down(self, tile):
        start = self.base + LANES + self.hidden
        return self.weights.block(tile, start, start + self.hidden)


def tile_lanes(tile):
    if isinstance(tile, int):
        return pl.ds(tile * LANES, LANES)
    return pl.ds(pl.multiple_of(tile * LANES, LANES), LANES)


def add_up(parts):
    total = None
    for part in parts:
        total = part if total is None else total + part
    return total


def whole_spec(shape):
    return pl.BlockSpec(shape, lambda at: (0,) * len(shape))


def columns_spec(weights, columns, at_block):
    groups, tiles, rows, _ = weights.shape
    return pl.BlockSpec((groups, tiles, rows, columns), lambda at: (0, 0, 0, at_block))


def scalar_spec():
    return pl.BlockSpec(memory_space=pltpu.SMEM)


def call(kernel, name, ins, in_specs, outs, micros, scratch=()):
    return pl.pallas_call(
        kernel,
        grid=(1,),
        in_specs=in_specs,
        out_specs=[whole_spec(out.shape) for out in outs],
        out_shape=outs,
        scratch_shapes=list(scratch),
        compiler_params=params(),
        cost_estimate=cost(micros),
        name=name,
    )(*ins)


def embed_kernel(
    table_ref, ids_ref, vocab_ref, cos_ref, sin_ref, q_ref, own_ref, other_ref, resid_ref
):
    own = q_ref.shape[0]
    length = ids_ref.shape[1]
    tiles = table_ref.shape[0]
    hot = lax.broadcasted_iota(jnp.int32, (64, length), 0) == ids_ref[...]
    hot = hot.astype(single).T.astype(brain)
    resid_ref[...] = dot(hot[:own], vocab_ref[...])
    hot = hot[:, :TABLE_ROWS]
    cosine = cos_ref[...]
    sine = sin_ref[...]
    for at in range(tiles):
        lanes = slice(at * LANES, (at + 1) * LANES)
        rows = dot_exact(hot, table_ref[at])
        q_ref[:, lanes] = rotate(rows[:own, :LANES], cosine[:own], sine[:own]).astype(brain)
        keys = rotate(rows[:, LANES : 2 * LANES], cosine, sine).astype(brain)
        values = rows[:, 2 * LANES :].astype(brain)
        own_ref[0, :, lanes] = keys[:own]
        own_ref[1, :, lanes] = values[:own]
        other_ref[0, :, lanes] = keys[own:]
        other_ref[1, :, lanes] = values[own:]


def embed(table, ids, vocab, cosine, sine):
    tiles = table.shape[0]
    own = ids.shape[1] // 2
    wide = tiles * LANES
    ins = (table, ids, vocab, cosine, sine)
    outs = [
        jax.ShapeDtypeStruct((own, wide), brain),
        jax.ShapeDtypeStruct((2, own, wide), brain),
        jax.ShapeDtypeStruct((2, own, wide), brain),
        jax.ShapeDtypeStruct((own, vocab.shape[1]), single),
    ]
    return call(embed_kernel, "embed", ins, [whole_spec(x.shape) for x in ins], outs, 6)


def attend_kernel(heads, chunk, q_ref, own_ref, other_ref, out_ref, logsum_ref):
    own = q_ref.shape[0]
    q_turned = q_ref[...].T
    keys = jnp.concatenate([own_ref[0], other_ref[0]], 0)
    v_turned = jnp.concatenate([own_ref[1], other_ref[1]], 0).T
    rows = lax.broadcasted_iota(jnp.int32, (LANES, chunk), 0)
    for start in range(0, own, chunk):
        part = slice(start, start + chunk)
        q_part = q_turned[:, part]
        mixed = jnp.zeros((LANES, chunk), single)
        for head in range(heads):
            mine = (rows >= head * HEAD) & (rows < (head + 1) * HEAD)
            scores = dot(keys, jnp.where(mine, q_part, jnp.zeros_like(q_part)))
            peak = column_max(scores) * scale_two
            weights = jnp.exp2(scores * scale_two - peak)
            total = column_sum(weights)
            probs = (weights * (1.0 / total)).astype(brain)
            mixed = jnp.where(mine, dot(v_turned, probs), mixed)
            logsum_ref[0, head : head + 1, part] = peak + jnp.log2(total)
        out_ref[part, :] = mixed.T.astype(brain)


def attend(q, kv_own, kv_other, heads):
    own, wide = q.shape
    tiles = wide // LANES
    own_spec = pl.BlockSpec((own, LANES), lambda at: (0, at))
    pair_spec = pl.BlockSpec((2, own, LANES), lambda at: (0, 0, at))
    return pl.pallas_call(
        functools.partial(attend_kernel, heads, LANES),
        grid=(tiles,),
        in_specs=[own_spec, pair_spec, pair_spec],
        out_specs=[own_spec, pl.BlockSpec((1, 8, own), lambda at: (at, 0, 0))],
        out_shape=[
            jax.ShapeDtypeStruct((own, wide), brain),
            jax.ShapeDtypeStruct((tiles, 8, own), single),
        ],
        compiler_params=params(),
        cost_estimate=cost(20),
        name="attend",
    )(q, kv_own, kv_other)


def attend_back_kernel(
    heads, chunk, q_ref, kv_own_ref, kv_other_ref, g_ref, logsum_ref, dq_ref, own_ref, other_ref
):
    own = q_ref.shape[0]
    q = q_ref[...]
    grad = g_ref[...]
    q_turned = q.T
    g_turned = grad.T
    keys = jnp.concatenate([kv_own_ref[0], kv_other_ref[0]], 0)
    values = jnp.concatenate([kv_own_ref[1], kv_other_ref[1]], 0)
    k_turned = keys.T
    rows = lax.broadcasted_iota(jnp.int32, (LANES, chunk), 0)
    lanes = lax.broadcasted_iota(jnp.int32, (chunk, LANES), 1)
    none = jnp.zeros((LANES, chunk), brain)
    none_low = jnp.zeros((chunk, LANES), brain)
    for start in range(0, own, chunk):
        part = slice(start, start + chunk)
        dq = jnp.zeros((LANES, chunk), single)
        for head in range(heads):
            mine = (rows >= head * HEAD) & (rows < (head + 1) * HEAD)
            mine_low = (lanes >= head * HEAD) & (lanes < (head + 1) * HEAD)
            scores = dot(keys, jnp.where(mine, q_turned[:, part], none))
            probs = jnp.exp2(scores * scale_two - logsum_ref[0, head : head + 1, part])
            g_probs = dot(values, jnp.where(mine, g_turned[:, part], none))
            inner = column_sum(probs * g_probs)
            g_scores = (probs * (g_probs - inner)).astype(brain)
            dv = dot(probs.astype(brain), jnp.where(mine_low, grad[part, :], none_low))
            dk = dot(g_scores, jnp.where(mine_low, q[part, :], none_low)) * scale
            if start == 0 and head == 0:
                own_ref[0] = dk[:own]
                own_ref[1] = dv[:own]
                other_ref[0] = dk[own:]
                other_ref[1] = dv[own:]
            else:
                own_ref[0] += dk[:own]
                own_ref[1] += dv[:own]
                other_ref[0] += dk[own:]
                other_ref[1] += dv[own:]
            dq = jnp.where(mine, dot(k_turned, g_scores), dq)
        dq_ref[part, :] = (dq * scale).T


def attend_back(q, kv_own, kv_other, grad, logsum, heads):
    own, wide = q.shape
    tiles = wide // LANES
    own_spec = pl.BlockSpec((own, LANES), lambda at: (0, at))
    pair_spec = pl.BlockSpec((2, own, LANES), lambda at: (0, 0, at))
    pair_shape = jax.ShapeDtypeStruct((2, own, wide), single)
    return pl.pallas_call(
        functools.partial(attend_back_kernel, heads, own),
        grid=(tiles,),
        in_specs=[
            own_spec,
            pair_spec,
            pair_spec,
            own_spec,
            pl.BlockSpec((1, 8, own), lambda at: (at, 0, 0)),
        ],
        out_specs=[own_spec, pair_spec, pair_spec],
        out_shape=[jax.ShapeDtypeStruct((own, wide), single), pair_shape, pair_shape],
        compiler_params=params(),
        cost_estimate=cost(33),
        name="attend_back",
    )(q, kv_own, kv_other, grad, logsum)


def attention_out(mixed, resid, layer, tiles):
    parts = [
        dot(mixed[:, at * LANES : (at + 1) * LANES], layer.out(at), 1, 1) for at in range(tiles)
    ]
    return resid + add_up(parts)


def middle_kernel(
    feats, cube, cuts, orders, hidden, me_ref, mixed_ref, resid_ref, *refs
):
    count = len(orders)
    part_refs = refs[:count]
    w_next_ref, norms_ref, cos_ref, sin_ref, mid_ref, next_ref, q_ref, kv_ref = refs[count:]
    layer = Layer(Relative(cube, me_ref[0], part_refs, cuts, orders), 0, hidden)
    tiles = cube.tensors
    mid = attention_out(mixed_ref[...], resid_ref[...], layer, tiles)
    mid_ref[...] = mid
    normed = feats.norm(mid, norms_ref[2:3], norms_ref[3:4])
    parts = []
    for at in range(tiles):
        act = gelu(dot(normed, layer.up(at))).astype(brain)
        parts.append(dot(act, layer.down(at), 1, 1))
    total = mid + add_up(parts)
    next_ref[...] = total
    normed = feats.norm(total, norms_ref[4:5], norms_ref[5:6])
    weights = Gathered(w_next_ref)
    for at in range(tiles):
        lanes = slice(at * LANES, (at + 1) * LANES)
        rows = dot(normed, weights.block(at, 0, 3 * LANES))
        cosine = cos_ref[...]
        sine = sin_ref[...]
        q_ref[:, lanes] = rotate(rows[:, :LANES], cosine, sine).astype(brain)
        kv_ref[0, :, lanes] = rotate(rows[:, LANES : 2 * LANES], cosine, sine).astype(brain)
        kv_ref[1, :, lanes] = rows[:, 2 * LANES :].astype(brain)


def middle(feats, cube, cuts, orders, me, mixed, resid, parts, w_next, norms, cosine, sine):
    own, wide = mixed.shape
    hidden = (cuts[-1] - LANES) // 2
    plain = jax.ShapeDtypeStruct(resid.shape, single)
    outs = [
        plain,
        plain,
        jax.ShapeDtypeStruct((own, wide), brain),
        jax.ShapeDtypeStruct((2, own, wide), brain),
    ]
    in_specs = [
        scalar_spec(),
        whole_spec(mixed.shape),
        whole_spec(resid.shape),
        *[whole_spec(part.shape) for part in parts],
        columns_spec(w_next, 3 * LANES, 0),
        whole_spec(norms.shape),
        whole_spec(cosine.shape),
        whole_spec(sine.shape),
    ]
    ins = (me, mixed, resid, *parts, w_next, norms, cosine, sine)
    kernel = functools.partial(middle_kernel, feats, cube, cuts, orders, hidden)
    return call(kernel, "middle", ins, in_specs, outs, 12)


def feed_back(
    feats, turns, g_resid, mid, normed, mixed_ref, layer, gain, act_ref, slope_ref,
    grads, base, g_mid_ref, g_mixed_ref,
):
    hidden = layer.hidden
    g_low = g_resid.astype(brain)
    g_turned = g_low.T
    normed_turned = normed.T
    parts = []
    for turn, tile in turns:
        g_hidden = (dot(g_low, layer.down(tile)) * slope_ref[turn]).astype(brain)
        grads.store(tile, turn, base + LANES + hidden, dot(g_turned, act_ref[turn]))
        grads.store(tile, turn, base + LANES, dot(normed_turned, g_hidden))
        parts.append(dot(g_hidden, layer.up(tile), 1, 1))
    g_normed = add_up(parts)
    unit, inverse = feats.centred(mid)
    g_gain = jnp.sum(g_normed * unit, 0, keepdims=True)
    g_shift = jnp.sum(g_normed, 0, keepdims=True)
    g_mid = g_resid + feats.norm_back(unit, inverse, gain, g_normed)
    g_mid_ref[...] = g_mid
    g_low = g_mid.astype(brain)
    g_turned = g_low.T
    for turn, tile in turns:
        lanes = tile_lanes(tile)
        g_mixed_ref[:, lanes] = dot(g_low, layer.out(tile)).astype(brain)
        grads.store(tile, turn, base, dot(g_turned, mixed_ref[:, lanes]))
    return g_gain, g_shift


def top_kernel(
    feats, vocab_count, mixed_ref, resid_ref, w_ref, norms_ref, vocab_ref, slot_ref, target_ref,
    count_ref, grads_ref, g_mid_ref, g_mixed_ref, g_norms_ref, g_vocab_ref,
    act_ref, slope_ref,
):
    tiles = w_ref.shape[1]
    layer = Layer(Gathered(w_ref), 3 * LANES, act_ref.shape[2])
    mid = attention_out(mixed_ref[...], resid_ref[...], layer, tiles)
    normed = feats.norm(mid, norms_ref[6:7], norms_ref[7:8])
    parts = []
    for at in range(tiles):
        hidden = dot(normed, layer.up(at))
        share = normal_share(hidden)
        act = (hidden * share).astype(brain)
        act_ref[at] = act
        slope_ref[at] = gelu_slope(hidden, share)
        parts.append(dot(act, layer.down(at), 1, 1))
    total = mid + add_up(parts)
    unit, inverse = feats.centred(total)
    gain = norms_ref[8:9]
    final = (unit * gain + norms_ref[9:10]).astype(brain)
    own = total.shape[0]
    slots = slot_ref.shape[0]
    vocab = vocab_ref[...]
    where_hot = (lax.broadcasted_iota(jnp.int32, (slots, own), 1) == slot_ref[...]).astype(single)
    where_hot = where_hot.astype(brain)
    present = (slot_ref[...] >= 0).astype(single)
    picked = dot(where_hot, final).astype(brain)
    logits = dot(picked, vocab, 1, 1)
    lane = lax.broadcasted_iota(jnp.int32, logits.shape, 1)
    logits = jnp.where(lane < vocab_count, logits, -1e30)
    peak = jnp.max(logits, 1, keepdims=True)
    logsum = peak + jnp.log(jnp.sum(jnp.exp(logits - peak), 1, keepdims=True))
    target_hot = (lane == target_ref[...]).astype(single)
    target_logit = jnp.sum(
        jnp.where(lane < vocab_count, logits * target_hot, 0.0), 1, keepdims=True
    )
    loss = jnp.sum((logsum - target_logit) * present, 0, keepdims=True)
    share = present / count_ref[0:1, 0:1]
    g_logits = ((jnp.exp(logits - logsum) - target_hot) * share).astype(brain)
    g_vocab_ref[...] = dot(g_logits, picked, 0, 0)[:TABLE_ROWS]
    g_picked = dot(g_logits, vocab)
    g_final = dot_exact(where_hot, g_picked, 0, 0)
    g_norms_ref[...] = jnp.zeros_like(g_norms_ref)
    g_norms_ref[8:9] = jnp.sum(g_final * unit, 0, keepdims=True)
    g_norms_ref[9:10] = jnp.sum(g_final, 0, keepdims=True)
    g_norms_ref[LOSS_ROW : LOSS_ROW + 1] = jnp.broadcast_to(loss, (1, g_norms_ref.shape[1]))
    g_resid = feats.norm_back(unit, inverse, gain, g_final)
    g_gain, g_shift = feed_back(
        feats, [(at, at) for at in range(tiles)], g_resid, mid, normed, mixed_ref, layer,
        norms_ref[6:7], act_ref, slope_ref, Whole(grads_ref), 0, g_mid_ref, g_mixed_ref,
    )
    g_norms_ref[6:7] = g_gain
    g_norms_ref[7:8] = g_shift


def top(feats, mixed, resid, weights, columns, norms, vocab, vocab_count, slot, target, count):
    own, wide = mixed.shape
    groups, tiles, rows, _ = weights.shape
    grads = columns - 3 * LANES
    hidden = (grads - LANES) // 2
    outs = [
        jax.ShapeDtypeStruct((groups, tiles, rows, grads), single),
        jax.ShapeDtypeStruct(resid.shape, single),
        jax.ShapeDtypeStruct(mixed.shape, brain),
        jax.ShapeDtypeStruct(norms.shape, single),
        jax.ShapeDtypeStruct((TABLE_ROWS, resid.shape[1]), single),
    ]
    in_specs = [
        whole_spec(mixed.shape),
        whole_spec(resid.shape),
        columns_spec(weights, columns, 0),
        whole_spec(norms.shape),
        whole_spec(vocab.shape),
        whole_spec(slot.shape),
        whole_spec(target.shape),
        whole_spec(count.shape),
    ]
    scratch = [
        pltpu.VMEM((tiles, own, hidden), brain),
        pltpu.VMEM((tiles, own, hidden), single),
    ]
    ins = (mixed, resid, weights, norms, vocab, slot, target, count)
    kernel = functools.partial(top_kernel, feats, vocab_count)
    return call(kernel, "top", ins, in_specs, outs, 21, scratch)


def head_grads(tile, dq_ref, own_ref, other_ref, cosine, sine):
    lanes = tile_lanes(tile)
    g_q = unrotate(dq_ref[:, lanes], cosine, sine)
    g_k = unrotate(own_ref[0, :, lanes] + other_ref[0, :, lanes], cosine, sine)
    g_v = own_ref[1, :, lanes] + other_ref[1, :, lanes]
    return jnp.concatenate([g_q, g_k, g_v], 1).astype(brain)


def lower_kernel(
    feats, cube, cuts, orders, grad_orders, me_ref, dq_ref, own_ref, other_ref, g_mid_in_ref,
    resid_ref, mid_ref, mixed_ref, w_in_ref, *refs
):
    count = len(orders)
    part_refs = refs[:count]
    (
        norms_ref, cos_ref, sin_ref, g_norms_in_ref,
        keep_ref, send_ref, g_mid_ref, g_mixed_ref, g_norms_ref,
        act_ref, slope_ref,
    ) = refs[count:]
    me = me_ref[0]
    tiles = cube.tensors
    turns = [(turn, turn ^ (me & (tiles - 1))) for turn in range(tiles)]
    layer = Layer(Relative(cube, me, part_refs, cuts, orders), 0, act_ref.shape[2])
    weights = Gathered(w_in_ref)
    grads = Scattered(cube, me, keep_ref, send_ref, grad_orders)
    unit, inverse = feats.centred(resid_ref[...])
    gain = norms_ref[4:5]
    normed_turned = (unit * gain + norms_ref[5:6]).astype(brain).T
    cosine = cos_ref[...]
    sine = sin_ref[...]
    parts = []
    for turn, tile in turns:
        g_heads = head_grads(tile, dq_ref, own_ref, other_ref, cosine, sine)
        grads.store(tile, turn, 0, dot(normed_turned, g_heads))
        parts.append(dot(g_heads, weights.block(tile, 0, 3 * LANES), 1, 1))
    g_normed = add_up(parts)
    g_norms_ref[...] = g_norms_in_ref[...]
    g_norms_ref[4:5] = jnp.sum(g_normed * unit, 0, keepdims=True)
    g_norms_ref[5:6] = jnp.sum(g_normed, 0, keepdims=True)
    g_resid = g_mid_in_ref[...] + feats.norm_back(unit, inverse, gain, g_normed)
    mid = mid_ref[...]
    normed = feats.norm(mid, norms_ref[2:3], norms_ref[3:4])
    for turn, tile in turns:
        hidden = dot(normed, layer.up(tile))
        share = normal_share(hidden)
        act_ref[turn] = (hidden * share).astype(brain)
        slope_ref[turn] = gelu_slope(hidden, share)
    g_gain, g_shift = feed_back(
        feats, turns, g_resid, mid, normed, mixed_ref, layer, norms_ref[2:3], act_ref, slope_ref,
        grads, 3 * LANES, g_mid_ref, g_mixed_ref,
    )
    g_norms_ref[2:3] = g_gain
    g_norms_ref[3:4] = g_shift


def lower(
    feats, cube, cuts, orders, grad_orders, me, dq, own_part, other_part, g_mid, resid, mid,
    mixed, w_in, parts, norms, cosine, sine, g_norms,
):
    own, wide = mixed.shape
    tiles = cube.tensors
    rows = w_in.shape[2]
    hidden = (cuts[-1] - LANES) // 2
    columns = cuts[-1] + 3 * LANES
    count = len(grad_orders)
    grads = (count, cube.devices // 2, rows, columns // count)
    outs = [
        jax.ShapeDtypeStruct(grads, single),
        jax.ShapeDtypeStruct(grads, single),
        jax.ShapeDtypeStruct(resid.shape, single),
        jax.ShapeDtypeStruct(mixed.shape, brain),
        jax.ShapeDtypeStruct(norms.shape, single),
    ]
    before = (dq, own_part, other_part, g_mid, resid, mid, mixed)
    after = (norms, cosine, sine, g_norms)
    in_specs = [
        scalar_spec(),
        *[whole_spec(x.shape) for x in before],
        columns_spec(w_in, 3 * LANES, 0),
        *[whole_spec(x.shape) for x in (*parts, *after)],
    ]
    scratch = [
        pltpu.VMEM((tiles, own, hidden), brain),
        pltpu.VMEM((tiles, own, hidden), single),
    ]
    ins = (me, *before, w_in, *parts, *after)
    kernel = functools.partial(lower_kernel, feats, cube, cuts, orders, grad_orders)
    return call(kernel, "lower", ins, in_specs, outs, 22, scratch)


def stacked_lanes(ref, row, value):
    rows = value.shape[0]
    for at in range(value.shape[1] // LANES):
        ref[row : row + rows, :] = value[:, at * LANES : (at + 1) * LANES]
        row += rows
    return row


def side_by_side(x, rows):
    return jnp.concatenate([x[at : at + rows] for at in range(0, x.shape[0], rows)], 1)


def bottom_kernel(
    feats, cube, me_ref, dq_ref, own_ref, other_ref, g_mid_ref, ids_ref, w_ref, norms_ref,
    vocab_ref, g_vocab_in_ref, g_norms_in_ref, cos_ref, sin_ref, keep_ref, send_ref, norms_out_ref,
):
    tiles = cube.tensors
    own = dq_ref.shape[0]
    mine = me_ref[0] & (tiles - 1)
    hot = lax.broadcasted_iota(jnp.int32, (TABLE_ROWS, own), 0) == ids_ref[...]
    hot = hot.astype(single).astype(brain)
    cosine = cos_ref[...]
    sine = sin_ref[...]
    weights = Gathered(w_ref)
    refs = (keep_ref, send_ref)
    rows = [0, 0]
    parts = []
    for turn in range(tiles):
        tile = turn ^ mine
        g_table = dot(hot, head_grads(tile, dq_ref, own_ref, other_ref, cosine, sine))
        rows[turn & 1] = stacked_lanes(refs[turn & 1], rows[turn & 1], g_table)
        weight = weights.block(tile, 0, 3 * LANES)
        high, middle_part, low = split_three(g_table)
        parts.append(dot(high, weight, 1, 1))
        parts.append(dot(middle_part, weight, 1, 1))
        parts.append(dot(low, weight, 1, 1))
    g_normed = add_up(parts)
    unit, inverse = feats.centred(vocab_ref[...].astype(single)[:TABLE_ROWS])
    norms_out_ref[...] = g_norms_in_ref[...]
    norms_out_ref[0:1] = jnp.sum(g_normed * unit, 0, keepdims=True)
    norms_out_ref[1:2] = jnp.sum(g_normed, 0, keepdims=True)
    g_norms = norms_out_ref[...]
    g_rows = feats.norm_back(unit, inverse, norms_ref[0:1], g_normed)
    g_vocab = g_vocab_in_ref[...] + (dot_exact(hot, g_mid_ref[...]) + g_rows)
    for ref, row in zip(refs, rows):
        row = stacked_lanes(ref, row, g_vocab)
        stacked_lanes(ref, row, g_norms)


def bottom(
    feats, cube, me, dq, own_part, other_part, g_mid, ids, w_in, at_block, norms, vocab, g_vocab,
    g_norms, cosine, sine,
):
    tiles = cube.tensors
    table_rows = 3 * TABLE_ROWS * tiles // 2
    vector_rows = (g_vocab.shape[0] + g_norms.shape[0]) * g_vocab.shape[1] // LANES
    out = jax.ShapeDtypeStruct((table_rows + vector_rows, LANES), single)
    before = (dq, own_part, other_part, g_mid, ids)
    after = (norms, vocab, g_vocab, g_norms, cosine, sine)
    in_specs = [
        scalar_spec(),
        *[whole_spec(x.shape) for x in before],
        columns_spec(w_in, 3 * LANES, at_block),
        *[whole_spec(x.shape) for x in after],
    ]
    outs = [out, out, jax.ShapeDtypeStruct(norms.shape, single)]
    ins = (me, *before, w_in, *after)
    kernel = functools.partial(bottom_kernel, feats, cube)
    return call(kernel, "bottom", ins, in_specs, outs, 7)[:2]


def halve_kernel(count, together, keep_ref, *refs):
    got = refs[:1] if together else refs[:count]
    outs = refs[len(got) :]
    size = keep_ref.shape[1]
    half = size // 2
    for part in range(count):
        arrived = got[0].at[part] if together else got[part]
        if size == 1:
            outs[0][part] = keep_ref[part] + arrived[...]
        else:
            outs[0][part] = keep_ref[part, :half] + arrived[:half]
            outs[1 + part][...] = keep_ref[part, half:] + arrived[half:]


def halve(keep, got):
    count, size, rows, wide = keep.shape
    together = not isinstance(got, list)
    got = [got] if together else got
    step = 16
    half = max(size // 2, 1)

    def spec(*lead):
        return pl.BlockSpec((*lead, step, wide), lambda at: (*([0] * len(lead)), at, 0))

    outs = [jax.ShapeDtypeStruct((count, half, rows, wide), single)]
    out_specs = [spec(count, half)]
    if size > 1:
        outs += [jax.ShapeDtypeStruct((half, rows, wide), single)] * count
        out_specs += [spec(half)] * count
    got_specs = [spec(count, size)] if together else [spec(size)] * count
    return pl.pallas_call(
        functools.partial(halve_kernel, count, together),
        grid=(rows // step,),
        in_specs=[spec(count, size), *got_specs],
        out_specs=out_specs,
        out_shape=outs,
        compiler_params=params(),
        cost_estimate=cost(2),
        name="halve",
    )(keep, *got)


def scatter_sums(cube, keep, send, orders):
    got = cube.swap(send, 0)
    for step in range(len(orders[0])):
        keep, *sends = halve(keep, got)
        got = [cube.swap(x, order[step]) for x, order in zip(sends, orders)]
    return halve(keep, got)[0][:, 0]


def normalize_features(resid, gain, shift):
    centre = resid - jnp.mean(resid, -1, keepdims=True)
    spread = jnp.mean(centre * centre, -1, keepdims=True)
    return centre * lax.rsqrt(spread + norm_eps) * gain + shift


def adamw(master, first, second, grad, step_rate):
    mean = beta_first * first + (1.0 - beta_first) * grad
    square = beta_second * second + (1.0 - beta_second) * grad * grad
    corrected = mean / (1.0 - beta_first**STEP)
    rescaled_values = square / (1.0 - beta_second**STEP)
    fresh = master - step_rate * (
        corrected / (jnp.sqrt(rescaled_values) + adam_eps) + weight_decay * master
    )
    return (fresh, mean, square)


def pad_lanes(x, lanes):
    return jnp.pad(x, [(0, 0)] * (x.ndim - 1) + [(0, lanes - x.shape[-1])])


def make_shards(groups, tensors):
    axes = ("dp", "tensor")
    cube = Cube(groups, tensors)

    def shards(
        token_ids,
        mask_pos,
        mask_target,
        mask_count,
        weight_in,
        weight_out,
        weight_up,
        weight_down,
        norm_params,
        vocab_table,
        first_in,
        first_out,
        first_up,
        first_down,
        first_norm,
        first_vocab,
        second_in,
        second_out,
        second_up,
        second_down,
        second_norm,
        second_vocab,
    ):
        layers, block, in_wide = weight_in.shape
        heads = in_wide // (3 * HEAD)
        per_heads = heads * HEAD
        hidden = weight_up.shape[2]
        hidden_padded = -(-hidden // LANES) * LANES
        vocab_count, width = vocab_table.shape
        feats = Features(width, groups)
        local_len = token_ids.shape[1]
        length = local_len * tensors
        own = length // 2
        here = lax.axis_index("tensor")
        group_at = lax.axis_index("dp")
        me = (group_at * tensors + here).astype(jnp.int32).reshape(1)
        sequence = here // 2
        quarters = jnp.stack([here, here ^ 2, here ^ 1, here ^ 3])

        heads_in = weight_in.astype(brain).transpose(1, 0, 2)
        heads_in = heads_in.reshape(block, layers, heads, 3, HEAD).transpose(0, 1, 3, 2, 4)
        heads_in = pad_lanes(heads_in.reshape(block, layers, 3, per_heads), LANES)
        heads_in = heads_in.reshape(block, layers, 3 * LANES)
        feed = jnp.concatenate(
            [
                pad_lanes(weight_out.astype(brain).transpose(2, 0, 1), LANES),
                pad_lanes(weight_up.astype(brain).transpose(1, 0, 2), hidden_padded),
                pad_lanes(weight_down.astype(brain).transpose(2, 0, 1), hidden_padded),
            ],
            2,
        )
        feed_columns = feed.shape[2]
        all_columns = 3 * LANES + feed_columns

        def pad_rows(x):
            return jnp.pad(x, ((0, feats.padded - block), (0, 0)))

        vocab_low = vocab_table.astype(brain)
        vocab_padded = jnp.pad(feats.pad(vocab_low), ((0, 64 - vocab_count), (0, 0)))
        norms = jnp.pad(feats.pad(norm_params), ((0, 16 - norm_params.shape[0]), (0, 0)))

        table_low = normalize_features(
            lax.reduce_precision(vocab_table, 8, 7), norm_params[0], norm_params[1]
        ).astype(brain)
        table_own = lax.dynamic_slice_in_dim(
            table_low.reshape(vocab_count, groups, block), group_at, 1, 1
        )[:, 0]
        table = dot(table_own, heads_in[:, 0])
        extra = jnp.zeros((TABLE_ROWS - vocab_count, 3 * LANES), single)
        extra = extra.at[0, 0].set(jnp.sum(mask_count).astype(single))
        table = jnp.concatenate([table, extra], 0)
        for at in range(2, cube.size):
            table = table + cube.swap(table, at)
        count_total = table[vocab_count, 0]
        ids_row = vocab_count + 1
        table = lax.dynamic_update_slice(
            table, pad_lanes(token_ids.astype(single), 3 * LANES), (ids_row, 0)
        )
        got = cube.swap(table, 1)
        upper = (here & 2) == 2
        pair = jnp.stack([jnp.where(upper, got, table), jnp.where(upper, table, got)])
        got = cube.swap(pair, 0)
        upper = (here & 1) == 1
        table = jnp.stack([jnp.where(upper, got, pair), jnp.where(upper, pair, got)], 1)
        table = table.reshape(tensors, TABLE_ROWS, 3 * LANES)
        ids = jnp.take(table[:, ids_row : ids_row + 2, :local_len], sequence, axis=1)
        ids = jnp.take(ids, quarters, axis=0).reshape(1, length).astype(jnp.int32)

        cuts = (0, LANES + hidden_padded, feed_columns)
        orders = [cube.outer(0) + [0], cube.outer(2) + [0]]
        feed_low = pad_rows(feed[:, 0])
        parts = [
            cube.gather(feed_low[:, low:high], order)
            for low, high, order in zip(cuts[:-1], cuts[1:], orders)
        ]
        rest = pad_rows(jnp.concatenate([heads_in[:, 1], feed[:, 1], heads_in[:, 0]], 1))
        weights = lax.all_gather(rest, axes, axis=0, tiled=False)
        weights = weights.reshape((groups, tensors) + rest.shape)
        low_block = all_columns // (3 * LANES)

        half = HEAD // 2
        freqs = 10000.0 ** (-jnp.arange(half, dtype=single) * 2.0 / HEAD)
        positions = (quarters[:, None] * local_len + jnp.arange(local_len)[None, :]).reshape(length)
        angles = positions.astype(single)[:, None] * freqs[None, :]
        cosine, sine = (jnp.cos(angles), jnp.sin(angles))
        cosine = pad_lanes(jnp.tile(jnp.concatenate([cosine, cosine], 1), (1, heads)), LANES)
        sine = pad_lanes(jnp.tile(jnp.concatenate([-sine, sine], 1), (1, heads)), LANES)
        cos_own, sin_own = (cosine[:own], sine[:own])

        slots = mask_pos.shape[1]
        my_pos = jnp.take(mask_pos, sequence, axis=0)
        my_count = jnp.take(mask_count, sequence, axis=0)
        quarter = my_pos // local_len
        inside = my_pos % local_len
        slot = jnp.where(
            quarter == here, inside, jnp.where(quarter == (here ^ 2), inside + local_len, -1)
        )
        slot = jnp.where(jnp.arange(slots) < my_count, slot, -1).reshape(slots, 1)
        target = jnp.take(mask_target, sequence, axis=0).reshape(slots, 1)
        count = jnp.broadcast_to(count_total, (8, LANES))

        q_low, kv_low, kv_low_other, resid_low = embed(table, ids, vocab_padded, cosine, sine)
        mixed_low, logsum_low = attend(q_low, kv_low, kv_low_other, heads)
        mid_low, resid, q, kv = middle(
            feats, cube, cuts, orders, me, mixed_low, resid_low, parts, weights, norms,
            cos_own, sin_own,
        )
        kv_other = cube.swap(kv, 0)
        mixed, logsum = attend(q, kv, kv_other, heads)
        grads_top, g_mid, g_mixed, g_norms, g_vocab = top(
            feats, mixed, resid, weights, all_columns, norms, vocab_padded, vocab_count, slot,
            target, count,
        )
        grads_top = grads_top.reshape((cube.devices,) + grads_top.shape[2:])
        grads_top = lax.psum_scatter(grads_top, axes, scatter_dimension=0, tiled=True)[0]
        dq, own_part, other_part = attend_back(q, kv, kv_other, g_mixed, logsum, heads)
        got = cube.swap(other_part, 0)
        grad_orders = [cube.outer(turn) for turn in range(4)]
        keep, send, g_mid, g_mixed, g_norms = lower(
            feats, cube, cuts, orders, grad_orders, me, dq, own_part, got, g_mid, resid, mid_low,
            mixed_low, weights, parts, norms, cos_own, sin_own, g_norms,
        )
        grads_low = scatter_sums(cube, keep, send, grad_orders)
        dq, own_part, other_part = attend_back(
            q_low, kv_low, kv_low_other, g_mixed, logsum_low, heads
        )
        got = cube.swap(other_part, 0)
        keep, send = bottom(
            feats, cube, me, dq, own_part, got, g_mid, ids[:, :own], weights, low_block, norms,
            vocab_padded, g_vocab, g_norms, cos_own, sin_own,
        )
        total = keep + cube.swap(send, 0)
        tile_rows = 3 * TABLE_ROWS
        got = cube.swap(total[tile_rows:], 1)
        total = jnp.concatenate(
            [total[:tile_rows] + got[:tile_rows], total[2 * tile_rows :] + got[tile_rows:]], 0
        )
        for at in range(2, cube.size):
            total = total + cube.swap(total, at)
        g_table = side_by_side(total[:tile_rows], TABLE_ROWS)[:vocab_count]
        vocab_rows = TABLE_ROWS * feats.total // LANES
        g_vocab = side_by_side(total[tile_rows : tile_rows + vocab_rows], TABLE_ROWS)
        g_vocab = feats.unpad(g_vocab[:vocab_count])
        g_norms = side_by_side(total[tile_rows + vocab_rows :], norms.shape[0])
        loss_total = g_norms[LOSS_ROW, 0]
        g_norms = feats.unpad(g_norms[: norm_params.shape[0]])
        grads_in_low = lax.dot_general(
            table_own.astype(single),
            g_table,
            (((0,), (0,)), ((), ())),
            precision=highest,
            preferred_element_type=single,
        )

        def unpack_in(grad):
            grad = grad[:block].reshape(block, 3, LANES)[:, :, :per_heads]
            return grad.reshape(block, 3, heads, HEAD).transpose(0, 2, 1, 3).reshape(block, in_wide)

        grads_low = jnp.concatenate(list(grads_low), 1)
        grad_in = jnp.stack([unpack_in(grads_in_low), unpack_in(grads_low[:, : 3 * LANES])], 1)
        both = jnp.stack([grads_low[:block, 3 * LANES :], grads_top[:block]], 1)
        grad_in = grad_in.transpose(1, 0, 2)
        grad_out = both[:, :, :per_heads].transpose(1, 2, 0)
        grad_up = both[:, :, LANES : LANES + hidden].transpose(1, 0, 2)
        start = LANES + hidden_padded
        grad_down = both[:, :, start : start + hidden].transpose(1, 2, 0)

        masters = (weight_in, weight_out, weight_up, weight_down, norm_params, vocab_table)
        firsts = (first_in, first_out, first_up, first_down, first_norm, first_vocab)
        seconds = (second_in, second_out, second_up, second_down, second_norm, second_vocab)
        grads = (grad_in, grad_out, grad_up, grad_down, g_norms, g_vocab)
        results = [
            adamw(masters[which], firsts[which], seconds[which], grads[which], step_rates[which])
            for which in range(6)
        ]
        news = [entry[0] for entry in results]
        means = [entry[1] for entry in results]
        squares = [entry[2] for entry in results]
        copies = [news[which].astype(brain) for which in (0, 1, 2, 3, 5)]
        return (loss_total, count_total, *news, *means, *squares, *copies)

    return shards


def solution(mesh):
    rows_in = P(None, "dp", "tensor")
    rows_out = P(None, "tensor", "dp")
    six = (rows_in, rows_out, rows_in, rows_out, P(), P())
    five = (rows_in, rows_out, rows_in, rows_out, P())
    return jax.shard_map(
        make_shards(mesh.shape["dp"], mesh.shape["tensor"]),
        mesh=mesh,
        in_specs=(P("dp", "tensor"), P("dp", None), P("dp", None), P("dp"), *six, *six, *six),
        out_specs=(P(), P(), *six, *six, *six, *five),
        check_vma=False,
    )
```

```python
import functools
import math

import jax
import jax.numpy as jnp
from jax import lax
from jax.experimental import pallas as pl
from jax.experimental.pallas import tpu as pltpu
from jax.sharding import PartitionSpec as P

HEAD = 24
STEP = 5
LANES = 128
TABLE_ROWS = 40
LOSS_ROW = 10
VMEM_BYTES = 60 * 1024 * 1024

norm_eps = 1e-05
step_rates = (0.02, 0.3, 0.02, 0.02, 0.3, 0.05)
beta_first = 0.5
beta_second = 0.5
adam_eps = 1e-08
weight_decay = 0.01
highest = lax.Precision.HIGHEST
brain = jnp.bfloat16
single = jnp.float32
scale = HEAD ** (-0.5)
scale_two = scale * math.log2(math.e)

params = functools.partial(pltpu.CompilerParams, vmem_limit_bytes=VMEM_BYTES)


class Cube:
    def __init__(self, groups, tensors):
        self.groups = groups
        self.tensors = tensors
        self.devices = groups * tensors
        self.size = self.devices.bit_length() - 1
        self.masks = [1 << at for at in range(self.size)]
        self.folded = groups >= 4
        if self.folded:
            self.masks[-1] |= self.masks[-2]

    def swap(self, x, at):
        mask = self.masks[at]
        pairs = [(device, device ^ mask) for device in range(self.devices)]
        return lax.ppermute(x, ("dp", "tensor"), pairs)

    def outer(self, turn):
        rest = list(range(1, self.size))
        rest = rest[1:2] + rest[:1] + rest[2:]
        turning = rest[:-1]
        turn = turn % len(turning)
        return turning[turn:] + turning[:turn] + rest[-1:]

    def steps(self, offset):
        bits = [(offset >> at) & 1 for at in range(self.size)]
        if self.folded:
            bits[-2] = bits[-2] ^ bits[-1]
        return bits

    def slot(self, offset, order):
        bits = self.steps(offset)
        place = 0
        for rank, at in enumerate(order):
            place = place + (bits[at] << rank)
        return place


def dot(left, right, left_dim=1, right_dim=0):
    return lax.dot_general(
        left, right, (((left_dim,), (right_dim,)), ((), ())), preferred_element_type=single
    )


def split_three(x):
    high = x.astype(brain)
    rest = x - high.astype(single)
    middle = rest.astype(brain)
    return high, middle, (rest - middle.astype(single)).astype(brain)


def dot_exact(hot, x, left_dim=1, right_dim=0):
    high, middle, low = split_three(x)
    tail = dot(hot, middle, left_dim, right_dim) + dot(hot, low, left_dim, right_dim)
    return dot(hot, high, left_dim, right_dim) + tail


def fold_rows(x, op, parts=8):
    size = x.shape[0] // parts
    pieces = [x[at * size : (at + 1) * size] for at in range(parts)]
    while len(pieces) > 1:
        pieces = [op(pieces[at], pieces[at + 1]) for at in range(0, len(pieces), 2)]
    return pieces[0]


def column_max(x):
    return jnp.max(fold_rows(x, jnp.maximum), 0, keepdims=True)


def column_sum(x):
    return jnp.sum(fold_rows(x, jnp.add), 0, keepdims=True)


erf_top = (
    -2.72614225801306e-10,
    2.77068142495902e-08,
    -2.10102402082508e-06,
    -5.69250639462346e-05,
    -7.34990630326855e-04,
    -2.95459980854025e-03,
    -1.60960333262415e-02,
)
erf_bottom = (
    -1.45660718464996e-05,
    -2.13374055278905e-04,
    -1.68282697438203e-03,
    -7.37332916720468e-03,
    -1.42647390514189e-02,
)


def erf(x):
    x = jnp.clip(x, -4.0, 4.0)
    square = x * x
    top = jnp.full_like(x, erf_top[0])
    for term in erf_top[1:]:
        top = top * square + term
    bottom = jnp.full_like(x, erf_bottom[0])
    for term in erf_bottom[1:]:
        bottom = bottom * square + term
    return x * top / bottom


def normal_share(x):
    return 0.5 + 0.5 * erf(x * math.sqrt(0.5))


def gelu(x):
    return x * normal_share(x)


def gelu_slope(x, share):
    return share + x * jnp.exp(-0.5 * x * x) * (1.0 / math.sqrt(2.0 * math.pi))


def rotary_partner(x):
    lane = lax.broadcasted_iota(jnp.int32, x.shape, 1) % HEAD
    return jnp.where(
        lane < HEAD // 2,
        pltpu.roll(x, LANES - HEAD // 2, 1),
        pltpu.roll(x, HEAD // 2, 1),
    )


def rotate(x, cosine, sine):
    return x * cosine + rotary_partner(x) * sine


def unrotate(x, cosine, sine):
    return x * cosine - rotary_partner(x) * sine


class Features:
    def __init__(self, width, groups):
        self.width = width
        self.groups = groups
        self.block = width // groups
        self.padded = -(-self.block // 16) * 16
        self.total = self.padded * groups

    def pad(self, x):
        rows = x.shape[0]
        x = x.reshape(rows, self.groups, self.block)
        x = jnp.pad(x, ((0, 0), (0, 0), (0, self.padded - self.block)))
        return x.reshape(rows, self.total)

    def unpad(self, x):
        rows = x.shape[0]
        x = x.reshape(rows, self.groups, self.padded)[:, :, : self.block]
        return x.reshape(rows, self.width)

    def live(self, shape):
        lane = lax.broadcasted_iota(jnp.int32, shape, 1) % self.padded
        return lane < self.block

    def centred(self, x):
        mean = jnp.sum(x, 1, keepdims=True) * (1.0 / self.width)
        centre = jnp.where(self.live(x.shape), x - mean, 0.0)
        spread = jnp.sum(centre * centre, 1, keepdims=True) * (1.0 / self.width)
        inverse = lax.rsqrt(spread + norm_eps)
        return centre * inverse, inverse

    def norm(self, x, gain, shift):
        unit, _ = self.centred(x)
        return (unit * gain + shift).astype(brain)

    def norm_back(self, unit, inverse, gain, grad):
        scaled = grad * gain
        mean = jnp.sum(scaled, 1, keepdims=True) * (1.0 / self.width)
        along = jnp.sum(scaled * unit, 1, keepdims=True) * (1.0 / self.width)
        back = inverse * (scaled - mean - unit * along)
        return jnp.where(self.live(back.shape), back, 0.0)


class Gathered:
    def __init__(self, ref):
        self.ref = ref

    def block(self, tile, start, stop):
        groups, _, rows, _ = self.ref.shape
        return self.ref[:, tile, :, start:stop].reshape(groups * rows, stop - start)


class Scattered:
    def __init__(self, cube, me, keep_ref, send_ref, orders):
        self.cube = cube
        self.me = me
        self.refs = (keep_ref, send_ref)
        self.orders = orders

    def store(self, tile, turn, start, value):
        rows, wide = self.refs[0].shape[2:]
        ref = self.refs[turn & 1]
        width = value.shape[1]
        for group in range(self.cube.groups):
            offset = (group * self.cube.tensors + tile) ^ self.me
            done = 0
            while done < width:
                part, place = divmod(start + done, wide)
                count = min(width - done, wide - place)
                slot = self.cube.slot(offset, self.orders[part][::-1])
                ref[part, slot, :, place : place + count] = value[
                    group * rows : (group + 1) * rows, done : done + count
                ]
                done += count


class Layer:
    def __init__(self, weights, base, hidden):
        self.weights = weights
        self.base = base
        self.hidden = hidden

    def out(self, tile):
        return self.weights.block(tile, self.base, self.base + LANES)

    def up(self, tile):
        start = self.base + LANES
        return self.weights.block(tile, start, start + self.hidden)

    def down(self, tile):
        start = self.base + LANES + self.hidden
        return self.weights.block(tile, start, start + self.hidden)


def tile_lanes(tile):
    if isinstance(tile, int):
        return pl.ds(tile * LANES, LANES)
    return pl.ds(pl.multiple_of(tile * LANES, LANES), LANES)


def add_up(parts):
    total = None
    for part in parts:
        total = part if total is None else total + part
    return total


def whole_spec(shape):
    return pl.BlockSpec(shape, lambda at: (0,) * len(shape))


def columns_spec(weights, columns, at_block):
    groups, tiles, rows, _ = weights.shape
    return pl.BlockSpec((groups, tiles, rows, columns), lambda at: (0, 0, 0, at_block))


def scalar_spec():
    return pl.BlockSpec(memory_space=pltpu.SMEM)


def follow(kernel, first, after):
    count = len(after)
    if not count:
        return kernel

    def late(*refs):
        return kernel(*refs[:first], *refs[first + count :])

    return late


def after_specs(after):
    return [pl.BlockSpec(memory_space=pl.ANY)] * len(after)


def call(kernel, name, ins, in_specs, outs, scratch=(), after=()):
    kernel = follow(kernel, len(ins), after)
    ins = (*ins, *after)
    in_specs = [*in_specs, *after_specs(after)]
    return pl.pallas_call(
        kernel,
        grid=(1,),
        in_specs=in_specs,
        out_specs=[whole_spec(out.shape) for out in outs],
        out_shape=outs,
        scratch_shapes=list(scratch),
        compiler_params=params(),
        name=name,
    )(*ins)


def embed_kernel(
    table_ref, ids_ref, vocab_ref, cos_ref, sin_ref, q_ref, own_ref, other_ref, resid_ref
):
    own = q_ref.shape[0]
    length = ids_ref.shape[1]
    tiles = table_ref.shape[0]
    hot = lax.broadcasted_iota(jnp.int32, (64, length), 0) == ids_ref[...]
    hot = hot.astype(single).T.astype(brain)
    resid_ref[...] = dot(hot[:own], vocab_ref[...])
    hot = hot[:, :TABLE_ROWS]
    cosine = cos_ref[...]
    sine = sin_ref[...]
    for at in range(tiles):
        lanes = slice(at * LANES, (at + 1) * LANES)
        rows = dot_exact(hot, table_ref[at])
        q_ref[:, lanes] = rotate(rows[:own, :LANES], cosine[:own], sine[:own]).astype(brain)
        keys = rotate(rows[:, LANES : 2 * LANES], cosine, sine).astype(brain)
        values = rows[:, 2 * LANES :].astype(brain)
        own_ref[0, :, lanes] = keys[:own]
        own_ref[1, :, lanes] = values[:own]
        other_ref[0, :, lanes] = keys[own:]
        other_ref[1, :, lanes] = values[own:]


def embed(table, ids, vocab, cosine, sine):
    tiles = table.shape[0]
    own = ids.shape[1] // 2
    wide = tiles * LANES
    ins = (table, ids, vocab, cosine, sine)
    outs = [
        jax.ShapeDtypeStruct((own, wide), brain),
        jax.ShapeDtypeStruct((2, own, wide), brain),
        jax.ShapeDtypeStruct((2, own, wide), brain),
        jax.ShapeDtypeStruct((own, vocab.shape[1]), single),
    ]
    return call(embed_kernel, "embed", ins, [whole_spec(x.shape) for x in ins], outs)


def attend_kernel(heads, chunk, q_ref, own_ref, other_ref, out_ref, logsum_ref):
    own = q_ref.shape[0]
    q_turned = q_ref[...].T
    keys = jnp.concatenate([own_ref[0], other_ref[0]], 0)
    v_turned = jnp.concatenate([own_ref[1], other_ref[1]], 0).T
    rows = lax.broadcasted_iota(jnp.int32, (LANES, chunk), 0)
    for start in range(0, own, chunk):
        part = slice(start, start + chunk)
        q_part = q_turned[:, part]
        mixed = jnp.zeros((LANES, chunk), single)
        for head in range(heads):
            mine = (rows >= head * HEAD) & (rows < (head + 1) * HEAD)
            scores = dot(keys, jnp.where(mine, q_part, jnp.zeros_like(q_part)))
            peak = column_max(scores) * scale_two
            weights = jnp.exp2(scores * scale_two - peak)
            total = column_sum(weights)
            probs = (weights * (1.0 / total)).astype(brain)
            mixed = jnp.where(mine, dot(v_turned, probs), mixed)
            logsum_ref[0, head : head + 1, part] = peak + jnp.log2(total)
        out_ref[part, :] = mixed.T.astype(brain)


def attend(q, kv_own, kv_other, heads):
    own, wide = q.shape
    tiles = wide // LANES
    own_spec = pl.BlockSpec((own, LANES), lambda at: (0, at))
    pair_spec = pl.BlockSpec((2, own, LANES), lambda at: (0, 0, at))
    return pl.pallas_call(
        functools.partial(attend_kernel, heads, LANES),
        grid=(tiles,),
        in_specs=[own_spec, pair_spec, pair_spec],
        out_specs=[own_spec, pl.BlockSpec((1, 8, own), lambda at: (at, 0, 0))],
        out_shape=[
            jax.ShapeDtypeStruct((own, wide), brain),
            jax.ShapeDtypeStruct((tiles, 8, own), single),
        ],
        compiler_params=params(),
        name="attend",
    )(q, kv_own, kv_other)


def attend_back_kernel(
    heads, chunk, count, me_ref, q_ref, kv_own_ref, kv_other_ref, g_ref, logsum_ref, *refs
):
    dq_ref, own_ref, other_k_ref, other_v_ref = refs[count:]
    own = q_ref.shape[0]
    q = q_ref[...]
    grad = g_ref[...]
    q_turned = q.T
    g_turned = grad.T
    keys = jnp.concatenate([kv_own_ref[0], kv_other_ref[0]], 0)
    values = jnp.concatenate([kv_own_ref[1], kv_other_ref[1]], 0)
    k_turned = keys.T
    rows = lax.broadcasted_iota(jnp.int32, (LANES, chunk), 0)
    lanes = lax.broadcasted_iota(jnp.int32, (chunk, LANES), 1)
    none = jnp.zeros((LANES, chunk), brain)
    none_low = jnp.zeros((chunk, LANES), brain)
    for start in range(0, own, chunk):
        part = slice(start, start + chunk)
        dq = jnp.zeros((LANES, chunk), single)
        for head in range(heads):
            mine = (rows >= head * HEAD) & (rows < (head + 1) * HEAD)
            mine_low = (lanes >= head * HEAD) & (lanes < (head + 1) * HEAD)
            scores = dot(keys, jnp.where(mine, q_turned[:, part], none))
            probs = jnp.exp2(scores * scale_two - logsum_ref[0, head : head + 1, part])
            g_probs = dot(values, jnp.where(mine, g_turned[:, part], none))
            inner = column_sum(probs * g_probs)
            g_scores = (probs * (g_probs - inner)).astype(brain)
            dv = dot(probs.astype(brain), jnp.where(mine_low, grad[part, :], none_low))
            dk = dot(g_scores, jnp.where(mine_low, q[part, :], none_low)) * scale
            if start == 0 and head == 0:
                own_ref[0] = dk[:own]
                own_ref[1] = dv[:own]
                other_k_ref[...] = dk[own:]
                other_v_ref[...] = dv[own:]
            else:
                own_ref[0] += dk[:own]
                own_ref[1] += dv[:own]
                other_k_ref[...] += dk[own:]
                other_v_ref[...] += dv[own:]
            dq = jnp.where(mine, dot(k_turned, g_scores), dq)
        dq_ref[part, :] = (dq * scale).T


def attend_back(q, kv_own, kv_other, grad, logsum, heads, me, turns, tensors, after=()):
    own, wide = q.shape
    first = turns[0]
    count = len(turns)

    def tile(at, me):
        return (at + first) ^ (me[0] & (tensors - 1))

    own_spec = pl.BlockSpec((own, LANES), lambda at, me: (0, tile(at, me)))
    pair_spec = pl.BlockSpec((2, own, LANES), lambda at, me: (0, 0, tile(at, me)))
    one_shape = jax.ShapeDtypeStruct((own, count * LANES), single)
    one_out = pl.BlockSpec((own, LANES), lambda at, me: (0, at))
    pair_shape = jax.ShapeDtypeStruct((2, own, count * LANES), single)
    pair_out = pl.BlockSpec((2, own, LANES), lambda at, me: (0, 0, at))
    return pl.pallas_call(
        functools.partial(attend_back_kernel, heads, own, len(after)),
        grid_spec=pltpu.PrefetchScalarGridSpec(
            num_scalar_prefetch=1,
            grid=(count,),
            in_specs=[
                own_spec,
                pair_spec,
                pair_spec,
                own_spec,
                pl.BlockSpec((1, 8, own), lambda at, me: (tile(at, me), 0, 0)),
                *after_specs(after),
            ],
            out_specs=[one_out, pair_out, one_out, one_out],
        ),
        out_shape=[one_shape, pair_shape, one_shape, one_shape],
        compiler_params=params(),
        name="attend_back",
    )(me, q, kv_own, kv_other, grad, logsum, *after)


def attention_out(mixed, resid, layer, tiles):
    parts = [
        dot(mixed[:, at * LANES : (at + 1) * LANES], layer.out(at), 1, 1) for at in range(tiles)
    ]
    return resid + add_up(parts)


def middle_kernel(
    feats, mixed_ref, resid_ref, w_ref, w_next_ref, norms_ref, cos_ref, sin_ref,
    mid_ref, next_ref, q_ref, kv_ref,
):
    tiles = w_ref.shape[1]
    layer = Layer(Gathered(w_ref), 0, (w_ref.shape[3] - LANES) // 2)
    mid = attention_out(mixed_ref[...], resid_ref[...], layer, tiles)
    mid_ref[...] = mid
    normed = feats.norm(mid, norms_ref[2:3], norms_ref[3:4])
    parts = []
    for at in range(tiles):
        act = gelu(dot(normed, layer.up(at))).astype(brain)
        parts.append(dot(act, layer.down(at), 1, 1))
    total = mid + add_up(parts)
    next_ref[...] = total
    normed = feats.norm(total, norms_ref[4:5], norms_ref[5:6])
    weights = Gathered(w_next_ref)
    cosine = cos_ref[...]
    sine = sin_ref[...]
    for at in range(tiles):
        lanes = slice(at * LANES, (at + 1) * LANES)
        rows = dot(normed, weights.block(at, 0, 3 * LANES))
        q_ref[:, lanes] = rotate(rows[:, :LANES], cosine, sine).astype(brain)
        kv_ref[0, :, lanes] = rotate(rows[:, LANES : 2 * LANES], cosine, sine).astype(brain)
        kv_ref[1, :, lanes] = rows[:, 2 * LANES :].astype(brain)


def middle(feats, mixed, resid, weights, columns, at_heads, norms, cosine, sine):
    own, wide = mixed.shape
    plain = jax.ShapeDtypeStruct(resid.shape, single)
    in_specs = [
        whole_spec(mixed.shape),
        whole_spec(resid.shape),
        columns_spec(weights, columns, 0),
        columns_spec(weights, 3 * LANES, at_heads),
        whole_spec(norms.shape),
        whole_spec(cosine.shape),
        whole_spec(sine.shape),
    ]
    outs = [
        plain,
        plain,
        jax.ShapeDtypeStruct((own, wide), brain),
        jax.ShapeDtypeStruct((2, own, wide), brain),
    ]
    ins = (mixed, resid, weights, weights, norms, cosine, sine)
    return call(functools.partial(middle_kernel, feats), "middle", ins, in_specs, outs)


def feed_back(
    feats, turns, g_resid, mid, normed, mixed_ref, layer, gain, act_ref, slope_ref,
    grads, base, g_mid_ref, g_mixed_ref,
):
    hidden = layer.hidden
    g_low = g_resid.astype(brain)
    g_turned = g_low.T
    normed_turned = normed.T
    parts = []
    for turn, tile in turns:
        g_hidden = (dot(g_low, layer.down(tile)) * slope_ref[turn]).astype(brain)
        grads.store(tile, turn, base + LANES + hidden, dot(g_turned, act_ref[turn]))
        grads.store(tile, turn, base + LANES, dot(normed_turned, g_hidden))
        parts.append(dot(g_hidden, layer.up(tile), 1, 1))
    g_normed = add_up(parts)
    unit, inverse = feats.centred(mid)
    g_gain = jnp.sum(g_normed * unit, 0, keepdims=True)
    g_shift = jnp.sum(g_normed, 0, keepdims=True)
    g_mid = g_resid + feats.norm_back(unit, inverse, gain, g_normed)
    g_mid_ref[...] = g_mid
    g_low = g_mid.astype(brain)
    g_turned = g_low.T
    for turn, tile in turns:
        lanes = tile_lanes(tile)
        g_mixed_ref[:, lanes] = dot(g_low, layer.out(tile)).astype(brain)
        grads.store(tile, turn, base, dot(g_turned, mixed_ref[:, lanes]))
    return g_gain, g_shift


def top_kernel(
    feats, cube, vocab_count, grad_orders, me_ref, mixed_ref, resid_ref, w_ref, norms_ref,
    vocab_ref, slot_ref, target_ref, count_ref, keep_ref, send_ref, g_mid_ref, g_mixed_ref,
    g_norms_ref, g_vocab_ref, act_ref, slope_ref,
):
    me = me_ref[0]
    tiles = cube.tensors
    turns = [(turn, turn ^ (me & (tiles - 1))) for turn in range(tiles)]
    grads = Scattered(cube, me, keep_ref, send_ref, grad_orders)
    layer = Layer(Gathered(w_ref), 3 * LANES, act_ref.shape[2])
    mid = attention_out(mixed_ref[...], resid_ref[...], layer, tiles)
    normed = feats.norm(mid, norms_ref[6:7], norms_ref[7:8])
    parts = []
    for turn, tile in turns:
        hidden = dot(normed, layer.up(tile))
        share = normal_share(hidden)
        act = (hidden * share).astype(brain)
        act_ref[turn] = act
        slope_ref[turn] = gelu_slope(hidden, share)
        parts.append(dot(act, layer.down(tile), 1, 1))
    total = mid + add_up(parts)
    unit, inverse = feats.centred(total)
    gain = norms_ref[8:9]
    final = (unit * gain + norms_ref[9:10]).astype(brain)
    own = total.shape[0]
    slots = slot_ref.shape[0]
    vocab = vocab_ref[...]
    where_hot = (lax.broadcasted_iota(jnp.int32, (slots, own), 1) == slot_ref[...]).astype(single)
    where_hot = where_hot.astype(brain)
    present = (slot_ref[...] >= 0).astype(single)
    picked = dot(where_hot, final).astype(brain)
    logits = dot(picked, vocab, 1, 1)
    lane = lax.broadcasted_iota(jnp.int32, logits.shape, 1)
    logits = jnp.where(lane < vocab_count, logits, -1e30)
    peak = jnp.max(logits, 1, keepdims=True)
    logsum = peak + jnp.log(jnp.sum(jnp.exp(logits - peak), 1, keepdims=True))
    target_hot = (lane == target_ref[...]).astype(single)
    target_logit = jnp.sum(
        jnp.where(lane < vocab_count, logits * target_hot, 0.0), 1, keepdims=True
    )
    loss = jnp.sum((logsum - target_logit) * present, 0, keepdims=True)
    share = present / count_ref[0:1, 0:1]
    g_logits = ((jnp.exp(logits - logsum) - target_hot) * share).astype(brain)
    g_vocab_ref[...] = dot(g_logits, picked, 0, 0)[:TABLE_ROWS]
    g_picked = dot(g_logits, vocab)
    g_final = dot_exact(where_hot, g_picked, 0, 0)
    g_norms_ref[...] = jnp.zeros_like(g_norms_ref)
    g_norms_ref[8:9] = jnp.sum(g_final * unit, 0, keepdims=True)
    g_norms_ref[9:10] = jnp.sum(g_final, 0, keepdims=True)
    g_norms_ref[LOSS_ROW : LOSS_ROW + 1] = jnp.broadcast_to(loss, (1, g_norms_ref.shape[1]))
    g_resid = feats.norm_back(unit, inverse, gain, g_final)
    g_gain, g_shift = feed_back(
        feats, turns, g_resid, mid, normed, mixed_ref, layer, norms_ref[6:7], act_ref, slope_ref,
        grads, 0, g_mid_ref, g_mixed_ref,
    )
    g_norms_ref[6:7] = g_gain
    g_norms_ref[7:8] = g_shift


def top(
    feats, cube, grad_orders, me, mixed, resid, weights, columns, at_block, norms, vocab,
    vocab_count, slot, target, count,
):
    own, wide = mixed.shape
    tiles = cube.tensors
    rows = weights.shape[2]
    hidden = (columns - 4 * LANES) // 2
    pieces = len(grad_orders)
    grads = (pieces, cube.devices // 2, rows, (columns - 3 * LANES) // pieces)
    outs = [
        jax.ShapeDtypeStruct(grads, single),
        jax.ShapeDtypeStruct(grads, single),
        jax.ShapeDtypeStruct(resid.shape, single),
        jax.ShapeDtypeStruct(mixed.shape, brain),
        jax.ShapeDtypeStruct(norms.shape, single),
        jax.ShapeDtypeStruct((TABLE_ROWS, resid.shape[1]), single),
    ]
    in_specs = [
        scalar_spec(),
        whole_spec(mixed.shape),
        whole_spec(resid.shape),
        columns_spec(weights, columns, at_block),
        whole_spec(norms.shape),
        whole_spec(vocab.shape),
        whole_spec(slot.shape),
        whole_spec(target.shape),
        whole_spec(count.shape),
    ]
    scratch = [
        pltpu.VMEM((tiles, own, hidden), brain),
        pltpu.VMEM((tiles, own, hidden), single),
    ]
    ins = (me, mixed, resid, weights, norms, vocab, slot, target, count)
    kernel = functools.partial(top_kernel, feats, cube, vocab_count, grad_orders)
    return call(kernel, "top", ins, in_specs, outs, scratch)


def head_grads(turn, heads_refs, cosine, sine):
    dq_ref, own_ref, other_k_ref, other_v_ref = heads_refs[4 * (turn // 2) : 4 * (turn // 2) + 4]
    lanes = tile_lanes(turn % 2)
    other = tile_lanes(1 - turn % 2)
    g_q = unrotate(dq_ref[:, lanes], cosine, sine)
    g_k = unrotate(own_ref[0, :, lanes] + other_k_ref[:, other], cosine, sine)
    g_v = own_ref[1, :, lanes] + other_v_ref[:, other]
    return jnp.concatenate([g_q, g_k, g_v], 1).astype(brain)


def lower_kernel(feats, cube, grad_orders, me_ref, *refs):
    heads_refs = refs[:8]
    (
        g_mid_in_ref, resid_ref, mid_ref, mixed_ref, w_in_ref, w_ref, norms_ref, cos_ref, sin_ref,
        g_norms_in_ref, keep_ref, send_ref, g_mid_ref, g_mixed_ref, g_norms_ref,
        act_ref, slope_ref,
    ) = refs[8:]
    me = me_ref[0]
    tiles = cube.tensors
    turns = [(turn, turn ^ (me & (tiles - 1))) for turn in range(tiles)]
    layer = Layer(Gathered(w_ref), 0, act_ref.shape[2])
    weights = Gathered(w_in_ref)
    grads = Scattered(cube, me, keep_ref, send_ref, grad_orders)
    unit, inverse = feats.centred(resid_ref[...])
    gain = norms_ref[4:5]
    normed_turned = (unit * gain + norms_ref[5:6]).astype(brain).T
    cosine = cos_ref[...]
    sine = sin_ref[...]
    parts = []
    for turn, tile in turns:
        g_heads = head_grads(turn, heads_refs, cosine, sine)
        grads.store(tile, turn, 0, dot(normed_turned, g_heads))
        parts.append(dot(g_heads, weights.block(tile, 0, 3 * LANES), 1, 1))
    g_normed = add_up(parts)
    g_norms_ref[...] = g_norms_in_ref[...]
    g_norms_ref[4:5] = jnp.sum(g_normed * unit, 0, keepdims=True)
    g_norms_ref[5:6] = jnp.sum(g_normed, 0, keepdims=True)
    g_resid = g_mid_in_ref[...] + feats.norm_back(unit, inverse, gain, g_normed)
    mid = mid_ref[...]
    normed = feats.norm(mid, norms_ref[2:3], norms_ref[3:4])
    for turn, tile in turns:
        hidden = dot(normed, layer.up(tile))
        share = normal_share(hidden)
        act_ref[turn] = (hidden * share).astype(brain)
        slope_ref[turn] = gelu_slope(hidden, share)
    g_gain, g_shift = feed_back(
        feats, turns, g_resid, mid, normed, mixed_ref, layer, norms_ref[2:3], act_ref, slope_ref,
        grads, 3 * LANES, g_mid_ref, g_mixed_ref,
    )
    g_norms_ref[2:3] = g_gain
    g_norms_ref[3:4] = g_shift


def lower(
    feats, cube, grad_orders, me, head_parts, g_mid, resid, mid, mixed, weights, at_heads,
    feed_columns, norms, cosine, sine, g_norms, after,
):
    own, wide = mixed.shape
    tiles = cube.tensors
    rows = weights.shape[2]
    hidden = (feed_columns - LANES) // 2
    columns = feed_columns + 3 * LANES
    count = len(grad_orders)
    grads = (count, cube.devices // 2, rows, columns // count)
    outs = [
        jax.ShapeDtypeStruct(grads, single),
        jax.ShapeDtypeStruct(grads, single),
        jax.ShapeDtypeStruct(resid.shape, single),
        jax.ShapeDtypeStruct(mixed.shape, brain),
        jax.ShapeDtypeStruct(norms.shape, single),
    ]
    before = (*head_parts, g_mid, resid, mid, mixed)
    rest = (norms, cosine, sine, g_norms)
    in_specs = [
        scalar_spec(),
        *[whole_spec(x.shape) for x in before],
        columns_spec(weights, 3 * LANES, at_heads),
        columns_spec(weights, feed_columns, 0),
        *[whole_spec(x.shape) for x in rest],
    ]
    scratch = [
        pltpu.VMEM((tiles, own, hidden), brain),
        pltpu.VMEM((tiles, own, hidden), single),
    ]
    ins = (me, *before, weights, weights, *rest)
    kernel = functools.partial(lower_kernel, feats, cube, grad_orders)
    return call(kernel, "lower", ins, in_specs, outs, scratch, after)


def stacked_lanes(ref, row, value):
    rows = value.shape[0]
    for at in range(value.shape[1] // LANES):
        ref[row : row + rows, :] = value[:, at * LANES : (at + 1) * LANES]
        row += rows
    return row


def side_by_side(x, rows):
    return jnp.concatenate([x[at : at + rows] for at in range(0, x.shape[0], rows)], 1)


def bottom_kernel(
    feats, cube, me_ref, *refs
):
    heads_refs = refs[:8]
    (
        g_mid_ref, ids_ref, w_ref, norms_ref, vocab_ref, g_vocab_in_ref, g_norms_in_ref, cos_ref,
        sin_ref, keep_ref, send_ref, norms_out_ref,
    ) = refs[8:]
    tiles = cube.tensors
    own = g_mid_ref.shape[0]
    mine = me_ref[0] & (tiles - 1)
    hot = lax.broadcasted_iota(jnp.int32, (TABLE_ROWS, own), 0) == ids_ref[...]
    hot = hot.astype(single).astype(brain)
    cosine = cos_ref[...]
    sine = sin_ref[...]
    weights = Gathered(w_ref)
    refs = (keep_ref, send_ref)
    rows = [0, 0]
    parts = []
    for turn in range(tiles):
        tile = turn ^ mine
        g_table = dot(hot, head_grads(turn, heads_refs, cosine, sine))
        rows[turn & 1] = stacked_lanes(refs[turn & 1], rows[turn & 1], g_table)
        weight = weights.block(tile, 0, 3 * LANES)
        high, middle_part, low = split_three(g_table)
        parts.append(dot(high, weight, 1, 1))
        parts.append(dot(middle_part, weight, 1, 1))
        parts.append(dot(low, weight, 1, 1))
    g_normed = add_up(parts)
    unit, inverse = feats.centred(vocab_ref[...].astype(single)[:TABLE_ROWS])
    norms_out_ref[...] = g_norms_in_ref[...]
    norms_out_ref[0:1] = jnp.sum(g_normed * unit, 0, keepdims=True)
    norms_out_ref[1:2] = jnp.sum(g_normed, 0, keepdims=True)
    g_norms = norms_out_ref[...]
    g_rows = feats.norm_back(unit, inverse, norms_ref[0:1], g_normed)
    g_vocab = g_vocab_in_ref[...] + (dot_exact(hot, g_mid_ref[...]) + g_rows)
    for ref, row in zip(refs, rows):
        row = stacked_lanes(ref, row, g_vocab)
        stacked_lanes(ref, row, g_norms)


def bottom(
    feats, cube, me, head_parts, g_mid, ids, w_in, at_block, norms, vocab, g_vocab,
    g_norms, cosine, sine, after,
):
    tiles = cube.tensors
    table_rows = 3 * TABLE_ROWS * tiles // 2
    vector_rows = (g_vocab.shape[0] + g_norms.shape[0]) * g_vocab.shape[1] // LANES
    out = jax.ShapeDtypeStruct((table_rows + vector_rows, LANES), single)
    before = (*head_parts, g_mid, ids)
    rest = (norms, vocab, g_vocab, g_norms, cosine, sine)
    in_specs = [
        scalar_spec(),
        *[whole_spec(x.shape) for x in before],
        columns_spec(w_in, 3 * LANES, at_block),
        *[whole_spec(x.shape) for x in rest],
    ]
    outs = [out, out, jax.ShapeDtypeStruct(norms.shape, single)]
    ins = (me, *before, w_in, *rest)
    kernel = functools.partial(bottom_kernel, feats, cube)
    return call(kernel, "bottom", ins, in_specs, outs, (), after)[:2]


def halve_kernel(count, together, stacked, skip, keep_ref, *refs):
    got_count = 1 if together else count
    got = refs[:got_count]
    outs = refs[got_count + skip :]
    size = keep_ref.shape[1]
    half = size // 2
    for part in range(count):
        arrived = got[0].at[part] if together else got[part]
        if size == 1:
            outs[0][part] = keep_ref[part] + arrived[...]
        else:
            outs[0][part] = keep_ref[part, :half] + arrived[:half]
            send = outs[1].at[part] if stacked else outs[1 + part]
            send[...] = keep_ref[part, half:] + arrived[half:]


def halve(keep, got, through=(), after=(), stacked=False):
    count, size, rows, wide = keep.shape
    together = not isinstance(got, list)
    got = [got] if together else got
    step = 16 if size >= 8 else rows
    half = max(size // 2, 1)

    def spec(*lead):
        return pl.BlockSpec((*lead, step, wide), lambda at: (*([0] * len(lead)), at, 0))

    outs = [jax.ShapeDtypeStruct((count, half, rows, wide), single)]
    out_specs = [spec(count, half)]
    if size > 1 and stacked:
        outs += outs
        out_specs += out_specs
    elif size > 1:
        outs += [jax.ShapeDtypeStruct((half, rows, wide), single)] * count
        out_specs += [spec(half)] * count
    sends = len(outs) - 1
    got_specs = [spec(count, size)] if together else [spec(size)] * count
    ins = (keep, *got)
    aliases = {len(ins) + at: len(outs) + at for at in range(len(through))}
    outs += [jax.ShapeDtypeStruct(x.shape, x.dtype) for x in through]
    results = pl.pallas_call(
        functools.partial(halve_kernel, count, together, stacked, len(through) + len(after)),
        grid=(rows // step,),
        in_specs=[spec(count, size), *got_specs, *after_specs(through), *after_specs(after)],
        out_specs=[*out_specs, *after_specs(through)],
        out_shape=outs,
        input_output_aliases=aliases,
        compiler_params=params(),
        name="halve",
    )(*ins, *through, *after)
    going = results[1] if stacked and sends else results[1 : 1 + sends]
    return results[0], going, results[1 + sends :]


def normalize_features(resid, gain, shift):
    centre = resid - jnp.mean(resid, -1, keepdims=True)
    spread = jnp.mean(centre * centre, -1, keepdims=True)
    return centre * lax.rsqrt(spread + norm_eps) * gain + shift


def adamw(master, first, second, grad, step_rate):
    mean = beta_first * first + (1.0 - beta_first) * grad
    square = beta_second * second + (1.0 - beta_second) * grad * grad
    corrected = mean / (1.0 - beta_first**STEP)
    rescaled_values = square / (1.0 - beta_second**STEP)
    fresh = master - step_rate * (
        corrected / (jnp.sqrt(rescaled_values) + adam_eps) + weight_decay * master
    )
    return (fresh, mean, square)


def pad_lanes(x, lanes):
    return jnp.pad(x, [(0, 0)] * (x.ndim - 1) + [(0, lanes - x.shape[-1])])


def make_shards(groups, tensors):
    axes = ("dp", "tensor")
    cube = Cube(groups, tensors)

    def shards(
        token_ids,
        mask_pos,
        mask_target,
        mask_count,
        weight_in,
        weight_out,
        weight_up,
        weight_down,
        norm_params,
        vocab_table,
        first_in,
        first_out,
        first_up,
        first_down,
        first_norm,
        first_vocab,
        second_in,
        second_out,
        second_up,
        second_down,
        second_norm,
        second_vocab,
    ):
        layers, block, in_wide = weight_in.shape
        heads = in_wide // (3 * HEAD)
        per_heads = heads * HEAD
        hidden = weight_up.shape[2]
        hidden_padded = -(-hidden // LANES) * LANES
        vocab_count, width = vocab_table.shape
        feats = Features(width, groups)
        local_len = token_ids.shape[1]
        length = local_len * tensors
        own = length // 2
        here = lax.axis_index("tensor")
        group_at = lax.axis_index("dp")
        me = (group_at * tensors + here).astype(jnp.int32).reshape(1)
        sequence = here // 2
        quarters = jnp.stack([here, here ^ 2, here ^ 1, here ^ 3])

        heads_in = weight_in.astype(brain).transpose(1, 0, 2)
        heads_in = heads_in.reshape(block, layers, heads, 3, HEAD).transpose(0, 1, 3, 2, 4)
        heads_in = pad_lanes(heads_in.reshape(block, layers, 3, per_heads), LANES)
        heads_in = heads_in.reshape(block, layers, 3 * LANES)
        feed = jnp.concatenate(
            [
                pad_lanes(weight_out.astype(brain).transpose(2, 0, 1), LANES),
                pad_lanes(weight_up.astype(brain).transpose(1, 0, 2), hidden_padded),
                pad_lanes(weight_down.astype(brain).transpose(2, 0, 1), hidden_padded),
            ],
            2,
        )
        feed_columns = feed.shape[2]
        all_columns = 3 * LANES + feed_columns

        def pad_rows(x):
            return jnp.pad(x, ((0, feats.padded - block), (0, 0)))

        vocab_low = vocab_table.astype(brain)
        vocab_padded = jnp.pad(feats.pad(vocab_low), ((0, 64 - vocab_count), (0, 0)))
        norms = jnp.pad(feats.pad(norm_params), ((0, 16 - norm_params.shape[0]), (0, 0)))

        table_low = normalize_features(
            lax.reduce_precision(vocab_table, 8, 7), norm_params[0], norm_params[1]
        ).astype(brain)
        table_own = lax.dynamic_slice_in_dim(
            table_low.reshape(vocab_count, groups, block), group_at, 1, 1
        )[:, 0]
        table = dot(table_own, heads_in[:, 0])
        extra = jnp.zeros((TABLE_ROWS - vocab_count, 3 * LANES), single)
        extra = extra.at[0, 0].set(jnp.sum(mask_count).astype(single))
        table = jnp.concatenate([table, extra], 0)
        for at in range(2, cube.size):
            table = table + cube.swap(table, at)
        count_total = table[vocab_count, 0]
        ids_row = vocab_count + 1
        table = lax.dynamic_update_slice(
            table, pad_lanes(token_ids.astype(single), 3 * LANES), (ids_row, 0)
        )
        got = cube.swap(table, 1)
        upper = (here & 2) == 2
        pair = jnp.stack([jnp.where(upper, got, table), jnp.where(upper, table, got)])
        got = cube.swap(pair, 0)
        upper = (here & 1) == 1
        table = jnp.stack([jnp.where(upper, got, pair), jnp.where(upper, pair, got)], 1)
        table = table.reshape(tensors, TABLE_ROWS, 3 * LANES)
        ids = jnp.take(table[:, ids_row : ids_row + 2, :local_len], sequence, axis=1)
        ids = jnp.take(ids, quarters, axis=0).reshape(1, length).astype(jnp.int32)

        packed = [feed[:, 0], heads_in[:, 0], heads_in[:, 1], feed[:, 1]]
        packed = pad_rows(jnp.concatenate(packed, 1))
        weights = lax.all_gather(packed, axes, axis=0, tiled=False)
        weights = weights.reshape((groups, tensors) + packed.shape)
        at_low = feed_columns // (3 * LANES)
        at_heads = at_low + 1

        half = HEAD // 2
        freqs = 10000.0 ** (-jnp.arange(half, dtype=single) * 2.0 / HEAD)
        positions = (quarters[:, None] * local_len + jnp.arange(local_len)[None, :]).reshape(length)
        angles = positions.astype(single)[:, None] * freqs[None, :]
        cosine, sine = (jnp.cos(angles), jnp.sin(angles))
        cosine = pad_lanes(jnp.tile(jnp.concatenate([cosine, cosine], 1), (1, heads)), LANES)
        sine = pad_lanes(jnp.tile(jnp.concatenate([-sine, sine], 1), (1, heads)), LANES)
        cos_own, sin_own = (cosine[:own], sine[:own])

        slots = mask_pos.shape[1]
        my_pos = jnp.take(mask_pos, sequence, axis=0)
        my_count = jnp.take(mask_count, sequence, axis=0)
        quarter = my_pos // local_len
        inside = my_pos % local_len
        slot = jnp.where(
            quarter == here, inside, jnp.where(quarter == (here ^ 2), inside + local_len, -1)
        )
        slot = jnp.where(jnp.arange(slots) < my_count, slot, -1).reshape(slots, 1)
        target = jnp.take(mask_target, sequence, axis=0).reshape(slots, 1)
        count = jnp.broadcast_to(count_total, (8, LANES))

        q_low, kv_low, kv_low_other, resid_low = embed(table, ids, vocab_padded, cosine, sine)
        mixed_low, logsum_low = attend(q_low, kv_low, kv_low_other, heads)
        mid_low, resid, q, kv = middle(
            feats, mixed_low, resid_low, weights, feed_columns, at_heads, norms, cos_own, sin_own
        )
        kv_other = cube.swap(kv, 0)
        mixed, logsum = attend(q, kv, kv_other, heads)
        grad_orders = [cube.outer(turn) for turn in range(3)]

        last_step = cube.size - 2

        class Sums:
            def __init__(self, keep, send):
                self.keep = keep
                self.got = cube.swap(send, 0)
                self.at = 0

            def step(self, through=(), after=()):
                stacked = self.at == last_step
                self.keep, sends, through = halve(self.keep, self.got, through, after, stacked)
                if stacked:
                    self.got = cube.swap(sends, grad_orders[0][-1])
                else:
                    self.got = [
                        cube.swap(x, order[self.at]) for x, order in zip(sends, grad_orders)
                    ]
                self.at += 1
                return through

            def finish(self, after=()):
                return halve(self.keep, self.got, (), after)[0][:, 0]

        def exchange(arrays):
            return [cube.swap(x, 0) for x in arrays]

        first_turns = list(range(tensors // 2))
        last_turns = list(range(tensors // 2, tensors))
        keep, send, g_mid, g_mixed, g_norms, g_vocab = top(
            feats, cube, grad_orders, me, mixed, resid, weights, all_columns, 1, norms,
            vocab_padded, vocab_count, slot, target, count,
        )
        sums_top = Sums(keep, send)
        part = (q, kv, kv_other, g_mixed, logsum, heads, me)
        first = attend_back(*part, first_turns, tensors)
        got_first = exchange(sums_top.step(first[2:], (first[0],)))
        last = attend_back(*part, last_turns, tensors, (sums_top.keep, *got_first))
        got_last = exchange(sums_top.step(last[2:], (last[0],)))
        head_parts = (*first[:2], *got_first, *last[:2], *got_last)
        keep, send, g_mid, g_mixed, g_norms = lower(
            feats, cube, grad_orders, me, head_parts, g_mid, resid, mid_low, mixed_low, weights,
            at_heads, feed_columns, norms, cos_own, sin_own, g_norms, (sums_top.keep,),
        )
        (send,) = sums_top.step((send,), (g_mid,))
        sums_low = Sums(keep, send)
        part = (q_low, kv_low, kv_low_other, g_mixed, logsum_low, heads, me)
        first = attend_back(*part, first_turns, tensors, (sums_top.keep,))
        got_first = exchange(sums_top.step(first[2:], (first[0],)))
        sums_low.step((), (sums_top.keep,))
        last = attend_back(*part, last_turns, tensors, (sums_low.keep, *got_first))
        got_last = exchange(sums_low.step(last[2:], (last[0],)))
        head_parts = (*first[:2], *got_first, *last[:2], *got_last)
        keep_table, send_table = bottom(
            feats, cube, me, head_parts, g_mid, ids[:, :own], weights, at_low, norms,
            vocab_padded, g_vocab, g_norms, cos_own, sin_own, (sums_low.keep,),
        )
        sums_low.step((), (keep_table,))
        while sums_low.at <= last_step:
            sums_low.step()
        while sums_top.at <= last_step:
            sums_top.step((), (keep_table,))
        grads_top = jnp.concatenate(list(sums_top.finish((keep_table,))), 1)
        grads_low = jnp.concatenate(list(sums_low.finish()), 1)
        total = keep_table + cube.swap(send_table, 0)
        tile_rows = 3 * TABLE_ROWS
        got = cube.swap(total[tile_rows:], 1)
        total = jnp.concatenate(
            [total[:tile_rows] + got[:tile_rows], total[2 * tile_rows :] + got[tile_rows:]], 0
        )
        for at in range(2, cube.size):
            total = total + cube.swap(total, at)
        g_table = side_by_side(total[:tile_rows], TABLE_ROWS)[:vocab_count]
        vocab_rows = TABLE_ROWS * feats.total // LANES
        g_vocab = side_by_side(total[tile_rows : tile_rows + vocab_rows], TABLE_ROWS)
        g_vocab = feats.unpad(g_vocab[:vocab_count])
        g_norms = side_by_side(total[tile_rows + vocab_rows :], norms.shape[0])
        loss_total = g_norms[LOSS_ROW, 0]
        g_norms = feats.unpad(g_norms[: norm_params.shape[0]])
        grads_in_low = lax.dot_general(
            table_own.astype(single),
            g_table,
            (((0,), (0,)), ((), ())),
            precision=highest,
            preferred_element_type=single,
        )

        def unpack_in(grad):
            grad = grad[:block].reshape(block, 3, LANES)[:, :, :per_heads]
            return grad.reshape(block, 3, heads, HEAD).transpose(0, 2, 1, 3).reshape(block, in_wide)

        grad_in = jnp.stack([unpack_in(grads_in_low), unpack_in(grads_low[:, : 3 * LANES])], 1)
        both = jnp.stack([grads_low[:block, 3 * LANES :], grads_top[:block]], 1)
        grad_in = grad_in.transpose(1, 0, 2)
        grad_out = both[:, :, :per_heads].transpose(1, 2, 0)
        grad_up = both[:, :, LANES : LANES + hidden].transpose(1, 0, 2)
        start = LANES + hidden_padded
        grad_down = both[:, :, start : start + hidden].transpose(1, 2, 0)

        masters = (weight_in, weight_out, weight_up, weight_down, norm_params, vocab_table)
        firsts = (first_in, first_out, first_up, first_down, first_norm, first_vocab)
        seconds = (second_in, second_out, second_up, second_down, second_norm, second_vocab)
        grads = (grad_in, grad_out, grad_up, grad_down, g_norms, g_vocab)
        results = [
            adamw(masters[which], firsts[which], seconds[which], grads[which], step_rates[which])
            for which in range(6)
        ]
        news = [entry[0] for entry in results]
        means = [entry[1] for entry in results]
        squares = [entry[2] for entry in results]
        copies = [news[which].astype(brain) for which in (0, 1, 2, 3, 5)]
        return (loss_total, count_total, *news, *means, *squares, *copies)

    return shards


def solution(mesh):
    rows_in = P(None, "dp", "tensor")
    rows_out = P(None, "tensor", "dp")
    six = (rows_in, rows_out, rows_in, rows_out, P(), P())
    five = (rows_in, rows_out, rows_in, rows_out, P())
    return jax.shard_map(
        make_shards(mesh.shape["dp"], mesh.shape["tensor"]),
        mesh=mesh,
        in_specs=(P("dp", "tensor"), P("dp", None), P("dp", None), P("dp"), *six, *six, *six),
        out_specs=(P(), P(), *six, *six, *six, *five),
        check_vma=False,
    )
```

```python
import functools
import math

import jax
import jax.numpy as jnp
from jax import lax
from jax.experimental import pallas as pl
from jax.experimental.layout import Layout, with_layout_constraint
from jax.experimental.pallas import tpu as pltpu
from jax.sharding import PartitionSpec as P

HEAD = 24
STEP = 5
LANES = 128
TABLE_ROWS = 40
LOSS_ROW = 10
VMEM_BYTES = 60 * 1024 * 1024

norm_eps = 1e-05
step_rates = (0.02, 0.3, 0.02, 0.02, 0.3, 0.05)
beta_first = 0.5
beta_second = 0.5
adam_eps = 1e-08
weight_decay = 0.01
highest = lax.Precision.HIGHEST
brain = jnp.bfloat16
single = jnp.float32
scale = HEAD ** (-0.5)
scale_two = scale * math.log2(math.e)

params = functools.partial(pltpu.CompilerParams, vmem_limit_bytes=VMEM_BYTES)


class Cube:
    def __init__(self, groups, tensors):
        self.groups = groups
        self.tensors = tensors
        self.devices = groups * tensors
        self.size = self.devices.bit_length() - 1
        self.masks = [1 << at for at in range(self.size)]
        self.folded = groups >= 4
        if self.folded:
            self.masks[-1] |= self.masks[-2]

    def swap(self, x, at):
        mask = self.masks[at]
        pairs = [(device, device ^ mask) for device in range(self.devices)]
        return lax.ppermute(x, ("dp", "tensor"), pairs)

    def outer(self, turn):
        rest = list(range(1, self.size))
        rest = rest[1:2] + rest[:1] + rest[2:]
        turning = rest[:-1]
        turn = turn % len(turning)
        return turning[turn:] + turning[:turn] + rest[-1:]

    def steps(self, offset):
        bits = [(offset >> at) & 1 for at in range(self.size)]
        if self.folded:
            bits[-2] = bits[-2] ^ bits[-1]
        return bits

    def slot(self, offset, order):
        bits = self.steps(offset)
        place = 0
        for rank, at in enumerate(order):
            place = place + (bits[at] << rank)
        return place


def dot(left, right, left_dim=1, right_dim=0):
    return lax.dot_general(
        left, right, (((left_dim,), (right_dim,)), ((), ())), preferred_element_type=single
    )


def split_three(x):
    high = x.astype(brain)
    rest = x - high.astype(single)
    middle = rest.astype(brain)
    return high, middle, (rest - middle.astype(single)).astype(brain)


def dot_exact(hot, x, left_dim=1, right_dim=0):
    high, middle, low = split_three(x)
    tail = dot(hot, middle, left_dim, right_dim) + dot(hot, low, left_dim, right_dim)
    return dot(hot, high, left_dim, right_dim) + tail


def fold_rows(x, op, parts=8):
    size = x.shape[0] // parts
    pieces = [x[at * size : (at + 1) * size] for at in range(parts)]
    while len(pieces) > 1:
        pieces = [op(pieces[at], pieces[at + 1]) for at in range(0, len(pieces), 2)]
    return pieces[0]


def column_max(x):
    return jnp.max(fold_rows(x, jnp.maximum), 0, keepdims=True)


def column_sum(x):
    return jnp.sum(fold_rows(x, jnp.add), 0, keepdims=True)


erf_top = (
    -2.72614225801306e-10,
    2.77068142495902e-08,
    -2.10102402082508e-06,
    -5.69250639462346e-05,
    -7.34990630326855e-04,
    -2.95459980854025e-03,
    -1.60960333262415e-02,
)
erf_bottom = (
    -1.45660718464996e-05,
    -2.13374055278905e-04,
    -1.68282697438203e-03,
    -7.37332916720468e-03,
    -1.42647390514189e-02,
)


def erf(x):
    x = jnp.clip(x, -4.0, 4.0)
    square = x * x
    top = jnp.full_like(x, erf_top[0])
    for term in erf_top[1:]:
        top = top * square + term
    bottom = jnp.full_like(x, erf_bottom[0])
    for term in erf_bottom[1:]:
        bottom = bottom * square + term
    return x * top / bottom


def normal_share(x):
    return 0.5 + 0.5 * erf(x * math.sqrt(0.5))


def gelu(x):
    return x * normal_share(x)


def gelu_slope(x, share):
    return share + x * jnp.exp(-0.5 * x * x) * (1.0 / math.sqrt(2.0 * math.pi))


def rotary_partner(x):
    lane = lax.broadcasted_iota(jnp.int32, x.shape, 1) % HEAD
    return jnp.where(
        lane < HEAD // 2,
        pltpu.roll(x, LANES - HEAD // 2, 1),
        pltpu.roll(x, HEAD // 2, 1),
    )


def rotate(x, cosine, sine):
    return x * cosine + rotary_partner(x) * sine


def unrotate(x, cosine, sine):
    return x * cosine - rotary_partner(x) * sine


class Features:
    def __init__(self, width, groups):
        self.width = width
        self.groups = groups
        self.block = width // groups
        self.padded = -(-self.block // 16) * 16
        self.total = self.padded * groups

    def pad(self, x):
        rows = x.shape[0]
        x = x.reshape(rows, self.groups, self.block)
        x = jnp.pad(x, ((0, 0), (0, 0), (0, self.padded - self.block)))
        return x.reshape(rows, self.total)

    def unpad(self, x):
        rows = x.shape[0]
        x = x.reshape(rows, self.groups, self.padded)[:, :, : self.block]
        return x.reshape(rows, self.width)

    def live(self, shape):
        lane = lax.broadcasted_iota(jnp.int32, shape, 1) % self.padded
        return lane < self.block

    def centred(self, x):
        mean = jnp.sum(x, 1, keepdims=True) * (1.0 / self.width)
        centre = jnp.where(self.live(x.shape), x - mean, 0.0)
        spread = jnp.sum(centre * centre, 1, keepdims=True) * (1.0 / self.width)
        inverse = lax.rsqrt(spread + norm_eps)
        return centre * inverse, inverse

    def norm(self, x, gain, shift):
        unit, _ = self.centred(x)
        return (unit * gain + shift).astype(brain)

    def norm_back(self, unit, inverse, gain, grad):
        scaled = grad * gain
        mean = jnp.sum(scaled, 1, keepdims=True) * (1.0 / self.width)
        along = jnp.sum(scaled * unit, 1, keepdims=True) * (1.0 / self.width)
        back = inverse * (scaled - mean - unit * along)
        return jnp.where(self.live(back.shape), back, 0.0)


class Gathered:
    def __init__(self, ref):
        self.ref = ref

    def block(self, place, start, stop):
        groups, _, rows, _ = self.ref.shape
        return self.ref[:, place[1], :, start:stop].reshape(groups * rows, stop - start)


class Relative:
    def __init__(self, cube, me, refs, orders):
        self.cube = cube
        self.me = me
        self.refs = refs
        self.orders = orders

    def block(self, place, start, stop):
        turn, tile = place
        ref = self.refs[turn & 1]
        wide = ref.shape[-1]
        pieces = []
        while start < stop:
            part, first = divmod(start, wide)
            last = min(wide, first + stop - start)
            rows = []
            for group in range(self.cube.groups):
                offset = (group * self.cube.tensors + tile) ^ self.me
                rows.append(ref[part, self.cube.slot(offset, self.orders[part]), :, first:last])
            pieces.append(jnp.concatenate(rows, 0))
            start += last - first
        return pieces[0] if len(pieces) == 1 else jnp.concatenate(pieces, 1)


class Scattered:
    def __init__(self, cube, me, keep_ref, send_ref, orders):
        self.cube = cube
        self.me = me
        self.refs = (keep_ref, send_ref)
        self.orders = orders

    def store(self, tile, turn, start, value):
        rows, wide = self.refs[0].shape[2:]
        ref = self.refs[turn & 1]
        width = value.shape[1]
        for group in range(self.cube.groups):
            offset = (group * self.cube.tensors + tile) ^ self.me
            done = 0
            while done < width:
                part, place = divmod(start + done, wide)
                count = min(width - done, wide - place)
                slot = self.cube.slot(offset, self.orders[part][::-1])
                ref[part, slot, :, place : place + count] = value[
                    group * rows : (group + 1) * rows, done : done + count
                ]
                done += count


class Layer:
    def __init__(self, weights, base, hidden):
        self.weights = weights
        self.base = base
        self.hidden = hidden

    def out(self, place):
        return self.weights.block(place, self.base, self.base + LANES)

    def up(self, place):
        start = self.base + LANES
        return self.weights.block(place, start, start + self.hidden)

    def down(self, place):
        start = self.base + LANES + self.hidden
        return self.weights.block(place, start, start + self.hidden)


def tile_lanes(tile):
    if isinstance(tile, int):
        return pl.ds(tile * LANES, LANES)
    return pl.ds(pl.multiple_of(tile * LANES, LANES), LANES)


def add_up(parts):
    total = None
    for part in parts:
        total = part if total is None else total + part
    return total


def whole_spec(shape):
    return pl.BlockSpec(shape, lambda at: (0,) * len(shape))


def columns_spec(weights, columns, at_block):
    groups, tiles, rows, _ = weights.shape
    return pl.BlockSpec((groups, tiles, rows, columns), lambda at: (0, 0, 0, at_block))


def scalar_spec():
    return pl.BlockSpec(memory_space=pltpu.SMEM)


def follow(kernel, first, after):
    count = len(after)
    if not count:
        return kernel

    def late(*refs):
        return kernel(*refs[:first], *refs[first + count :])

    return late


def after_specs(after):
    return [pl.BlockSpec(memory_space=pl.ANY)] * len(after)


def place_of(at):
    return (at, at)


def call(kernel, name, ins, in_specs, outs, scratch=(), after=()):
    kernel = follow(kernel, len(ins), after)
    ins = (*ins, *after)
    in_specs = [*in_specs, *after_specs(after)]
    return pl.pallas_call(
        kernel,
        grid=(1,),
        in_specs=in_specs,
        out_specs=[whole_spec(out.shape) for out in outs],
        out_shape=outs,
        scratch_shapes=list(scratch),
        compiler_params=params(),
        name=name,
    )(*ins)


def embed_kernel(
    table_ref, ids_ref, vocab_ref, cos_ref, sin_ref, q_ref, own_ref, other_ref, resid_ref
):
    own = q_ref.shape[0]
    length = ids_ref.shape[1]
    tiles = table_ref.shape[0]
    hot = lax.broadcasted_iota(jnp.int32, (64, length), 0) == ids_ref[...]
    hot = hot.astype(single).T.astype(brain)
    resid_ref[...] = dot(hot[:own], vocab_ref[...])
    hot = hot[:, :TABLE_ROWS]
    cosine = cos_ref[...]
    sine = sin_ref[...]
    for at in range(tiles):
        lanes = slice(at * LANES, (at + 1) * LANES)
        rows = dot_exact(hot, table_ref[at])
        q_ref[:, lanes] = rotate(rows[:own, :LANES], cosine[:own], sine[:own]).astype(brain)
        keys = rotate(rows[:, LANES : 2 * LANES], cosine, sine).astype(brain)
        values = rows[:, 2 * LANES :].astype(brain)
        own_ref[0, :, lanes] = keys[:own]
        own_ref[1, :, lanes] = values[:own]
        other_ref[0, :, lanes] = keys[own:]
        other_ref[1, :, lanes] = values[own:]


def embed(table, ids, vocab, cosine, sine, after):
    tiles = table.shape[0]
    own = ids.shape[1] // 2
    wide = tiles * LANES
    ins = (table, ids, vocab, cosine, sine)
    outs = [
        jax.ShapeDtypeStruct((own, wide), brain),
        jax.ShapeDtypeStruct((2, own, wide), brain),
        jax.ShapeDtypeStruct((2, own, wide), brain),
        jax.ShapeDtypeStruct((own, vocab.shape[1]), single),
    ]
    specs = [whole_spec(x.shape) for x in ins]
    return call(embed_kernel, "embed", ins, specs, outs, (), after)


def attend_kernel(heads, q_ref, own_ref, other_ref, out_ref, logsum_ref):
    own = q_ref.shape[0]
    q_turned = q_ref[...].T
    keys = jnp.concatenate([own_ref[0], other_ref[0]], 0)
    v_turned = jnp.concatenate([own_ref[1], other_ref[1]], 0).T
    rows = lax.broadcasted_iota(jnp.int32, (LANES, own), 0)

    def scores_of(head):
        mine = (rows >= head * HEAD) & (rows < (head + 1) * HEAD)
        return mine, dot(keys, jnp.where(mine, q_turned, jnp.zeros_like(q_turned)))

    mixed = jnp.zeros((LANES, own), single)
    ahead = scores_of(0)
    for head in range(heads):
        mine, scores = ahead
        if head + 1 < heads:
            ahead = scores_of(head + 1)
        peak = column_max(scores) * scale_two
        weights = jnp.exp2(scores * scale_two - peak)
        total = column_sum(weights)
        probs = (weights * (1.0 / total)).astype(brain)
        mixed = jnp.where(mine, dot(v_turned, probs), mixed)
        logsum_ref[0, head : head + 1, :] = peak + jnp.log2(total)
    out_ref[...] = mixed.T.astype(brain)


def attend(q, kv_own, kv_other, heads, after=()):
    own, wide = q.shape
    tiles = wide // LANES
    own_spec = pl.BlockSpec((own, LANES), lambda at: (0, at))
    pair_spec = pl.BlockSpec((2, own, LANES), lambda at: (0, 0, at))
    return pl.pallas_call(
        follow(functools.partial(attend_kernel, heads), 3, after),
        grid=(tiles,),
        in_specs=[own_spec, pair_spec, pair_spec, *after_specs(after)],
        out_specs=[own_spec, pl.BlockSpec((1, 8, own), lambda at: (at, 0, 0))],
        out_shape=[
            jax.ShapeDtypeStruct((own, wide), brain),
            jax.ShapeDtypeStruct((tiles, 8, own), single),
        ],
        compiler_params=params(),
        name="attend",
    )(q, kv_own, kv_other, *after)


def attend_back_kernel(
    heads, chunk, count, me_ref, q_ref, kv_own_ref, kv_other_ref, g_ref, logsum_ref, *refs
):
    dq_ref, own_ref, other_ref = refs[count:]
    own = q_ref.shape[0]
    q = q_ref[...]
    grad = g_ref[...]
    q_turned = q.T
    g_turned = grad.T
    keys = jnp.concatenate([kv_own_ref[0], kv_other_ref[0]], 0)
    values = jnp.concatenate([kv_own_ref[1], kv_other_ref[1]], 0)
    k_turned = keys.T
    rows = lax.broadcasted_iota(jnp.int32, (LANES, chunk), 0)
    lanes = lax.broadcasted_iota(jnp.int32, (chunk, LANES), 1)
    none = jnp.zeros((LANES, chunk), brain)
    none_low = jnp.zeros((chunk, LANES), brain)
    for start in range(0, own, chunk):
        part = slice(start, start + chunk)
        dq = jnp.zeros((LANES, chunk), single)
        for head in range(heads):
            mine = (rows >= head * HEAD) & (rows < (head + 1) * HEAD)
            mine_low = (lanes >= head * HEAD) & (lanes < (head + 1) * HEAD)
            scores = dot(keys, jnp.where(mine, q_turned[:, part], none))
            probs = jnp.exp2(scores * scale_two - logsum_ref[0, head : head + 1, part])
            g_probs = dot(values, jnp.where(mine, g_turned[:, part], none))
            inner = column_sum(probs * g_probs)
            g_scores = (probs * (g_probs - inner)).astype(brain)
            dv = dot(probs.astype(brain), jnp.where(mine_low, grad[part, :], none_low))
            dk = dot(g_scores, jnp.where(mine_low, q[part, :], none_low)) * scale
            if start == 0 and head == 0:
                own_ref[0] = dk[:own]
                own_ref[1] = dv[:own]
                other_ref[0] = dk[own:]
                other_ref[1] = dv[own:]
            else:
                own_ref[0] += dk[:own]
                own_ref[1] += dv[:own]
                other_ref[0] += dk[own:]
                other_ref[1] += dv[own:]
            dq = jnp.where(mine, dot(k_turned, g_scores), dq)
        dq_ref[part, :] = (dq * scale).T


def attend_back(q, kv_own, kv_other, grad, logsum, heads, me, turns, tensors, after=()):
    own, wide = q.shape
    first = turns[0]
    count = len(turns)

    def tile(at, me):
        return (at + first) ^ (me[0] & (tensors - 1))

    own_spec = pl.BlockSpec((own, LANES), lambda at, me: (0, tile(at, me)))
    pair_spec = pl.BlockSpec((2, own, LANES), lambda at, me: (0, 0, tile(at, me)))
    one_shape = jax.ShapeDtypeStruct((own, count * LANES), single)
    one_out = pl.BlockSpec((own, LANES), lambda at, me: (0, at))
    pair_shape = jax.ShapeDtypeStruct((2, own, count * LANES), single)
    pair_out = pl.BlockSpec((2, own, LANES), lambda at, me: (0, 0, at))
    return pl.pallas_call(
        functools.partial(attend_back_kernel, heads, own, len(after)),
        grid_spec=pltpu.PrefetchScalarGridSpec(
            num_scalar_prefetch=1,
            grid=(count,),
            in_specs=[
                own_spec,
                pair_spec,
                pair_spec,
                own_spec,
                pl.BlockSpec((1, 8, own), lambda at, me: (tile(at, me), 0, 0)),
                *after_specs(after),
            ],
            out_specs=[one_out, pair_out, pair_out],
        ),
        out_shape=[one_shape, pair_shape, pair_shape],
        compiler_params=params(),
        name="attend_back",
    )(me, q, kv_own, kv_other, grad, logsum, *after)


def attention_out(mixed, resid, layer, places):
    parts = [
        dot(mixed[:, tile_lanes(place[1])], layer.out(place), 1, 1) for place in places
    ]
    return resid + add_up(parts)


def middle_kernel(
    feats, mixed_ref, resid_ref, w_ref, w_next_ref, norms_ref, cos_ref, sin_ref,
    mid_ref, next_ref, q_ref, kv_ref,
):
    tiles = w_ref.shape[1]
    layer = Layer(Gathered(w_ref), 0, (w_ref.shape[3] - LANES) // 2)
    mid = attention_out(mixed_ref, resid_ref[...], layer, [place_of(at) for at in range(tiles)])
    mid_ref[...] = mid
    normed = feats.norm(mid, norms_ref[2:3], norms_ref[3:4])
    parts = []
    for at in range(tiles):
        act = gelu(dot(normed, layer.up(place_of(at)))).astype(brain)
        parts.append(dot(act, layer.down(place_of(at)), 1, 1))
    total = mid + add_up(parts)
    next_ref[...] = total
    normed = feats.norm(total, norms_ref[4:5], norms_ref[5:6])
    weights = Gathered(w_next_ref)
    cosine = cos_ref[...]
    sine = sin_ref[...]
    for at in range(tiles):
        lanes = slice(at * LANES, (at + 1) * LANES)
        rows = dot(normed, weights.block(place_of(at), 0, 3 * LANES))
        q_ref[:, lanes] = rotate(rows[:, :LANES], cosine, sine).astype(brain)
        kv_ref[0, :, lanes] = rotate(rows[:, LANES : 2 * LANES], cosine, sine).astype(brain)
        kv_ref[1, :, lanes] = rows[:, 2 * LANES :].astype(brain)


def middle(feats, mixed, resid, weights, columns, at_heads, norms, cosine, sine, after):
    own, wide = mixed.shape
    plain = jax.ShapeDtypeStruct(resid.shape, single)
    in_specs = [
        whole_spec(mixed.shape),
        whole_spec(resid.shape),
        columns_spec(weights, columns, 0),
        columns_spec(weights, 3 * LANES, at_heads),
        whole_spec(norms.shape),
        whole_spec(cosine.shape),
        whole_spec(sine.shape),
    ]
    outs = [
        plain,
        plain,
        jax.ShapeDtypeStruct((own, wide), brain),
        jax.ShapeDtypeStruct((2, own, wide), brain),
    ]
    ins = (mixed, resid, weights, weights, norms, cosine, sine)
    kernel = functools.partial(middle_kernel, feats)
    return call(kernel, "middle", ins, in_specs, outs, (), after)


def feed_back(
    feats, turns, g_resid, mid, normed, mixed_ref, layer, gain, act_ref, slope_ref,
    grads, base, g_mid_ref, g_mixed_ref,
):
    hidden = layer.hidden
    g_low = g_resid.astype(brain)
    g_turned = g_low.T
    normed_turned = normed.T
    parts = []
    for turn, tile in turns:
        g_hidden = (dot(g_low, layer.down((turn, tile))) * slope_ref[turn]).astype(brain)
        grads.store(tile, turn, base + LANES + hidden, dot(g_turned, act_ref[turn]))
        grads.store(tile, turn, base + LANES, dot(normed_turned, g_hidden))
        parts.append(dot(g_hidden, layer.up((turn, tile)), 1, 1))
    g_normed = add_up(parts)
    unit, inverse = feats.centred(mid)
    g_gain = jnp.sum(g_normed * unit, 0, keepdims=True)
    g_shift = jnp.sum(g_normed, 0, keepdims=True)
    g_mid = g_resid + feats.norm_back(unit, inverse, gain, g_normed)
    g_mid_ref[...] = g_mid
    g_low = g_mid.astype(brain)
    g_turned = g_low.T
    for turn, tile in turns:
        lanes = tile_lanes(tile)
        g_mixed_ref[:, lanes] = dot(g_low, layer.out((turn, tile))).astype(brain)
        grads.store(tile, turn, base, dot(g_turned, mixed_ref[:, lanes]))
    return g_gain, g_shift


def top_kernel(
    feats, cube, vocab_count, orders, grad_orders, me_ref, mixed_ref, resid_ref, w_own_ref,
    w_other_ref, norms_ref, vocab_ref, marks_ref, table_ref, keep_ref, send_ref, g_mid_ref, g_mixed_ref,
    g_norms_ref, g_vocab_ref, act_ref, slope_ref,
):
    me = me_ref[0]
    tiles = cube.tensors
    turns = [(turn, turn ^ (me & (tiles - 1))) for turn in range(tiles)]
    grads = Scattered(cube, me, keep_ref, send_ref, grad_orders)
    layer = Layer(Relative(cube, me, (w_own_ref, w_other_ref), orders), 0, act_ref.shape[2])
    mid = attention_out(mixed_ref, resid_ref[...], layer, turns)
    normed = feats.norm(mid, norms_ref[6:7], norms_ref[7:8])
    parts = []
    for turn, tile in turns:
        hidden = dot(normed, layer.up((turn, tile)))
        share = normal_share(hidden)
        act = (hidden * share).astype(brain)
        act_ref[turn] = act
        slope_ref[turn] = gelu_slope(hidden, share)
        parts.append(dot(act, layer.down((turn, tile)), 1, 1))
    total = mid + add_up(parts)
    unit, inverse = feats.centred(total)
    gain = norms_ref[8:9]
    final = (unit * gain + norms_ref[9:10]).astype(brain)
    own = total.shape[0]
    marks = marks_ref[...].T.astype(jnp.int32)
    slots = marks.shape[0]
    slot = marks[:, 0:1]
    target = marks[:, 1:2]
    vocab = vocab_ref[...]
    where_hot = (lax.broadcasted_iota(jnp.int32, (slots, own), 1) == slot).astype(single)
    where_hot = where_hot.astype(brain)
    present = (slot >= 0).astype(single)
    picked = dot(where_hot, final).astype(brain)
    logits = dot(picked, vocab, 1, 1)
    lane = lax.broadcasted_iota(jnp.int32, logits.shape, 1)
    logits = jnp.where(lane < vocab_count, logits, -1e30)
    peak = jnp.max(logits, 1, keepdims=True)
    logsum = peak + jnp.log(jnp.sum(jnp.exp(logits - peak), 1, keepdims=True))
    target_hot = (lane == target).astype(single)
    target_logit = jnp.sum(
        jnp.where(lane < vocab_count, logits * target_hot, 0.0), 1, keepdims=True
    )
    loss = jnp.sum((logsum - target_logit) * present, 0, keepdims=True)
    share = present / table_ref[0, vocab_count : vocab_count + 1, 0:1]
    g_logits = ((jnp.exp(logits - logsum) - target_hot) * share).astype(brain)
    g_vocab_ref[...] = dot(g_logits, picked, 0, 0)[:TABLE_ROWS]
    g_picked = dot(g_logits, vocab)
    g_final = dot_exact(where_hot, g_picked, 0, 0)
    g_norms_ref[...] = jnp.zeros_like(g_norms_ref)
    g_norms_ref[8:9] = jnp.sum(g_final * unit, 0, keepdims=True)
    g_norms_ref[9:10] = jnp.sum(g_final, 0, keepdims=True)
    g_norms_ref[LOSS_ROW : LOSS_ROW + 1] = jnp.broadcast_to(loss, (1, g_norms_ref.shape[1]))
    g_resid = feats.norm_back(unit, inverse, gain, g_final)
    g_gain, g_shift = feed_back(
        feats, turns, g_resid, mid, normed, mixed_ref, layer, norms_ref[6:7], act_ref, slope_ref,
        grads, 0, g_mid_ref, g_mixed_ref,
    )
    g_norms_ref[6:7] = g_gain
    g_norms_ref[7:8] = g_shift


def top(
    feats, cube, orders, grad_orders, me, mixed, resid, w_own, w_other, norms, vocab,
    vocab_count, marks, table,
):
    own, wide = mixed.shape
    tiles = cube.tensors
    rows = w_own.shape[2]
    columns = w_own.shape[0] * w_own.shape[3] - 3 * LANES
    hidden = (columns - LANES) // 2
    pieces = len(grad_orders)
    grads = (pieces, cube.devices // 2, rows, columns // pieces)
    outs = [
        jax.ShapeDtypeStruct(grads, single),
        jax.ShapeDtypeStruct(grads, single),
        jax.ShapeDtypeStruct(resid.shape, single),
        jax.ShapeDtypeStruct(mixed.shape, brain),
        jax.ShapeDtypeStruct(norms.shape, single),
        jax.ShapeDtypeStruct((TABLE_ROWS, resid.shape[1]), single),
    ]
    in_specs = [
        scalar_spec(),
        whole_spec(mixed.shape),
        whole_spec(resid.shape),
        whole_spec(w_own.shape),
        whole_spec(w_other.shape),
        whole_spec(norms.shape),
        whole_spec(vocab.shape),
        whole_spec(marks.shape),
        whole_spec(table.shape),
    ]
    scratch = [
        pltpu.VMEM((tiles, own, hidden), brain),
        pltpu.VMEM((tiles, own, hidden), single),
    ]
    ins = (me, mixed, resid, w_own, w_other, norms, vocab, marks, table)
    kernel = functools.partial(top_kernel, feats, cube, vocab_count, orders, grad_orders)
    return call(kernel, "top", ins, in_specs, outs, scratch)


def head_grads(turn, heads_refs, cosine, sine):
    dq_ref, own_ref, other_ref = heads_refs[3 * (turn // 2) : 3 * (turn // 2) + 3]
    lanes = tile_lanes(turn % 2)
    other = tile_lanes(1 - turn % 2)
    g_q = unrotate(dq_ref[:, lanes], cosine, sine)
    g_k = unrotate(own_ref[0, :, lanes] + other_ref[0, :, other], cosine, sine)
    g_v = own_ref[1, :, lanes] + other_ref[1, :, other]
    return jnp.concatenate([g_q, g_k, g_v], 1).astype(brain)


def lower_kernel(feats, cube, grad_orders, me_ref, *refs):
    heads_refs = refs[:6]
    (
        g_mid_in_ref, resid_ref, mid_ref, mixed_ref, w_in_ref, w_ref, norms_ref, cos_ref, sin_ref,
        g_norms_in_ref, keep_ref, send_ref, g_mid_ref, g_mixed_ref, g_norms_ref,
        act_ref, slope_ref,
    ) = refs[6:]
    me = me_ref[0]
    tiles = cube.tensors
    turns = [(turn, turn ^ (me & (tiles - 1))) for turn in range(tiles)]
    layer = Layer(Gathered(w_ref), 0, act_ref.shape[2])
    weights = Gathered(w_in_ref)
    grads = Scattered(cube, me, keep_ref, send_ref, grad_orders)
    unit, inverse = feats.centred(resid_ref[...])
    gain = norms_ref[4:5]
    normed_turned = (unit * gain + norms_ref[5:6]).astype(brain).T
    cosine = cos_ref[...]
    sine = sin_ref[...]
    parts = []
    for turn, tile in turns:
        g_heads = head_grads(turn, heads_refs, cosine, sine)
        grads.store(tile, turn, 0, dot(normed_turned, g_heads))
        parts.append(dot(g_heads, weights.block((turn, tile), 0, 3 * LANES), 1, 1))
    g_normed = add_up(parts)
    g_norms_ref[...] = g_norms_in_ref[...]
    g_norms_ref[4:5] = jnp.sum(g_normed * unit, 0, keepdims=True)
    g_norms_ref[5:6] = jnp.sum(g_normed, 0, keepdims=True)
    g_resid = g_mid_in_ref[...] + feats.norm_back(unit, inverse, gain, g_normed)
    mid = mid_ref[...]
    normed = feats.norm(mid, norms_ref[2:3], norms_ref[3:4])
    for turn, tile in turns:
        hidden = dot(normed, layer.up((turn, tile)))
        share = normal_share(hidden)
        act_ref[turn] = (hidden * share).astype(brain)
        slope_ref[turn] = gelu_slope(hidden, share)
    g_gain, g_shift = feed_back(
        feats, turns, g_resid, mid, normed, mixed_ref, layer, norms_ref[2:3], act_ref, slope_ref,
        grads, 3 * LANES, g_mid_ref, g_mixed_ref,
    )
    g_norms_ref[2:3] = g_gain
    g_norms_ref[3:4] = g_shift


def lower(
    feats, cube, grad_orders, me, head_parts, g_mid, resid, mid, mixed, weights, at_heads,
    feed_columns, norms, cosine, sine, g_norms, after,
):
    own, wide = mixed.shape
    tiles = cube.tensors
    rows = weights.shape[2]
    hidden = (feed_columns - LANES) // 2
    columns = feed_columns + 3 * LANES
    count = len(grad_orders)
    grads = (count, cube.devices // 2, rows, columns // count)
    outs = [
        jax.ShapeDtypeStruct(grads, single),
        jax.ShapeDtypeStruct(grads, single),
        jax.ShapeDtypeStruct(resid.shape, single),
        jax.ShapeDtypeStruct(mixed.shape, brain),
        jax.ShapeDtypeStruct(norms.shape, single),
    ]
    before = (*head_parts, g_mid, resid, mid, mixed)
    rest = (norms, cosine, sine, g_norms)
    in_specs = [
        scalar_spec(),
        *[whole_spec(x.shape) for x in before],
        columns_spec(weights, 3 * LANES, at_heads),
        columns_spec(weights, feed_columns, 0),
        *[whole_spec(x.shape) for x in rest],
    ]
    scratch = [
        pltpu.VMEM((tiles, own, hidden), brain),
        pltpu.VMEM((tiles, own, hidden), single),
    ]
    ins = (me, *before, weights, weights, *rest)
    kernel = functools.partial(lower_kernel, feats, cube, grad_orders)
    return call(kernel, "lower", ins, in_specs, outs, scratch, after)


def stacked_lanes(ref, row, value):
    rows = value.shape[0]
    for at in range(value.shape[1] // LANES):
        ref[row : row + rows, :] = value[:, at * LANES : (at + 1) * LANES]
        row += rows
    return row


def side_by_side(x, rows):
    return jnp.concatenate([x[at : at + rows] for at in range(0, x.shape[0], rows)], 1)


def bottom_kernel(
    feats, cube, orders, me_ref, *refs
):
    heads_refs = refs[:6]
    (
        g_mid_ref, ids_ref, w_own_ref, w_other_ref, norms_ref, vocab_ref, g_vocab_in_ref, g_norms_in_ref, cos_ref,
        sin_ref, keep_ref, send_ref, norms_out_ref,
    ) = refs[6:]
    tiles = cube.tensors
    own = g_mid_ref.shape[0]
    mine = me_ref[0] & (tiles - 1)
    hot = lax.broadcasted_iota(jnp.int32, (TABLE_ROWS, own), 0) == ids_ref[...]
    hot = hot.astype(single).astype(brain)
    cosine = cos_ref[...]
    sine = sin_ref[...]
    weights = Relative(cube, me_ref[0], (w_own_ref, w_other_ref), orders)
    first = w_own_ref.shape[-1] - 3 * LANES
    refs = (keep_ref, send_ref)
    rows = [0, 0]
    parts = []
    for turn in range(tiles):
        tile = turn ^ mine
        g_table = dot(hot, head_grads(turn, heads_refs, cosine, sine))
        rows[turn & 1] = stacked_lanes(refs[turn & 1], rows[turn & 1], g_table)
        weight = weights.block((turn, tile), first, first + 3 * LANES)
        high, middle_part, low = split_three(g_table)
        parts.append(dot(high, weight, 1, 1))
        parts.append(dot(middle_part, weight, 1, 1))
        parts.append(dot(low, weight, 1, 1))
    g_normed = add_up(parts)
    unit, inverse = feats.centred(vocab_ref[...].astype(single)[:TABLE_ROWS])
    norms_out_ref[...] = g_norms_in_ref[...]
    norms_out_ref[0:1] = jnp.sum(g_normed * unit, 0, keepdims=True)
    norms_out_ref[1:2] = jnp.sum(g_normed, 0, keepdims=True)
    g_norms = norms_out_ref[...]
    g_rows = feats.norm_back(unit, inverse, norms_ref[0:1], g_normed)
    g_vocab = g_vocab_in_ref[...] + (dot_exact(hot, g_mid_ref[...]) + g_rows)
    for ref, row in zip(refs, rows):
        row = stacked_lanes(ref, row, g_vocab)
        stacked_lanes(ref, row, g_norms)


def last_part(weights):
    parts = weights.shape[0]
    return pl.BlockSpec((1,) + weights.shape[1:], lambda at: (parts - 1, 0, 0, 0))


def bottom(
    feats, cube, orders, me, head_parts, g_mid, ids, w_own, w_other, norms, vocab, g_vocab,
    g_norms, cosine, sine, after,
):
    tiles = cube.tensors
    table_rows = 3 * TABLE_ROWS * tiles // 2
    vector_rows = (g_vocab.shape[0] + g_norms.shape[0]) * g_vocab.shape[1] // LANES
    out = jax.ShapeDtypeStruct((table_rows + vector_rows, LANES), single)
    before = (*head_parts, g_mid, ids)
    rest = (norms, vocab, g_vocab, g_norms, cosine, sine)
    in_specs = [
        scalar_spec(),
        *[whole_spec(x.shape) for x in before],
        last_part(w_own),
        last_part(w_other),
        *[whole_spec(x.shape) for x in rest],
    ]
    outs = [out, out, jax.ShapeDtypeStruct(norms.shape, single)]
    ins = (me, *before, w_own, w_other, *rest)
    kernel = functools.partial(bottom_kernel, feats, cube, orders[-1:])
    return call(kernel, "bottom", ins, in_specs, outs, (), after)[:2]


def halve_kernel(count, together, stacked, skip, keep_ref, *refs):
    got_count = 1 if together else count
    got = refs[:got_count]
    outs = refs[got_count + skip :]
    size = keep_ref.shape[1]
    half = size // 2
    for part in range(count):
        arrived = got[0].at[part] if together else got[part]
        if size == 1:
            outs[0][part] = keep_ref[part] + arrived[...]
        else:
            outs[0][part] = keep_ref[part, :half] + arrived[:half]
            send = outs[1].at[part] if stacked else outs[1 + part]
            send[...] = keep_ref[part, half:] + arrived[half:]


def halve(keep, got, through=(), after=(), stacked=False):
    count, size, rows, wide = keep.shape
    together = not isinstance(got, list)
    got = [got] if together else got
    step = rows // 2 if size >= 8 else rows
    half = max(size // 2, 1)

    def spec(*lead):
        return pl.BlockSpec((*lead, step, wide), lambda at: (*([0] * len(lead)), at, 0))

    outs = [jax.ShapeDtypeStruct((count, half, rows, wide), single)]
    out_specs = [spec(count, half)]
    if size > 1 and stacked:
        outs += outs
        out_specs += out_specs
    elif size > 1:
        outs += [jax.ShapeDtypeStruct((half, rows, wide), single)] * count
        out_specs += [spec(half)] * count
    sends = len(outs) - 1
    got_specs = [spec(count, size)] if together else [spec(size)] * count
    ins = (keep, *got)
    aliases = {len(ins) + at: len(outs) + at for at in range(len(through))}
    outs += [jax.ShapeDtypeStruct(x.shape, x.dtype) for x in through]
    results = pl.pallas_call(
        functools.partial(halve_kernel, count, together, stacked, len(through) + len(after)),
        grid=(rows // step,),
        in_specs=[spec(count, size), *got_specs, *after_specs(through), *after_specs(after)],
        out_specs=[*out_specs, *after_specs(through)],
        out_shape=outs,
        input_output_aliases=aliases,
        compiler_params=params(),
        name="halve",
    )(*ins, *through, *after)
    going = results[1] if stacked and sends else results[1 : 1 + sends]
    return results[0], going, results[1 + sends :]


def join_kernel(count, together, stacked, skip, *refs):
    ins = 1 if together else count
    helds, gots = refs[:ins], refs[ins : 2 * ins]
    outs = refs[2 * ins + skip :]
    for part in range(count):
        held = helds[0].at[part] if together else helds[part]
        got = gots[0].at[part] if together else gots[part]
        out = outs[0].at[part] if stacked else outs[part]
        size = held.shape[0]
        out[:size] = held[...]
        out[size:] = got[...]


def join(held, got, count, stacked, through=(), after=()):
    together = not isinstance(held, list)
    ins = (held, got) if together else (*held, *got)
    size, rows, wide = ins[0].shape[-3:]
    shape = (2 * size, rows, wide)
    if stacked:
        outs = [jax.ShapeDtypeStruct((count,) + shape, ins[0].dtype)]
    else:
        outs = [jax.ShapeDtypeStruct(shape, ins[0].dtype)] * count
    aliases = {len(ins) + at: len(outs) + at for at in range(len(through))}
    skip = len(through) + len(after)
    results = pl.pallas_call(
        functools.partial(join_kernel, count, together, stacked, skip),
        grid=(1,),
        in_specs=[
            *[whole_spec(x.shape) for x in ins], *after_specs(through), *after_specs(after)
        ],
        out_specs=[*[whole_spec(out.shape) for out in outs], *after_specs(through)],
        out_shape=[*outs, *[jax.ShapeDtypeStruct(x.shape, x.dtype) for x in through]],
        input_output_aliases=aliases,
        compiler_params=params(),
        name="join",
    )(*ins, *through, *after)
    joined = results[0] if stacked else list(results[:count])
    return joined, results[len(outs) :]


class Gather:
    def __init__(self, cube, parts):
        count = len(parts)
        self.cube = cube
        self.count = count
        turning = [cube.outer(turn)[:-1] for turn in range(count)]
        self.orders = [[cube.size - 1] + turns for turns in turning]
        self.held = jnp.stack(parts)[:, None]
        self.got = cube.swap(self.held, cube.size - 1)
        self.at = 1

    def step(self, through=(), after=()):
        last = self.at == len(self.orders[0])
        self.held, through = join(self.held, self.got, self.count, last, through, after)
        if last:
            self.got = self.cube.swap(self.held, 0)
        else:
            self.got = [
                self.cube.swap(x, order[self.at]) for x, order in zip(self.held, self.orders)
            ]
        self.at += 1
        return through


def normalize_features(resid, gain, shift):
    centre = resid - jnp.mean(resid, -1, keepdims=True)
    spread = jnp.mean(centre * centre, -1, keepdims=True)
    return centre * lax.rsqrt(spread + norm_eps) * gain + shift


def adamw(master, first, second, grad, step_rate):
    mean = beta_first * first + (1.0 - beta_first) * grad
    square = beta_second * second + (1.0 - beta_second) * grad * grad
    corrected = mean / (1.0 - beta_first**STEP)
    rescaled_values = square / (1.0 - beta_second**STEP)
    fresh = master - step_rate * (
        corrected / (jnp.sqrt(rescaled_values) + adam_eps) + weight_decay * master
    )
    return (fresh, mean, square)


def pad_lanes(x, lanes):
    return jnp.pad(x, [(0, 0)] * (x.ndim - 1) + [(0, lanes - x.shape[-1])])


def make_shards(groups, tensors):
    axes = ("dp", "tensor")
    cube = Cube(groups, tensors)

    def shards(
        token_ids,
        mask_pos,
        mask_target,
        mask_count,
        weight_in,
        weight_out,
        weight_up,
        weight_down,
        norm_params,
        vocab_table,
        first_in,
        first_out,
        first_up,
        first_down,
        first_norm,
        first_vocab,
        second_in,
        second_out,
        second_up,
        second_down,
        second_norm,
        second_vocab,
    ):
        layers, block, in_wide = weight_in.shape
        heads = in_wide // (3 * HEAD)
        per_heads = heads * HEAD
        hidden = weight_up.shape[2]
        hidden_padded = -(-hidden // LANES) * LANES
        vocab_count, width = vocab_table.shape
        feats = Features(width, groups)
        local_len = token_ids.shape[1]
        length = local_len * tensors
        own = length // 2
        here = lax.axis_index("tensor")
        group_at = lax.axis_index("dp")
        me = (group_at * tensors + here).astype(jnp.int32).reshape(1)
        sequence = here // 2
        quarters = jnp.stack([here, here ^ 2, here ^ 1, here ^ 3])

        heads_in = weight_in.astype(brain).transpose(1, 0, 2)
        heads_in = heads_in.reshape(block, layers, heads, 3, HEAD).transpose(0, 1, 3, 2, 4)
        heads_in = pad_lanes(heads_in.reshape(block, layers, 3, per_heads), LANES)
        heads_in = heads_in.reshape(block, layers, 3 * LANES)
        feed = jnp.concatenate(
            [
                pad_lanes(weight_out.astype(brain).transpose(2, 0, 1), LANES),
                pad_lanes(weight_up.astype(brain).transpose(1, 0, 2), hidden_padded),
                pad_lanes(weight_down.astype(brain).transpose(2, 0, 1), hidden_padded),
            ],
            2,
        )
        feed_columns = feed.shape[2]

        def pad_rows(x):
            return jnp.pad(x, ((0, feats.padded - block), (0, 0)))

        vocab_low = vocab_table.astype(brain)
        vocab_padded = jnp.pad(feats.pad(vocab_low), ((0, 64 - vocab_count), (0, 0)))
        norms = jnp.pad(feats.pad(norm_params), ((0, 16 - norm_params.shape[0]), (0, 0)))

        def gather_all(x):
            x = lax.all_gather(x, axes, axis=0, tiled=False)
            return x.reshape((groups, tensors) + x.shape[1:])

        weights = gather_all(pad_rows(jnp.concatenate([feed[:, 0], heads_in[:, 1]], 1)))
        at_heads = feed_columns // (3 * LANES)
        later = pad_rows(jnp.concatenate([feed[:, 1], heads_in[:, 0]], 1))
        third = later.shape[1] // 3
        gather = Gather(cube, [later[:, at : at + third] for at in range(0, 3 * third, third)])

        table_low = normalize_features(
            lax.reduce_precision(vocab_table, 8, 7), norm_params[0], norm_params[1]
        ).astype(brain)
        table_own = lax.dynamic_slice_in_dim(
            table_low.reshape(vocab_count, groups, block), group_at, 1, 1
        )[:, 0]
        table = dot(table_own, heads_in[:, 0])
        extra = jnp.zeros((TABLE_ROWS - vocab_count, 3 * LANES), single)
        extra = extra.at[0, 0].set(jnp.sum(mask_count).astype(single))
        table = jnp.concatenate([table, extra], 0)
        for at in range(2, cube.size):
            table = table + cube.swap(table, at)
        count_total = table[vocab_count, 0]
        ids_row = vocab_count + 1
        table = lax.dynamic_update_slice(
            table, pad_lanes(token_ids.astype(single), 3 * LANES), (ids_row, 0)
        )
        got = cube.swap(table, 1)
        upper = (here & 2) == 2
        pair = jnp.stack([jnp.where(upper, got, table), jnp.where(upper, table, got)])
        got = cube.swap(pair, 0)
        upper = (here & 1) == 1
        table = jnp.stack([jnp.where(upper, got, pair), jnp.where(upper, pair, got)], 1)
        table = table.reshape(tensors, TABLE_ROWS, 3 * LANES)
        ids = jnp.take(table[:, ids_row : ids_row + 2, :local_len], sequence, axis=1)
        ids = jnp.take(ids, quarters, axis=0).reshape(1, length).astype(jnp.int32)

        half = HEAD // 2
        freqs = 10000.0 ** (-jnp.arange(half, dtype=single) * 2.0 / HEAD)
        positions = (quarters[:, None] * local_len + jnp.arange(local_len)[None, :]).reshape(length)
        angles = positions.astype(single)[:, None] * freqs[None, :]
        cosine, sine = (jnp.cos(angles), jnp.sin(angles))
        cosine = pad_lanes(jnp.tile(jnp.concatenate([cosine, cosine], 1), (1, heads)), LANES)
        sine = pad_lanes(jnp.tile(jnp.concatenate([-sine, sine], 1), (1, heads)), LANES)
        cos_own, sin_own = (cosine[:own], sine[:own])

        slots = mask_pos.shape[1]
        my_pos = jnp.take(mask_pos, sequence, axis=0)
        my_count = jnp.take(mask_count, sequence, axis=0)
        quarter = my_pos // local_len
        inside = my_pos % local_len
        slot = jnp.where(
            quarter == here, inside, jnp.where(quarter == (here ^ 2), inside + local_len, -1)
        )
        slot = jnp.where(jnp.arange(slots) < my_count, slot, -1)
        target = jnp.take(mask_target, sequence, axis=0)
        marks = jnp.zeros((8, slots), jnp.int32).at[0].set(slot).at[1].set(target)
        marks = marks.astype(single)

        gather.step((), (table,))
        q_low, kv_low, kv_low_other, resid_low = embed(table, ids, vocab_padded, cosine, sine, ())
        while gather.at + 2 < cube.size:
            gather.step((), (q_low,))
        mixed_low, logsum_low = attend(q_low, kv_low, kv_low_other, heads)
        gather.step((), (logsum_low,))
        mid_low, resid, q, kv = middle(
            feats, mixed_low, resid_low, weights, feed_columns, at_heads, norms, cos_own, sin_own,
            (),
        )
        (kv,) = gather.step((kv,), (resid,))
        kv_other = cube.swap(kv, 0)
        mixed, logsum = attend(q, kv, kv_other, heads)
        grad_orders = [cube.outer(turn) for turn in range(3)]

        last_step = cube.size - 2

        class Sums:
            def __init__(self, keep, send):
                self.keep = keep
                self.got = cube.swap(send, 0)
                self.at = 0

            def step(self, through=(), after=()):
                stacked = self.at == last_step
                self.keep, sends, through = halve(self.keep, self.got, through, after, stacked)
                if stacked:
                    self.got = cube.swap(sends, grad_orders[0][-1])
                else:
                    self.got = [
                        cube.swap(x, order[self.at]) for x, order in zip(sends, grad_orders)
                    ]
                self.at += 1
                return through

            def finish(self, through=(), after=()):
                keep, _, through = halve(self.keep, self.got, through, after)
                return keep[:, 0], through

        def exchange(arrays):
            return [cube.swap(x, 0) for x in arrays]

        first_turns = list(range(tensors // 2))
        last_turns = list(range(tensors // 2, tensors))
        keep, send, g_mid, g_mixed, g_norms, g_vocab = top(
            feats, cube, gather.orders, grad_orders, me, mixed, resid, gather.held, gather.got,
            norms, vocab_padded, vocab_count, marks, table,
        )
        sums_top = Sums(keep, send)
        part = (q, kv, kv_other, g_mixed, logsum, heads, me)
        first = attend_back(*part, first_turns, tensors)
        got_first = exchange(sums_top.step(first[2:], (first[0],)))
        last = attend_back(*part, last_turns, tensors, (sums_top.keep,))
        got_last = exchange(sums_top.step(last[2:], (last[0],)))
        head_parts = (*first[:2], *got_first, *last[:2], *got_last)
        keep, send, g_mid, g_mixed, g_norms = lower(
            feats, cube, grad_orders, me, head_parts, g_mid, resid, mid_low, mixed_low, weights,
            at_heads, feed_columns, norms, cos_own, sin_own, g_norms, (sums_top.keep,),
        )
        (send,) = sums_top.step((send,), (g_mid,))
        sums_low = Sums(keep, send)
        part = (q_low, kv_low, kv_low_other, g_mixed, logsum_low, heads, me)
        first = attend_back(*part, first_turns, tensors, (sums_top.keep,))
        got_first = exchange(sums_top.step(first[2:], (first[0],)))
        sums_low.step((), (sums_top.keep,))
        last = attend_back(*part, last_turns, tensors, (sums_low.keep,))
        got_last = exchange(sums_low.step(last[2:], (last[0],)))
        head_parts = (*first[:2], *got_first, *last[:2], *got_last)
        keep_table, send_table = bottom(
            feats, cube, gather.orders, me, head_parts, g_mid, ids[:, :own], gather.held,
            gather.got, norms, vocab_padded, g_vocab, g_norms, cos_own, sin_own, (sums_low.keep,),
        )
        got = cube.swap(send_table, 0)
        (keep_table,) = sums_low.step((keep_table,))
        total = keep_table + got
        tile_rows = 3 * TABLE_ROWS
        got = cube.swap(total[tile_rows:], 1)
        (total,) = sums_low.step((total,))
        total = jnp.concatenate(
            [total[:tile_rows] + got[:tile_rows], total[2 * tile_rows :] + got[tile_rows:]], 0
        )
        for at in range(2, cube.size):
            total = total + cube.swap(total, at)
        while sums_low.at <= last_step:
            sums_low.step()
        while sums_top.at <= last_step:
            sums_top.step((), (keep_table,))
        grads_low, _ = sums_low.finish()
        grads_top, _ = sums_top.finish((), (sums_low.keep,))
        grads_top = jnp.concatenate(list(grads_top), 1)
        grads_low = jnp.concatenate(list(grads_low), 1)
        g_table = side_by_side(total[:tile_rows], TABLE_ROWS)[:vocab_count]
        vocab_rows = TABLE_ROWS * feats.total // LANES
        g_vocab = side_by_side(total[tile_rows : tile_rows + vocab_rows], TABLE_ROWS)
        g_vocab = feats.unpad(g_vocab[:vocab_count])
        g_norms = side_by_side(total[tile_rows + vocab_rows :], norms.shape[0])
        loss_total = g_norms[LOSS_ROW, 0]
        g_norms = feats.unpad(g_norms[: norm_params.shape[0]])
        grads_in_low = lax.dot_general(
            table_own.astype(single),
            g_table,
            (((0,), (0,)), ((), ())),
            precision=highest,
            preferred_element_type=single,
        )

        def unpack_in(grad):
            grad = grad[:block].reshape(block, 3, LANES)[:, :, :per_heads]
            return grad.reshape(block, 3, heads, HEAD).transpose(0, 2, 1, 3).reshape(block, in_wide)

        low_start = 3 * LANES
        start = LANES + hidden_padded
        grad_in = jnp.stack([unpack_in(grads_in_low), unpack_in(grads_low[:, :low_start])], 1)
        both = jnp.stack([grads_low[:block, low_start:], grads_top[:block]], 1)
        grads = (
            grad_in,
            both[:, :, :per_heads],
            both[:, :, LANES : LANES + hidden],
            both[:, :, start : start + hidden],
            g_norms,
            g_vocab,
        )
        by_rows = Layout(major_to_minor=(0, 1, 2))
        grads = [with_layout_constraint(x, by_rows) for x in grads[:4]] + list(grads[4:])
        turned = [(1, 0, 2), (2, 0, 1), (1, 0, 2), (2, 0, 1), None, None]
        turned_back = [(1, 0, 2), (1, 2, 0), (1, 0, 2), (1, 2, 0), None, None]

        def turn_all(arrays, orders):
            return [x if order is None else x.transpose(order) for x, order in zip(arrays, orders)]

        masters = (weight_in, weight_out, weight_up, weight_down, norm_params, vocab_table)
        firsts = (first_in, first_out, first_up, first_down, first_norm, first_vocab)
        seconds = (second_in, second_out, second_up, second_down, second_norm, second_vocab)
        masters, firsts, seconds = [turn_all(x, turned) for x in (masters, firsts, seconds)]
        results = [
            adamw(masters[which], firsts[which], seconds[which], grads[which], step_rates[which])
            for which in range(6)
        ]
        news, means, squares = [
            turn_all([entry[which] for entry in results], turned_back) for which in range(3)
        ]
        copies = [news[which].astype(brain) for which in (0, 1, 2, 3, 5)]
        return (loss_total, count_total, *news, *means, *squares, *copies)

    return shards


def solution(mesh):
    rows_in = P(None, "dp", "tensor")
    rows_out = P(None, "tensor", "dp")
    six = (rows_in, rows_out, rows_in, rows_out, P(), P())
    five = (rows_in, rows_out, rows_in, rows_out, P())
    return jax.shard_map(
        make_shards(mesh.shape["dp"], mesh.shape["tensor"]),
        mesh=mesh,
        in_specs=(P("dp", "tensor"), P("dp", None), P("dp", None), P("dp"), *six, *six, *six),
        out_specs=(P(), P(), *six, *six, *six, *five),
        check_vma=False,
    )
```

```python
import functools
import math

import jax
import jax.numpy as jnp
from jax import lax
from jax.experimental import pallas as pl
from jax.experimental.layout import Layout, with_layout_constraint
from jax.experimental.pallas import tpu as pltpu
from jax.sharding import PartitionSpec as P

HEAD = 24
STEP = 5
LANES = 128
TABLE_ROWS = 40
LOSS_ROW = 10
VMEM_BYTES = 60 * 1024 * 1024

norm_eps = 1e-05
step_rates = (0.02, 0.3, 0.02, 0.02, 0.3, 0.05)
beta_first = 0.5
beta_second = 0.5
adam_eps = 1e-08
weight_decay = 0.01
highest = lax.Precision.HIGHEST
brain = jnp.bfloat16
single = jnp.float32
scale = HEAD ** (-0.5)
scale_two = scale * math.log2(math.e)

params = functools.partial(pltpu.CompilerParams, vmem_limit_bytes=VMEM_BYTES)


class Cube:
    def __init__(self, groups, tensors):
        self.groups = groups
        self.tensors = tensors
        self.devices = groups * tensors
        self.size = self.devices.bit_length() - 1
        self.masks = [1 << at for at in range(self.size)]
        self.folded = groups >= 4
        if self.folded:
            self.masks[-1] |= self.masks[-2]

    def swap(self, x, *dimensions):
        mask = 0
        for at in dimensions:
            mask ^= self.masks[at]
        pairs = [(device, device ^ mask) for device in range(self.devices)]
        return lax.ppermute(x, ("dp", "tensor"), pairs)

    def outer(self, turn):
        rest = list(range(1, self.size))
        rest = rest[1:2] + rest[:1] + rest[2:]
        turning = rest[:-1]
        turn = turn % len(turning)
        return turning[turn:] + turning[:turn] + rest[-1:]

    def steps(self, offset):
        bits = [(offset >> at) & 1 for at in range(self.size)]
        if self.folded:
            bits[-2] = bits[-2] ^ bits[-1]
        return bits

    def slot(self, offset, order):
        bits = self.steps(offset)
        place = 0
        for rank, at in enumerate(order):
            place = place + (bits[at] << rank)
        return place


def dot(left, right, left_dim=1, right_dim=0):
    return lax.dot_general(
        left, right, (((left_dim,), (right_dim,)), ((), ())), preferred_element_type=single
    )


def split_three(x):
    high = x.astype(brain)
    rest = x - high.astype(single)
    middle = rest.astype(brain)
    return high, middle, (rest - middle.astype(single)).astype(brain)


def dot_exact(hot, x, left_dim=1, right_dim=0):
    high, middle, low = split_three(x)
    tail = dot(hot, middle, left_dim, right_dim) + dot(hot, low, left_dim, right_dim)
    return dot(hot, high, left_dim, right_dim) + tail


def fold_rows(x, op, parts=8):
    size = x.shape[0] // parts
    pieces = [x[at * size : (at + 1) * size] for at in range(parts)]
    while len(pieces) > 1:
        pieces = [op(pieces[at], pieces[at + 1]) for at in range(0, len(pieces), 2)]
    return pieces[0]


def column_max(x):
    return jnp.max(fold_rows(x, jnp.maximum), 0, keepdims=True)


def column_sum(x):
    return jnp.sum(fold_rows(x, jnp.add), 0, keepdims=True)


tail_slope = 0.3275911 * math.sqrt(0.5)
tail_terms = tuple(
    0.5 * term for term in (1.061405429, -1.453152027, 1.421413741, -0.284496736, 0.254829592)
)


def normal_share(x):
    bell = jnp.exp2(x * x * (-0.5 * math.log2(math.e)))
    below = 1.0 + jnp.abs(x) * tail_slope
    t = 1.0 / below
    tail = tail_terms[0] * t + tail_terms[1]
    for term in tail_terms[2:]:
        tail = tail * t + term
    tail = tail * (t * bell)
    return jnp.where(x < 0.0, tail, 1.0 - tail), bell


def gelu(x):
    return x * normal_share(x)[0]


def gelu_slope(x, share, bell):
    return share + (x * (1.0 / math.sqrt(2.0 * math.pi))) * bell


def rotary_partner(x):
    lane = lax.broadcasted_iota(jnp.int32, x.shape, 1) % HEAD
    return jnp.where(
        lane < HEAD // 2,
        pltpu.roll(x, LANES - HEAD // 2, 1),
        pltpu.roll(x, HEAD // 2, 1),
    )


def rotate(x, cosine, sine):
    return x * cosine + rotary_partner(x) * sine


def unrotate(x, cosine, sine):
    return x * cosine - rotary_partner(x) * sine


class Features:
    def __init__(self, width, groups):
        self.width = width
        self.groups = groups
        self.block = width // groups
        self.padded = -(-self.block // 16) * 16
        self.total = self.padded * groups

    def pad(self, x):
        rows = x.shape[0]
        x = x.reshape(rows, self.groups, self.block)
        x = jnp.pad(x, ((0, 0), (0, 0), (0, self.padded - self.block)))
        return x.reshape(rows, self.total)

    def unpad(self, x):
        rows = x.shape[0]
        x = x.reshape(rows, self.groups, self.padded)[:, :, : self.block]
        return x.reshape(rows, self.width)

    def live(self, shape):
        lane = lax.broadcasted_iota(jnp.int32, shape, 1) % self.padded
        return lane < self.block

    def centred(self, x):
        mean = jnp.sum(x, 1, keepdims=True) * (1.0 / self.width)
        centre = jnp.where(self.live(x.shape), x - mean, 0.0)
        spread = jnp.sum(centre * centre, 1, keepdims=True) * (1.0 / self.width)
        inverse = lax.rsqrt(spread + norm_eps)
        return centre * inverse, inverse

    def norm(self, x, gain, shift):
        unit, _ = self.centred(x)
        return (unit * gain + shift).astype(brain)

    def norm_back(self, unit, inverse, gain, grad):
        scaled = grad * gain
        mean = jnp.sum(scaled, 1, keepdims=True) * (1.0 / self.width)
        along = jnp.sum(scaled * unit, 1, keepdims=True) * (1.0 / self.width)
        back = inverse * (scaled - mean - unit * along)
        return jnp.where(self.live(back.shape), back, 0.0)


class Gathered:
    def __init__(self, ref):
        self.ref = ref

    def block(self, place, start, stop):
        groups, _, rows, _ = self.ref.shape
        return self.ref[:, place[1], :, start:stop].reshape(groups * rows, stop - start)


class Relative:
    def __init__(self, cube, me, refs, orders):
        self.cube = cube
        self.me = me
        self.refs = refs
        self.orders = orders

    def block(self, place, start, stop):
        turn, tile = place
        ref = self.refs[turn & 1]
        wide = ref.shape[-1]
        pieces = []
        while start < stop:
            part, first = divmod(start, wide)
            last = min(wide, first + stop - start)
            rows = []
            for group in range(self.cube.groups):
                offset = (group * self.cube.tensors + tile) ^ self.me
                rows.append(ref[part, self.cube.slot(offset, self.orders[part]), :, first:last])
            pieces.append(jnp.concatenate(rows, 0))
            start += last - first
        return pieces[0] if len(pieces) == 1 else jnp.concatenate(pieces, 1)


class Scattered:
    def __init__(self, cube, me, refs, outs, semaphores, orders):
        self.cube = cube
        self.me = me
        self.refs = refs
        self.outs = outs
        self.semaphores = semaphores
        self.orders = orders

    def copies(self, part):
        return [
            pltpu.make_async_copy(ref.at[part], out.at[part], self.semaphores.at[part, at])
            for at, (ref, out) in enumerate(zip(self.refs, self.outs))
        ]

    def flush(self, parts):
        for part in parts:
            for copy in self.copies(part):
                copy.start()

    def wait(self):
        for part in range(len(self.orders)):
            for copy in self.copies(part):
                copy.wait()

    def store(self, tile, turn, start, value):
        rows, wide = self.refs[0].shape[2:]
        ref = self.refs[turn & 1]
        width = value.shape[1]
        for group in range(self.cube.groups):
            offset = (group * self.cube.tensors + tile) ^ self.me
            done = 0
            while done < width:
                part, place = divmod(start + done, wide)
                count = min(width - done, wide - place)
                slot = self.cube.slot(offset, self.orders[part][::-1])
                ref[part, slot, :, place : place + count] = value[
                    group * rows : (group + 1) * rows, done : done + count
                ]
                done += count


class Layer:
    def __init__(self, weights, base, hidden):
        self.weights = weights
        self.base = base
        self.hidden = hidden

    def out(self, place):
        return self.weights.block(place, self.base, self.base + LANES)

    def up(self, place):
        start = self.base + LANES
        return self.weights.block(place, start, start + self.hidden)

    def down(self, place):
        start = self.base + LANES + self.hidden
        return self.weights.block(place, start, start + self.hidden)


def tile_lanes(tile):
    if isinstance(tile, int):
        return pl.ds(tile * LANES, LANES)
    return pl.ds(pl.multiple_of(tile * LANES, LANES), LANES)


def add_up(parts):
    total = None
    for part in parts:
        total = part if total is None else total + part
    return total


def whole_spec(shape):
    return pl.BlockSpec(shape, lambda at: (0,) * len(shape))


def columns_spec(weights, columns, at_block):
    groups, tiles, rows, _ = weights.shape
    return pl.BlockSpec((groups, tiles, rows, columns), lambda at: (0, 0, 0, at_block))


def scalar_spec():
    return pl.BlockSpec(memory_space=pltpu.SMEM)


def follow(kernel, first, after):
    count = len(after)
    if not count:
        return kernel

    def late(*refs):
        return kernel(*refs[:first], *refs[first + count :])

    return late


def after_specs(after):
    return [pl.BlockSpec(memory_space=pl.ANY)] * len(after)


def place_of(at):
    return (at, at)


def call(kernel, name, ins, in_specs, outs, scratch=(), after=(), unblocked=0):
    kernel = follow(kernel, len(ins), after)
    ins = (*ins, *after)
    in_specs = [*in_specs, *after_specs(after)]
    return pl.pallas_call(
        kernel,
        grid=(1,),
        in_specs=in_specs,
        out_specs=[
            *after_specs(outs[:unblocked]), *[whole_spec(out.shape) for out in outs[unblocked:]]
        ],
        out_shape=outs,
        scratch_shapes=list(scratch),
        compiler_params=params(),
        name=name,
    )(*ins)


def embed_kernel(
    table_ref, ids_ref, vocab_ref, cos_ref, sin_ref, q_ref, own_ref, other_ref, resid_ref
):
    own = q_ref.shape[0]
    length = ids_ref.shape[1]
    tiles = table_ref.shape[0]
    hot = lax.broadcasted_iota(jnp.int32, (64, length), 0) == ids_ref[...]
    hot = hot.astype(single).T.astype(brain)
    resid_ref[...] = dot(hot[:own], vocab_ref[...])
    hot = hot[:, :TABLE_ROWS]
    cosine = cos_ref[...]
    sine = sin_ref[...]
    for at in range(tiles):
        lanes = slice(at * LANES, (at + 1) * LANES)
        rows = dot_exact(hot, table_ref[at])
        q_ref[:, lanes] = rotate(rows[:own, :LANES], cosine[:own], sine[:own]).astype(brain)
        keys = rotate(rows[:, LANES : 2 * LANES], cosine, sine).astype(brain)
        values = rows[:, 2 * LANES :].astype(brain)
        own_ref[0, :, lanes] = keys[:own]
        own_ref[1, :, lanes] = values[:own]
        other_ref[0, :, lanes] = keys[own:]
        other_ref[1, :, lanes] = values[own:]


def embed(table, ids, vocab, cosine, sine, after):
    tiles = table.shape[0]
    own = ids.shape[1] // 2
    wide = tiles * LANES
    ins = (table, ids, vocab, cosine, sine)
    outs = [
        jax.ShapeDtypeStruct((own, wide), brain),
        jax.ShapeDtypeStruct((2, own, wide), brain),
        jax.ShapeDtypeStruct((2, own, wide), brain),
        jax.ShapeDtypeStruct((own, vocab.shape[1]), single),
    ]
    specs = [whole_spec(x.shape) for x in ins]
    return call(embed_kernel, "embed", ins, specs, outs, (), after)


def attend_kernel(heads, q_ref, own_ref, other_ref, out_ref, logsum_ref):
    own = q_ref.shape[0]
    q_turned = q_ref[...].T
    keys = jnp.concatenate([own_ref[0], other_ref[0]], 0)
    v_turned = jnp.concatenate([own_ref[1], other_ref[1]], 0).T
    rows = lax.broadcasted_iota(jnp.int32, (LANES, own), 0)

    def scores_of(head):
        mine = (rows >= head * HEAD) & (rows < (head + 1) * HEAD)
        return mine, dot(keys, jnp.where(mine, q_turned, jnp.zeros_like(q_turned)))

    mixed = jnp.zeros((LANES, own), single)
    ahead = scores_of(0)
    for head in range(heads):
        mine, scores = ahead
        if head + 1 < heads:
            ahead = scores_of(head + 1)
        peak = column_max(scores) * scale_two
        weights = jnp.exp2(scores * scale_two - peak)
        total = column_sum(weights)
        probs = (weights * (1.0 / total)).astype(brain)
        mixed = jnp.where(mine, dot(v_turned, probs), mixed)
        logsum_ref[0, head : head + 1, :] = peak + jnp.log2(total)
    out_ref[...] = mixed.T.astype(brain)


def attend(q, kv_own, kv_other, heads, after=()):
    own, wide = q.shape
    tiles = wide // LANES
    own_spec = pl.BlockSpec((own, LANES), lambda at: (0, at))
    pair_spec = pl.BlockSpec((2, own, LANES), lambda at: (0, 0, at))
    return pl.pallas_call(
        follow(functools.partial(attend_kernel, heads), 3, after),
        grid=(tiles,),
        in_specs=[own_spec, pair_spec, pair_spec, *after_specs(after)],
        out_specs=[own_spec, pl.BlockSpec((1, 8, own), lambda at: (at, 0, 0))],
        out_shape=[
            jax.ShapeDtypeStruct((own, wide), brain),
            jax.ShapeDtypeStruct((tiles, 8, own), single),
        ],
        compiler_params=params(),
        name="attend",
    )(q, kv_own, kv_other, *after)


def attend_back_kernel(
    heads, chunk, count, me_ref, q_ref, kv_own_ref, kv_other_ref, g_ref, logsum_ref, *refs
):
    dq_ref, own_ref, other_ref = refs[count:]
    own = q_ref.shape[0]
    q = q_ref[...]
    grad = g_ref[...]
    q_turned = q.T
    g_turned = grad.T
    keys = jnp.concatenate([kv_own_ref[0], kv_other_ref[0]], 0)
    values = jnp.concatenate([kv_own_ref[1], kv_other_ref[1]], 0)
    k_turned = keys.T
    rows = lax.broadcasted_iota(jnp.int32, (LANES, chunk), 0)
    lanes = lax.broadcasted_iota(jnp.int32, (chunk, LANES), 1)
    none = jnp.zeros((LANES, chunk), brain)
    none_low = jnp.zeros((chunk, LANES), brain)
    for start in range(0, own, chunk):
        part = slice(start, start + chunk)
        dq = jnp.zeros((LANES, chunk), single)
        for head in range(heads):
            mine = (rows >= head * HEAD) & (rows < (head + 1) * HEAD)
            mine_low = (lanes >= head * HEAD) & (lanes < (head + 1) * HEAD)
            scores = dot(keys, jnp.where(mine, q_turned[:, part], none))
            probs = jnp.exp2(scores * scale_two - logsum_ref[0, head : head + 1, part])
            g_probs = dot(values, jnp.where(mine, g_turned[:, part], none))
            inner = column_sum(probs * g_probs)
            g_scores = (probs * (g_probs - inner)).astype(brain)
            dv = dot(probs.astype(brain), jnp.where(mine_low, grad[part, :], none_low))
            dk = dot(g_scores, jnp.where(mine_low, q[part, :], none_low)) * scale
            if start == 0 and head == 0:
                own_ref[0] = dk[:own]
                own_ref[1] = dv[:own]
                other_ref[0] = dk[own:]
                other_ref[1] = dv[own:]
            else:
                own_ref[0] += dk[:own]
                own_ref[1] += dv[:own]
                other_ref[0] += dk[own:]
                other_ref[1] += dv[own:]
            dq = jnp.where(mine, dot(k_turned, g_scores), dq)
        dq_ref[part, :] = (dq * scale).T


def attend_back(q, kv_own, kv_other, grad, logsum, heads, me, turns, tensors, after=()):
    own, wide = q.shape
    first = turns[0]
    count = len(turns)

    def tile(at, me):
        return (at + first) ^ (me[0] & (tensors - 1))

    own_spec = pl.BlockSpec((own, LANES), lambda at, me: (0, tile(at, me)))
    pair_spec = pl.BlockSpec((2, own, LANES), lambda at, me: (0, 0, tile(at, me)))
    one_shape = jax.ShapeDtypeStruct((own, count * LANES), single)
    one_out = pl.BlockSpec((own, LANES), lambda at, me: (0, at))
    pair_shape = jax.ShapeDtypeStruct((2, own, count * LANES), single)
    pair_out = pl.BlockSpec((2, own, LANES), lambda at, me: (0, 0, at))
    return pl.pallas_call(
        functools.partial(attend_back_kernel, heads, own, len(after)),
        grid_spec=pltpu.PrefetchScalarGridSpec(
            num_scalar_prefetch=1,
            grid=(count,),
            in_specs=[
                own_spec,
                pair_spec,
                pair_spec,
                own_spec,
                pl.BlockSpec((1, 8, own), lambda at, me: (tile(at, me), 0, 0)),
                *after_specs(after),
            ],
            out_specs=[one_out, pair_out, pair_out],
        ),
        out_shape=[one_shape, pair_shape, pair_shape],
        compiler_params=params(),
        name="attend_back",
    )(me, q, kv_own, kv_other, grad, logsum, *after)


def attention_out(mixed, resid, layer, places):
    parts = [
        dot(mixed[:, tile_lanes(place[1])], layer.out(place), 1, 1) for place in places
    ]
    return resid + add_up(parts)


def middle_kernel(
    feats, mixed_ref, resid_ref, w_ref, w_next_ref, norms_ref, cos_ref, sin_ref,
    mid_ref, next_ref, q_ref, kv_ref, w_held, w_semaphores,
):
    tiles = w_ref.shape[1]
    columns = w_held.shape[3]
    copies = [
        pltpu.make_async_copy(
            w_ref.at[:, :, :, first:last], w_held.at[:, :, :, first:last], w_semaphores.at[at]
        )
        for at, (first, last) in enumerate(((0, LANES), (LANES, columns)))
    ]
    for copy in copies:
        copy.start()
    copies[0].wait()
    layer = Layer(Gathered(w_held), 0, (columns - LANES) // 2)
    mid = attention_out(mixed_ref, resid_ref[...], layer, [place_of(at) for at in range(tiles)])
    mid_ref[...] = mid
    normed = feats.norm(mid, norms_ref[2:3], norms_ref[3:4])
    copies[1].wait()
    parts = []
    for at in range(tiles):
        act = gelu(dot(normed, layer.up(place_of(at)))).astype(brain)
        parts.append(dot(act, layer.down(place_of(at)), 1, 1))
    total = mid + add_up(parts)
    next_ref[...] = total
    normed = feats.norm(total, norms_ref[4:5], norms_ref[5:6])
    weights = Gathered(w_next_ref)
    cosine = cos_ref[...]
    sine = sin_ref[...]
    for at in range(tiles):
        lanes = slice(at * LANES, (at + 1) * LANES)
        rows = dot(normed, weights.block(place_of(at), 0, 3 * LANES))
        q_ref[:, lanes] = rotate(rows[:, :LANES], cosine, sine).astype(brain)
        kv_ref[0, :, lanes] = rotate(rows[:, LANES : 2 * LANES], cosine, sine).astype(brain)
        kv_ref[1, :, lanes] = rows[:, 2 * LANES :].astype(brain)


def middle(feats, mixed, resid, weights, columns, at_heads, norms, cosine, sine, after):
    own, wide = mixed.shape
    plain = jax.ShapeDtypeStruct(resid.shape, single)
    in_specs = [
        whole_spec(mixed.shape),
        whole_spec(resid.shape),
        *after_specs((weights,)),
        columns_spec(weights, 3 * LANES, at_heads),
        whole_spec(norms.shape),
        whole_spec(cosine.shape),
        whole_spec(sine.shape),
    ]
    outs = [
        plain,
        plain,
        jax.ShapeDtypeStruct((own, wide), brain),
        jax.ShapeDtypeStruct((2, own, wide), brain),
    ]
    ins = (mixed, resid, weights, weights, norms, cosine, sine)
    scratch = [
        pltpu.VMEM(weights.shape[:3] + (columns,), brain), pltpu.SemaphoreType.DMA((2,))
    ]
    kernel = functools.partial(middle_kernel, feats)
    return call(kernel, "middle", ins, in_specs, outs, scratch, after)


def feed_back(
    feats, turns, g_resid, mid, normed, mixed_ref, layer, gain, act_ref, slope_ref,
    grads, base, g_mid_ref, g_mixed_ref,
):
    hidden = layer.hidden
    g_low = g_resid.astype(brain)
    g_turned = g_low.T
    normed_turned = normed.T
    parts = []
    for turn, tile in turns:
        g_hidden = (dot(g_low, layer.down((turn, tile))) * slope_ref[turn]).astype(brain)
        grads.store(tile, turn, base + LANES + hidden, dot(g_turned, act_ref[turn]))
        grads.store(tile, turn, base + LANES, dot(normed_turned, g_hidden))
        parts.append(dot(g_hidden, layer.up((turn, tile)), 1, 1))
    grads.flush(range(1, len(grads.orders)))
    g_normed = add_up(parts)
    unit, inverse = feats.centred(mid)
    g_gain = jnp.sum(g_normed * unit, 0, keepdims=True)
    g_shift = jnp.sum(g_normed, 0, keepdims=True)
    g_mid = g_resid + feats.norm_back(unit, inverse, gain, g_normed)
    g_mid_ref[...] = g_mid
    g_low = g_mid.astype(brain)
    g_turned = g_low.T
    for turn, tile in turns:
        lanes = tile_lanes(tile)
        g_mixed_ref[:, lanes] = dot(g_low, layer.out((turn, tile))).astype(brain)
        grads.store(tile, turn, base, dot(g_turned, mixed_ref[:, lanes]))
    grads.flush([0])
    return g_gain, g_shift


def top_kernel(
    feats, cube, vocab_count, orders, grad_orders, me_ref, mixed_ref, resid_ref, w_own_ref,
    w_other_ref, norms_ref, vocab_ref, marks_ref, table_ref, keep_ref, send_ref, g_mid_ref, g_mixed_ref,
    g_norms_ref, g_vocab_ref, act_ref, slope_ref, keep_held, send_held, grad_semaphores,
    w_own_held, w_other_held, w_semaphores,
):
    me = me_ref[0]
    tiles = cube.tensors
    turns = [(turn, turn ^ (me & (tiles - 1))) for turn in range(tiles)]
    grads = Scattered(
        cube, me, (keep_held, send_held), (keep_ref, send_ref), grad_semaphores, grad_orders
    )
    copies = [
        [
            pltpu.make_async_copy(ref.at[part], held.at[part], w_semaphores.at[part, at])
            for at, (ref, held) in enumerate(((w_own_ref, w_own_held), (w_other_ref, w_other_held)))
        ]
        for part in range(len(orders))
    ]
    for part in copies:
        for copy in part:
            copy.start()
    for copy in copies[0]:
        copy.wait()
    layer = Layer(Relative(cube, me, (w_own_held, w_other_held), orders), 0, act_ref.shape[2])
    mid = attention_out(mixed_ref, resid_ref[...], layer, turns)
    normed = feats.norm(mid, norms_ref[6:7], norms_ref[7:8])
    for part in copies[1:]:
        for copy in part:
            copy.wait()
    parts = []
    for turn, tile in turns:
        hidden = dot(normed, layer.up((turn, tile)))
        share, bell = normal_share(hidden)
        act = (hidden * share).astype(brain)
        act_ref[turn] = act
        slope_ref[turn] = gelu_slope(hidden, share, bell)
        parts.append(dot(act, layer.down((turn, tile)), 1, 1))
    total = mid + add_up(parts)
    unit, inverse = feats.centred(total)
    gain = norms_ref[8:9]
    final = (unit * gain + norms_ref[9:10]).astype(brain)
    own = total.shape[0]
    marks = marks_ref[...].T.astype(jnp.int32)
    slots = marks.shape[0]
    slot = marks[:, 0:1]
    target = marks[:, 1:2]
    vocab = vocab_ref[...]
    where_hot = (lax.broadcasted_iota(jnp.int32, (slots, own), 1) == slot).astype(single)
    where_hot = where_hot.astype(brain)
    present = (slot >= 0).astype(single)
    picked = dot(where_hot, final).astype(brain)
    logits = dot(picked, vocab, 1, 1)
    lane = lax.broadcasted_iota(jnp.int32, logits.shape, 1)
    logits = jnp.where(lane < vocab_count, logits, -1e30)
    peak = jnp.max(logits, 1, keepdims=True)
    logsum = peak + jnp.log(jnp.sum(jnp.exp(logits - peak), 1, keepdims=True))
    target_hot = (lane == target).astype(single)
    target_logit = jnp.sum(
        jnp.where(lane < vocab_count, logits * target_hot, 0.0), 1, keepdims=True
    )
    loss = jnp.sum((logsum - target_logit) * present, 0, keepdims=True)
    share = present / table_ref[0, vocab_count : vocab_count + 1, 0:1]
    g_logits = ((jnp.exp(logits - logsum) - target_hot) * share).astype(brain)
    g_vocab_ref[...] = dot(g_logits, picked, 0, 0)[:TABLE_ROWS]
    g_picked = dot(g_logits, vocab)
    g_final = dot_exact(where_hot, g_picked, 0, 0)
    g_norms_ref[...] = jnp.zeros_like(g_norms_ref)
    g_norms_ref[8:9] = jnp.sum(g_final * unit, 0, keepdims=True)
    g_norms_ref[9:10] = jnp.sum(g_final, 0, keepdims=True)
    g_norms_ref[LOSS_ROW : LOSS_ROW + 1] = jnp.broadcast_to(loss, (1, g_norms_ref.shape[1]))
    g_resid = feats.norm_back(unit, inverse, gain, g_final)
    g_gain, g_shift = feed_back(
        feats, turns, g_resid, mid, normed, mixed_ref, layer, norms_ref[6:7], act_ref, slope_ref,
        grads, 0, g_mid_ref, g_mixed_ref,
    )
    g_norms_ref[6:7] = g_gain
    g_norms_ref[7:8] = g_shift
    grads.wait()


def top(
    feats, cube, orders, grad_orders, me, mixed, resid, w_own, w_other, norms, vocab,
    vocab_count, marks, table,
):
    own, wide = mixed.shape
    tiles = cube.tensors
    rows = w_own.shape[2]
    columns = w_own.shape[0] * w_own.shape[3] - 3 * LANES
    hidden = (columns - LANES) // 2
    pieces = len(grad_orders)
    grads = (pieces, cube.devices // 2, rows, columns // pieces)
    outs = [
        jax.ShapeDtypeStruct(grads, single),
        jax.ShapeDtypeStruct(grads, single),
        jax.ShapeDtypeStruct(resid.shape, single),
        jax.ShapeDtypeStruct(mixed.shape, brain),
        jax.ShapeDtypeStruct(norms.shape, single),
        jax.ShapeDtypeStruct((TABLE_ROWS, resid.shape[1]), single),
    ]
    in_specs = [
        scalar_spec(),
        whole_spec(mixed.shape),
        whole_spec(resid.shape),
        *after_specs((w_own, w_other)),
        whole_spec(norms.shape),
        whole_spec(vocab.shape),
        whole_spec(marks.shape),
        whole_spec(table.shape),
    ]
    scratch = [
        pltpu.VMEM((tiles, own, hidden), brain),
        pltpu.VMEM((tiles, own, hidden), single),
        pltpu.VMEM(grads, single),
        pltpu.VMEM(grads, single),
        pltpu.SemaphoreType.DMA((pieces, 2)),
        pltpu.VMEM(w_own.shape, brain),
        pltpu.VMEM(w_other.shape, brain),
        pltpu.SemaphoreType.DMA((w_own.shape[0], 2)),
    ]
    ins = (me, mixed, resid, w_own, w_other, norms, vocab, marks, table)
    kernel = functools.partial(top_kernel, feats, cube, vocab_count, orders, grad_orders)
    return call(kernel, "top", ins, in_specs, outs, scratch, (), 2)


def head_grads(turn, heads_refs, cosine, sine):
    dq_ref, own_ref, other_ref = heads_refs[3 * (turn // 2) : 3 * (turn // 2) + 3]
    lanes = tile_lanes(turn % 2)
    other = tile_lanes(1 - turn % 2)
    g_q = unrotate(dq_ref[:, lanes], cosine, sine)
    g_k = unrotate(own_ref[0, :, lanes] + other_ref[0, :, other], cosine, sine)
    g_v = own_ref[1, :, lanes] + other_ref[1, :, other]
    return jnp.concatenate([g_q, g_k, g_v], 1).astype(brain)


def lower_kernel(feats, cube, grad_orders, me_ref, *refs):
    heads_refs = refs[:6]
    (
        g_mid_in_ref, resid_ref, mid_ref, mixed_ref, w_in_ref, w_ref, norms_ref, cos_ref, sin_ref,
        g_norms_in_ref, keep_ref, send_ref, g_mid_ref, g_mixed_ref, g_norms_ref,
        act_ref, slope_ref, keep_held, send_held, grad_semaphores, w_held, w_semaphore,
    ) = refs[6:]
    copy = pltpu.make_async_copy(w_ref.at[:, :, :, : w_held.shape[3]], w_held, w_semaphore)
    copy.start()
    me = me_ref[0]
    tiles = cube.tensors
    turns = [(turn, turn ^ (me & (tiles - 1))) for turn in range(tiles)]
    layer = Layer(Gathered(w_held), 0, act_ref.shape[2])
    weights = Gathered(w_in_ref)
    grads = Scattered(
        cube, me, (keep_held, send_held), (keep_ref, send_ref), grad_semaphores, grad_orders
    )
    unit, inverse = feats.centred(resid_ref[...])
    gain = norms_ref[4:5]
    normed_turned = (unit * gain + norms_ref[5:6]).astype(brain).T
    cosine = cos_ref[...]
    sine = sin_ref[...]
    parts = []
    for turn, tile in turns:
        g_heads = head_grads(turn, heads_refs, cosine, sine)
        grads.store(tile, turn, 0, dot(normed_turned, g_heads))
        parts.append(dot(g_heads, weights.block((turn, tile), 0, 3 * LANES), 1, 1))
    g_normed = add_up(parts)
    g_norms_ref[...] = g_norms_in_ref[...]
    g_norms_ref[4:5] = jnp.sum(g_normed * unit, 0, keepdims=True)
    g_norms_ref[5:6] = jnp.sum(g_normed, 0, keepdims=True)
    g_resid = g_mid_in_ref[...] + feats.norm_back(unit, inverse, gain, g_normed)
    mid = mid_ref[...]
    normed = feats.norm(mid, norms_ref[2:3], norms_ref[3:4])
    copy.wait()
    for turn, tile in turns:
        hidden = dot(normed, layer.up((turn, tile)))
        share, bell = normal_share(hidden)
        act_ref[turn] = (hidden * share).astype(brain)
        slope_ref[turn] = gelu_slope(hidden, share, bell)
    g_gain, g_shift = feed_back(
        feats, turns, g_resid, mid, normed, mixed_ref, layer, norms_ref[2:3], act_ref, slope_ref,
        grads, 3 * LANES, g_mid_ref, g_mixed_ref,
    )
    g_norms_ref[2:3] = g_gain
    g_norms_ref[3:4] = g_shift
    grads.wait()


def lower(
    feats, cube, grad_orders, me, head_parts, g_mid, resid, mid, mixed, weights, at_heads,
    feed_columns, norms, cosine, sine, g_norms, after,
):
    own, wide = mixed.shape
    tiles = cube.tensors
    rows = weights.shape[2]
    hidden = (feed_columns - LANES) // 2
    columns = feed_columns + 3 * LANES
    count = len(grad_orders)
    grads = (count, cube.devices // 2, rows, columns // count)
    outs = [
        jax.ShapeDtypeStruct(grads, single),
        jax.ShapeDtypeStruct(grads, single),
        jax.ShapeDtypeStruct(resid.shape, single),
        jax.ShapeDtypeStruct(mixed.shape, brain),
        jax.ShapeDtypeStruct(norms.shape, single),
    ]
    before = (*head_parts, g_mid, resid, mid, mixed)
    rest = (norms, cosine, sine, g_norms)
    in_specs = [
        scalar_spec(),
        *[whole_spec(x.shape) for x in before],
        columns_spec(weights, 3 * LANES, at_heads),
        *after_specs((weights,)),
        *[whole_spec(x.shape) for x in rest],
    ]
    scratch = [
        pltpu.VMEM((tiles, own, hidden), brain),
        pltpu.VMEM((tiles, own, hidden), single),
        pltpu.VMEM(grads, single),
        pltpu.VMEM(grads, single),
        pltpu.SemaphoreType.DMA((count, 2)),
        pltpu.VMEM(weights.shape[:3] + (feed_columns,), brain),
        pltpu.SemaphoreType.DMA,
    ]
    ins = (me, *before, weights, weights, *rest)
    kernel = functools.partial(lower_kernel, feats, cube, grad_orders)
    return call(kernel, "lower", ins, in_specs, outs, scratch, after, 2)


def stacked_lanes(ref, row, value):
    rows = value.shape[0]
    for at in range(value.shape[1] // LANES):
        ref[row : row + rows, :] = value[:, at * LANES : (at + 1) * LANES]
        row += rows
    return row


def side_by_side(x, rows):
    return jnp.concatenate([x[at : at + rows] for at in range(0, x.shape[0], rows)], 1)


def bottom_kernel(
    feats, cube, orders, me_ref, *refs
):
    heads_refs = refs[:6]
    (
        g_mid_ref, ids_ref, w_own_ref, w_other_ref, norms_ref, vocab_ref, g_vocab_in_ref, g_norms_in_ref, cos_ref,
        sin_ref, keep_ref, send_ref, norms_out_ref,
    ) = refs[6:]
    tiles = cube.tensors
    own = g_mid_ref.shape[0]
    mine = me_ref[0] & (tiles - 1)
    hot = lax.broadcasted_iota(jnp.int32, (TABLE_ROWS, own), 0) == ids_ref[...]
    hot = hot.astype(single).astype(brain)
    cosine = cos_ref[...]
    sine = sin_ref[...]
    weights = Relative(cube, me_ref[0], (w_own_ref, w_other_ref), orders)
    first = w_own_ref.shape[-1] - 3 * LANES
    refs = (keep_ref, send_ref)
    rows = [0, 0]
    parts = []
    for turn in range(tiles):
        tile = turn ^ mine
        g_table = dot(hot, head_grads(turn, heads_refs, cosine, sine))
        rows[turn & 1] = stacked_lanes(refs[turn & 1], rows[turn & 1], g_table)
        weight = weights.block((turn, tile), first, first + 3 * LANES)
        high, middle_part, low = split_three(g_table)
        parts.append(dot(high, weight, 1, 1))
        parts.append(dot(middle_part, weight, 1, 1))
        parts.append(dot(low, weight, 1, 1))
    g_normed = add_up(parts)
    unit, inverse = feats.centred(vocab_ref[...].astype(single)[:TABLE_ROWS])
    norms_out_ref[...] = g_norms_in_ref[...]
    norms_out_ref[0:1] = jnp.sum(g_normed * unit, 0, keepdims=True)
    norms_out_ref[1:2] = jnp.sum(g_normed, 0, keepdims=True)
    g_norms = norms_out_ref[...]
    g_rows = feats.norm_back(unit, inverse, norms_ref[0:1], g_normed)
    g_vocab = g_vocab_in_ref[...] + (dot_exact(hot, g_mid_ref[...]) + g_rows)
    for ref, row in zip(refs, rows):
        row = stacked_lanes(ref, row, g_vocab)
        stacked_lanes(ref, row, g_norms)


def last_part(weights):
    parts = weights.shape[0]
    return pl.BlockSpec((1,) + weights.shape[1:], lambda at: (parts - 1, 0, 0, 0))


def bottom(
    feats, cube, orders, me, head_parts, g_mid, ids, w_own, w_other, norms, vocab, g_vocab,
    g_norms, cosine, sine, after,
):
    tiles = cube.tensors
    table_rows = 3 * TABLE_ROWS * tiles // 2
    vector_rows = (g_vocab.shape[0] + g_norms.shape[0]) * g_vocab.shape[1] // LANES
    out = jax.ShapeDtypeStruct((table_rows + vector_rows, LANES), single)
    before = (*head_parts, g_mid, ids)
    rest = (norms, vocab, g_vocab, g_norms, cosine, sine)
    in_specs = [
        scalar_spec(),
        *[whole_spec(x.shape) for x in before],
        last_part(w_own),
        last_part(w_other),
        *[whole_spec(x.shape) for x in rest],
    ]
    outs = [out, out, jax.ShapeDtypeStruct(norms.shape, single)]
    ins = (me, *before, w_own, w_other, *rest)
    kernel = functools.partial(bottom_kernel, feats, cube, orders[-1:])
    return call(kernel, "bottom", ins, in_specs, outs, (), after)[:2]


def send_kernel(count, skip, keep_ref, got_ref, *refs):
    outs = refs[skip:]
    for part in range(count):
        outs[part][...] = keep_ref[part] + got_ref[part]


def send_upper(keep, got, through, after):
    count, size, rows, wide = keep.shape
    half = size // 2
    step = rows // 2
    upper = pl.BlockSpec((count, half, step, wide), lambda at: (0, 1, at, 0))
    out = jax.ShapeDtypeStruct((half, rows, wide), single)
    results = pl.pallas_call(
        functools.partial(send_kernel, count, len(through) + len(after)),
        grid=(rows // step,),
        in_specs=[upper, upper, *after_specs(through), *after_specs(after)],
        out_specs=[
            *[pl.BlockSpec((half, step, wide), lambda at: (0, at, 0))] * count,
            *after_specs(through),
        ],
        out_shape=[
            *[out] * count,
            *[jax.ShapeDtypeStruct(x.shape, x.dtype) for x in through],
        ],
        input_output_aliases={2 + at: count + at for at in range(len(through))},
        compiler_params=params(),
        name="send_upper",
    )(keep, got, *through, *after)
    return results[:count], results[count:]


def halve_kernel(count, together, stacked, keeps, skip, *refs):
    held = refs[:keeps]
    got_count = 1 if together else count
    got = refs[keeps : keeps + got_count]
    outs = refs[keeps + got_count + skip :]
    size = held[0].shape[1]
    half = size // 2
    for part in range(count):
        arrived = got[0].at[part] if together else got[part]

        def total(rows):
            return add_up([x[part, rows] for x in held]) + arrived[rows]

        if size == 1:
            outs[0][part] = total(slice(0, 1))
        else:
            outs[0][part] = total(slice(0, half))
            send = outs[1].at[part] if stacked else outs[1 + part]
            send[...] = total(slice(half, size))


def halve(keeps, got, through=(), after=(), stacked=False):
    together = not isinstance(got, list)
    got = [got] if together else got
    count, _, rows, wide = keeps[0].shape
    size = got[0].shape[-3]
    step = rows // 2 if size >= 8 else rows
    half = max(size // 2, 1)

    def spec(*lead):
        return pl.BlockSpec((*lead, step, wide), lambda at: (*([0] * len(lead)), at, 0))

    outs = [jax.ShapeDtypeStruct((count, half, rows, wide), single)]
    out_specs = [spec(count, half)]
    if size > 1 and stacked:
        outs += outs
        out_specs += out_specs
    elif size > 1:
        outs += [jax.ShapeDtypeStruct((half, rows, wide), single)] * count
        out_specs += [spec(half)] * count
    sends = len(outs) - 1
    got_specs = [spec(count, size)] if together else [spec(size)] * count
    ins = (*keeps, *got)
    aliases = {len(ins) + at: len(outs) + at for at in range(len(through))}
    outs += [jax.ShapeDtypeStruct(x.shape, x.dtype) for x in through]
    skip = len(through) + len(after)
    results = pl.pallas_call(
        functools.partial(halve_kernel, count, together, stacked, len(keeps), skip),
        grid=(rows // step,),
        in_specs=[
            *[spec(count, size)] * len(keeps),
            *got_specs,
            *after_specs(through),
            *after_specs(after),
        ],
        out_specs=[*out_specs, *after_specs(through)],
        out_shape=outs,
        input_output_aliases=aliases,
        compiler_params=params(),
        name="halve",
    )(*ins, *through, *after)
    going = results[1] if stacked and sends else results[1 : 1 + sends]
    return results[0], going, results[1 + sends :]


def join_kernel(count, together, stacked, skip, *refs):
    ins = 1 if together else count
    helds, gots = refs[:ins], refs[ins : 2 * ins]
    outs = refs[2 * ins + skip :]
    for part in range(count):
        held = helds[0].at[part] if together else helds[part]
        got = gots[0].at[part] if together else gots[part]
        out = outs[0].at[part] if stacked else outs[part]
        size = held.shape[0]
        out[:size] = held[...]
        out[size:] = got[...]


def join(held, got, count, stacked, through=(), after=()):
    together = not isinstance(held, list)
    ins = (held, got) if together else (*held, *got)
    size, rows, wide = ins[0].shape[-3:]
    shape = (2 * size, rows, wide)
    if stacked:
        outs = [jax.ShapeDtypeStruct((count,) + shape, ins[0].dtype)]
    else:
        outs = [jax.ShapeDtypeStruct(shape, ins[0].dtype)] * count
    aliases = {len(ins) + at: len(outs) + at for at in range(len(through))}
    skip = len(through) + len(after)
    results = pl.pallas_call(
        functools.partial(join_kernel, count, together, stacked, skip),
        grid=(1,),
        in_specs=[
            *[whole_spec(x.shape) for x in ins], *after_specs(through), *after_specs(after)
        ],
        out_specs=[*[whole_spec(out.shape) for out in outs], *after_specs(through)],
        out_shape=[*outs, *[jax.ShapeDtypeStruct(x.shape, x.dtype) for x in through]],
        input_output_aliases=aliases,
        compiler_params=params(),
        name="join",
    )(*ins, *through, *after)
    joined = results[0] if stacked else list(results[:count])
    return joined, results[len(outs) :]


def wait_kernel(*refs):
    pass


def wait_for(x, after):
    return pl.pallas_call(
        wait_kernel,
        in_specs=after_specs((x, *after)),
        out_specs=after_specs((x,))[0],
        out_shape=jax.ShapeDtypeStruct(x.shape, x.dtype),
        input_output_aliases={0: 0},
        compiler_params=params(),
        name="wait_for",
    )(x, *after)


class Gather:
    def __init__(self, cube, parts):
        count = len(parts)
        self.cube = cube
        self.count = count
        turning = [cube.outer(turn)[:-1] for turn in range(count)]
        self.orders = [[cube.size - 1] + turns for turns in turning]
        self.held = jnp.stack(parts)[:, None]
        self.got = cube.swap(self.held, cube.size - 1)
        self.at = 1

    def step(self, through=(), after=()):
        last = self.at == len(self.orders[0])
        self.held, through = join(self.held, self.got, self.count, last, through, after)
        if not last:
            self.got = [
                self.cube.swap(x, order[self.at]) for x, order in zip(self.held, self.orders)
            ]
        self.at += 1
        return through

    def finish(self, after):
        self.held = wait_for(self.held, after)
        self.got = self.cube.swap(self.held, 0)


def normalize_features(resid, gain, shift):
    centre = resid - jnp.mean(resid, -1, keepdims=True)
    spread = jnp.mean(centre * centre, -1, keepdims=True)
    return centre * lax.rsqrt(spread + norm_eps) * gain + shift


def adamw(master, first, second, grad, step_rate):
    mean = beta_first * first + (1.0 - beta_first) * grad
    square = beta_second * second + (1.0 - beta_second) * grad * grad
    corrected = mean / (1.0 - beta_first**STEP)
    rescaled_values = square / (1.0 - beta_second**STEP)
    fresh = master - step_rate * (
        corrected / (jnp.sqrt(rescaled_values) + adam_eps) + weight_decay * master
    )
    return (fresh, mean, square)


def pad_lanes(x, lanes):
    return jnp.pad(x, [(0, 0)] * (x.ndim - 1) + [(0, lanes - x.shape[-1])])


def make_shards(groups, tensors):
    axes = ("dp", "tensor")
    cube = Cube(groups, tensors)

    def shards(
        token_ids,
        mask_pos,
        mask_target,
        mask_count,
        weight_in,
        weight_out,
        weight_up,
        weight_down,
        norm_params,
        vocab_table,
        first_in,
        first_out,
        first_up,
        first_down,
        first_norm,
        first_vocab,
        second_in,
        second_out,
        second_up,
        second_down,
        second_norm,
        second_vocab,
    ):
        layers, block, in_wide = weight_in.shape
        heads = in_wide // (3 * HEAD)
        per_heads = heads * HEAD
        hidden = weight_up.shape[2]
        hidden_padded = -(-hidden // LANES) * LANES
        vocab_count, width = vocab_table.shape
        feats = Features(width, groups)
        local_len = token_ids.shape[1]
        length = local_len * tensors
        own = length // 2
        here = lax.axis_index("tensor")
        group_at = lax.axis_index("dp")
        me = (group_at * tensors + here).astype(jnp.int32).reshape(1)
        sequence = here // 2
        quarters = jnp.stack([here, here ^ 2, here ^ 1, here ^ 3])

        heads_in = weight_in.astype(brain).transpose(1, 0, 2)
        heads_in = heads_in.reshape(block, layers, heads, 3, HEAD).transpose(0, 1, 3, 2, 4)
        heads_in = pad_lanes(heads_in.reshape(block, layers, 3, per_heads), LANES)
        heads_in = heads_in.reshape(block, layers, 3 * LANES)
        feed = jnp.concatenate(
            [
                pad_lanes(weight_out.astype(brain).transpose(2, 0, 1), LANES),
                pad_lanes(weight_up.astype(brain).transpose(1, 0, 2), hidden_padded),
                pad_lanes(weight_down.astype(brain).transpose(2, 0, 1), hidden_padded),
            ],
            2,
        )
        feed_columns = feed.shape[2]

        def pad_rows(x):
            return jnp.pad(x, ((0, feats.padded - block), (0, 0)))

        vocab_low = vocab_table.astype(brain)
        vocab_padded = jnp.pad(feats.pad(vocab_low), ((0, 64 - vocab_count), (0, 0)))
        norms = jnp.pad(feats.pad(norm_params), ((0, 16 - norm_params.shape[0]), (0, 0)))

        def gather_all(x):
            x = lax.all_gather(x, axes, axis=0, tiled=False)
            return x.reshape((groups, tensors) + x.shape[1:])

        weights = gather_all(pad_rows(jnp.concatenate([feed[:, 0], heads_in[:, 1]], 1)))
        at_heads = feed_columns // (3 * LANES)
        later = pad_rows(jnp.concatenate([feed[:, 1], heads_in[:, 0]], 1))
        third = later.shape[1] // 3
        gather = Gather(cube, [later[:, at : at + third] for at in range(0, 3 * third, third)])

        table_low = normalize_features(
            lax.reduce_precision(vocab_table, 8, 7), norm_params[0], norm_params[1]
        ).astype(brain)
        table_own = lax.dynamic_slice_in_dim(
            table_low.reshape(vocab_count, groups, block), group_at, 1, 1
        )[:, 0]
        table = dot(table_own, heads_in[:, 0])
        extra = jnp.zeros((TABLE_ROWS - vocab_count, 3 * LANES), single)
        extra = extra.at[0, 0].set(jnp.sum(mask_count).astype(single))
        table = jnp.concatenate([table, extra], 0)
        for at in range(2, cube.size):
            table = table + cube.swap(table, at)
        count_total = table[vocab_count, 0]
        ids_row = vocab_count + 1
        table = lax.dynamic_update_slice(
            table, pad_lanes(token_ids.astype(single), 3 * LANES), (ids_row, 0)
        )
        got = cube.swap(table, 1)
        upper = (here & 2) == 2
        pair = jnp.stack([jnp.where(upper, got, table), jnp.where(upper, table, got)])
        got = cube.swap(pair, 0)
        upper = (here & 1) == 1
        table = jnp.stack([jnp.where(upper, got, pair), jnp.where(upper, pair, got)], 1)
        table = table.reshape(tensors, TABLE_ROWS, 3 * LANES)
        ids = jnp.take(table[:, ids_row : ids_row + 2, :local_len], sequence, axis=1)
        ids = jnp.take(ids, quarters, axis=0).reshape(1, length).astype(jnp.int32)

        half = HEAD // 2
        freqs = 10000.0 ** (-jnp.arange(half, dtype=single) * 2.0 / HEAD)
        positions = (quarters[:, None] * local_len + jnp.arange(local_len)[None, :]).reshape(length)
        angles = positions.astype(single)[:, None] * freqs[None, :]
        cosine, sine = (jnp.cos(angles), jnp.sin(angles))
        cosine = pad_lanes(jnp.tile(jnp.concatenate([cosine, cosine], 1), (1, heads)), LANES)
        sine = pad_lanes(jnp.tile(jnp.concatenate([-sine, sine], 1), (1, heads)), LANES)
        cos_own, sin_own = (cosine[:own], sine[:own])

        slots = mask_pos.shape[1]
        my_pos = jnp.take(mask_pos, sequence, axis=0)
        my_count = jnp.take(mask_count, sequence, axis=0)
        quarter = my_pos // local_len
        inside = my_pos % local_len
        slot = jnp.where(
            quarter == here, inside, jnp.where(quarter == (here ^ 2), inside + local_len, -1)
        )
        slot = jnp.where(jnp.arange(slots) < my_count, slot, -1)
        target = jnp.take(mask_target, sequence, axis=0)
        marks = jnp.zeros((8, slots), jnp.int32).at[0].set(slot).at[1].set(target)
        marks = marks.astype(single)

        gather.step((), (table,))
        q_low, kv_low, kv_low_other, resid_low = embed(table, ids, vocab_padded, cosine, sine, ())
        while gather.at + 2 < cube.size:
            gather.step((), (q_low,))
        mixed_low, logsum_low = attend(q_low, kv_low, kv_low_other, heads)
        gather.step((), (logsum_low,))
        mid_low, resid, q, kv = middle(
            feats, mixed_low, resid_low, weights, feed_columns, at_heads, norms, cos_own, sin_own,
            (),
        )
        (kv,) = gather.step((kv,), (resid,))
        kv_other = cube.swap(kv, 0)
        gather.finish((kv_other,))
        mixed, logsum = attend(q, kv, kv_other, heads)
        grad_orders = [cube.outer(turn) for turn in range(3)]

        last_step = cube.size - 2

        class Sums:
            def __init__(self, keep, send):
                self.keeps = (keep,)
                self.got = cube.swap(send, 0)
                self.at = 0

            def step(self, through=(), after=()):
                stacked = self.at == last_step
                if self.at == 0:
                    sends, through = send_upper(*self.keeps, self.got, through, after)
                    self.keeps = (*self.keeps, self.got)
                    self.done = sends[0]
                else:
                    keep, sends, through = halve(self.keeps, self.got, through, after, stacked)
                    self.keeps = (keep,)
                    self.done = keep
                if stacked:
                    self.got = cube.swap(sends, grad_orders[0][-1])
                else:
                    self.got = [
                        cube.swap(x, order[self.at]) for x, order in zip(sends, grad_orders)
                    ]
                self.at += 1
                return through

            def finish(self, through=(), after=()):
                keep, _, through = halve(self.keeps, self.got, through, after)
                return keep[:, 0], through

        def exchange(arrays):
            return [cube.swap(x, 0) for x in arrays]

        first_turns = list(range(tensors // 2))
        last_turns = list(range(tensors // 2, tensors))
        keep, send, g_mid, g_mixed, g_norms, g_vocab = top(
            feats, cube, gather.orders, grad_orders, me, mixed, resid, gather.held, gather.got,
            norms, vocab_padded, vocab_count, marks, table,
        )
        sums_top = Sums(keep, send)
        part = (q, kv, kv_other, g_mixed, logsum, heads, me)
        first = attend_back(*part, first_turns, tensors)
        got_first = exchange(sums_top.step(first[2:], (first[0],)))
        last = attend_back(*part, last_turns, tensors, (sums_top.done,))
        got_last = exchange(sums_top.step(last[2:], (last[0],)))
        head_parts = (*first[:2], *got_first, *last[:2], *got_last)
        keep, send, g_mid, g_mixed, g_norms = lower(
            feats, cube, grad_orders, me, head_parts, g_mid, resid, mid_low, mixed_low, weights,
            at_heads, feed_columns, norms, cos_own, sin_own, g_norms, (sums_top.done,),
        )
        (send,) = sums_top.step((send,), (g_mid,))
        sums_low = Sums(keep, send)
        part = (q_low, kv_low, kv_low_other, g_mixed, logsum_low, heads, me)
        first = attend_back(*part, first_turns, tensors, (sums_top.done,))
        got_first = exchange(sums_top.step(first[2:], (first[0],)))
        sums_low.step((), (sums_top.done,))
        last = attend_back(*part, last_turns, tensors, (sums_low.done,))
        got_last = exchange(sums_low.step(last[2:], (last[0],)))
        head_parts = (*first[:2], *got_first, *last[:2], *got_last)
        keep_table, send_table = bottom(
            feats, cube, gather.orders, me, head_parts, g_mid, ids[:, :own], gather.held,
            gather.got, norms, vocab_padded, g_vocab, g_norms, cos_own, sin_own, (sums_low.done,),
        )
        got = cube.swap(send_table, 0)
        (keep_table,) = sums_low.step((keep_table,))
        total = keep_table + got
        tile_rows = 3 * TABLE_ROWS
        got = cube.swap(total[tile_rows:], 1)
        (total,) = sums_low.step((total,))
        total = jnp.concatenate(
            [total[:tile_rows] + got[:tile_rows], total[2 * tile_rows :] + got[tile_rows:]], 0
        )
        done = 2
        if cube.size > 4:
            near, far, both = cube.swap(total, 2), cube.swap(total, 3), cube.swap(total, 2, 3)
            total = (total + near) + (far + both)
            done = 4
        for at in range(done, cube.size):
            total = total + cube.swap(total, at)
        while sums_low.at <= last_step:
            sums_low.step()
        while sums_top.at <= last_step:
            sums_top.step((), (keep_table,))
        grads_low, _ = sums_low.finish()
        grads_top, _ = sums_top.finish((), (sums_low.done,))
        grads_top = jnp.concatenate(list(grads_top), 1)
        grads_low = jnp.concatenate(list(grads_low), 1)
        g_table = side_by_side(total[:tile_rows], TABLE_ROWS)[:vocab_count]
        vocab_rows = TABLE_ROWS * feats.total // LANES
        g_vocab = side_by_side(total[tile_rows : tile_rows + vocab_rows], TABLE_ROWS)
        g_vocab = feats.unpad(g_vocab[:vocab_count])
        g_norms = side_by_side(total[tile_rows + vocab_rows :], norms.shape[0])
        loss_total = g_norms[LOSS_ROW, 0]
        g_norms = feats.unpad(g_norms[: norm_params.shape[0]])
        grads_in_low = lax.dot_general(
            table_own.astype(single),
            g_table,
            (((0,), (0,)), ((), ())),
            precision=highest,
            preferred_element_type=single,
        )

        def unpack_in(grad):
            grad = grad[:block].reshape(block, 3, LANES)[:, :, :per_heads]
            return grad.reshape(block, 3, heads, HEAD).transpose(0, 2, 1, 3).reshape(block, in_wide)

        low_start = 3 * LANES
        start = LANES + hidden_padded
        grad_in = jnp.stack([unpack_in(grads_in_low), unpack_in(grads_low[:, :low_start])], 1)
        both = jnp.stack([grads_low[:block, low_start:], grads_top[:block]], 1)
        grads = (
            grad_in,
            both[:, :, :per_heads],
            both[:, :, LANES : LANES + hidden],
            both[:, :, start : start + hidden],
            g_norms,
            g_vocab,
        )
        by_rows = Layout(major_to_minor=(0, 1, 2))
        grads = [with_layout_constraint(x, by_rows) for x in grads[:4]] + list(grads[4:])
        turned = [(1, 0, 2), (2, 0, 1), (1, 0, 2), (2, 0, 1), None, None]
        turned_back = [(1, 0, 2), (1, 2, 0), (1, 0, 2), (1, 2, 0), None, None]

        def turn_all(arrays, orders):
            return [x if order is None else x.transpose(order) for x, order in zip(arrays, orders)]

        masters = (weight_in, weight_out, weight_up, weight_down, norm_params, vocab_table)
        firsts = (first_in, first_out, first_up, first_down, first_norm, first_vocab)
        seconds = (second_in, second_out, second_up, second_down, second_norm, second_vocab)
        masters, firsts, seconds = [turn_all(x, turned) for x in (masters, firsts, seconds)]
        results = [
            adamw(masters[which], firsts[which], seconds[which], grads[which], step_rates[which])
            for which in range(6)
        ]
        news, means, squares = [
            turn_all([entry[which] for entry in results], turned_back) for which in range(3)
        ]
        copies = [news[which].astype(brain) for which in (0, 1, 2, 3, 5)]
        return (loss_total, count_total, *news, *means, *squares, *copies)

    return shards


def solution(mesh):
    rows_in = P(None, "dp", "tensor")
    rows_out = P(None, "tensor", "dp")
    six = (rows_in, rows_out, rows_in, rows_out, P(), P())
    five = (rows_in, rows_out, rows_in, rows_out, P())
    return jax.shard_map(
        make_shards(mesh.shape["dp"], mesh.shape["tensor"]),
        mesh=mesh,
        in_specs=(P("dp", "tensor"), P("dp", None), P("dp", None), P("dp"), *six, *six, *six),
        out_specs=(P(), P(), *six, *six, *six, *five),
        check_vma=False,
    )
```

```python
import functools
import math

import jax
import jax.numpy as jnp
from jax import lax
from jax.experimental import pallas as pl
from jax.experimental.layout import Layout, with_layout_constraint
from jax.experimental.pallas import tpu as pltpu
from jax.sharding import PartitionSpec as P

HEAD = 24
STEP = 5
LANES = 128
TABLE_ROWS = 40
LOSS_ROW = 10
VMEM_BYTES = 60 * 1024 * 1024

norm_eps = 1e-05
step_rates = (0.02, 0.3, 0.02, 0.02, 0.3, 0.05)
beta_first = 0.5
beta_second = 0.5
adam_eps = 1e-08
weight_decay = 0.01
highest = lax.Precision.HIGHEST
brain = jnp.bfloat16
single = jnp.float32
scale = HEAD ** (-0.5)
scale_two = scale * math.log2(math.e)

params = functools.partial(pltpu.CompilerParams, vmem_limit_bytes=VMEM_BYTES)


class Cube:
    def __init__(self, groups, tensors):
        self.groups = groups
        self.tensors = tensors
        self.devices = groups * tensors
        self.size = self.devices.bit_length() - 1
        self.masks = [1 << at for at in range(self.size)]
        self.folded = groups >= 4
        if self.folded:
            self.masks[-1] |= self.masks[-2]

    def swap(self, x, *dimensions):
        mask = 0
        for at in dimensions:
            mask ^= self.masks[at]
        pairs = [(device, device ^ mask) for device in range(self.devices)]
        return lax.ppermute(x, ("dp", "tensor"), pairs)

    def outer(self, turn):
        rest = list(range(1, self.size))
        rest = rest[1:2] + rest[:1] + rest[2:]
        turning = rest[:-1]
        turn = turn % len(turning)
        return turning[turn:] + turning[:turn] + rest[-1:]

    def steps(self, offset):
        bits = [(offset >> at) & 1 for at in range(self.size)]
        if self.folded:
            bits[-2] = bits[-2] ^ bits[-1]
        return bits

    def slot(self, offset, order):
        bits = self.steps(offset)
        place = 0
        for rank, at in enumerate(order):
            place = place + (bits[at] << rank)
        return place


def dot(left, right, left_dim=1, right_dim=0):
    return lax.dot_general(
        left, right, (((left_dim,), (right_dim,)), ((), ())), preferred_element_type=single
    )


def split_three(x):
    high = x.astype(brain)
    rest = x - high.astype(single)
    middle = rest.astype(brain)
    return high, middle, (rest - middle.astype(single)).astype(brain)


def dot_exact(hot, x, left_dim=1, right_dim=0):
    high, middle, low = split_three(x)
    tail = dot(hot, middle, left_dim, right_dim) + dot(hot, low, left_dim, right_dim)
    return dot(hot, high, left_dim, right_dim) + tail


def fold_rows(x, op, parts=8):
    size = x.shape[0] // parts
    pieces = [x[at * size : (at + 1) * size] for at in range(parts)]
    while len(pieces) > 1:
        pieces = [op(pieces[at], pieces[at + 1]) for at in range(0, len(pieces), 2)]
    return pieces[0]


def column_max(x):
    return jnp.max(fold_rows(x, jnp.maximum), 0, keepdims=True)


def column_sum(x):
    return jnp.sum(fold_rows(x, jnp.add), 0, keepdims=True)


tail_slope = 0.3275911 * math.sqrt(0.5)
tail_terms = tuple(
    0.5 * term for term in (1.061405429, -1.453152027, 1.421413741, -0.284496736, 0.254829592)
)


def normal_share(x):
    bell = jnp.exp2(x * x * (-0.5 * math.log2(math.e)))
    below = 1.0 + jnp.abs(x) * tail_slope
    t = 1.0 / below
    tail = tail_terms[0] * t + tail_terms[1]
    for term in tail_terms[2:]:
        tail = tail * t + term
    tail = tail * (t * bell)
    return jnp.where(x < 0.0, tail, 1.0 - tail), bell


def gelu(x):
    return x * normal_share(x)[0]


def gelu_slope(x, share, bell):
    return share + (x * (1.0 / math.sqrt(2.0 * math.pi))) * bell


def rotary_partner(x):
    lane = lax.broadcasted_iota(jnp.int32, x.shape, 1) % HEAD
    return jnp.where(
        lane < HEAD // 2,
        pltpu.roll(x, LANES - HEAD // 2, 1),
        pltpu.roll(x, HEAD // 2, 1),
    )


def rotate(x, cosine, sine):
    return x * cosine + rotary_partner(x) * sine


def unrotate(x, cosine, sine):
    return x * cosine - rotary_partner(x) * sine


class Features:
    def __init__(self, width, groups):
        self.width = width
        self.groups = groups
        self.block = width // groups
        self.padded = -(-self.block // 16) * 16
        self.total = self.padded * groups

    def pad(self, x):
        rows = x.shape[0]
        x = x.reshape(rows, self.groups, self.block)
        x = jnp.pad(x, ((0, 0), (0, 0), (0, self.padded - self.block)))
        return x.reshape(rows, self.total)

    def unpad(self, x):
        rows = x.shape[0]
        x = x.reshape(rows, self.groups, self.padded)[:, :, : self.block]
        return x.reshape(rows, self.width)

    def live(self, shape):
        lane = lax.broadcasted_iota(jnp.int32, shape, 1) % self.padded
        return lane < self.block

    def centred(self, x):
        mean = jnp.sum(x, 1, keepdims=True) * (1.0 / self.width)
        centre = jnp.where(self.live(x.shape), x - mean, 0.0)
        spread = jnp.sum(centre * centre, 1, keepdims=True) * (1.0 / self.width)
        inverse = lax.rsqrt(spread + norm_eps)
        return centre * inverse, inverse

    def norm(self, x, gain, shift):
        unit, _ = self.centred(x)
        return (unit * gain + shift).astype(brain)

    def norm_back(self, unit, inverse, gain, grad):
        scaled = grad * gain
        mean = jnp.sum(scaled, 1, keepdims=True) * (1.0 / self.width)
        along = jnp.sum(scaled * unit, 1, keepdims=True) * (1.0 / self.width)
        back = inverse * (scaled - mean - unit * along)
        return jnp.where(self.live(back.shape), back, 0.0)


class Gathered:
    def __init__(self, ref):
        self.ref = ref

    def block(self, place, start, stop):
        groups, _, rows, _ = self.ref.shape
        return self.ref[:, place[1], :, start:stop].reshape(groups * rows, stop - start)


class Relative:
    def __init__(self, cube, me, refs, orders):
        self.cube = cube
        self.me = me
        self.refs = refs
        self.orders = orders

    def block(self, place, start, stop):
        turn, tile = place
        ref = self.refs[turn & 1]
        wide = ref.shape[-1]
        pieces = []
        while start < stop:
            part, first = divmod(start, wide)
            last = min(wide, first + stop - start)
            rows = []
            for group in range(self.cube.groups):
                offset = (group * self.cube.tensors + tile) ^ self.me
                rows.append(ref[part, self.cube.slot(offset, self.orders[part]), :, first:last])
            pieces.append(jnp.concatenate(rows, 0))
            start += last - first
        return pieces[0] if len(pieces) == 1 else jnp.concatenate(pieces, 1)


class Scattered:
    def __init__(self, cube, me, refs, outs, semaphores, orders):
        self.cube = cube
        self.me = me
        self.refs = refs
        self.outs = outs
        self.semaphores = semaphores
        self.orders = orders

    def copies(self, part):
        return [
            pltpu.make_async_copy(ref.at[part], out.at[part], self.semaphores.at[part, at])
            for at, (ref, out) in enumerate(zip(self.refs, self.outs))
        ]

    def flush(self, parts):
        for part in parts:
            for copy in self.copies(part):
                copy.start()

    def wait(self):
        for part in range(len(self.orders)):
            for copy in self.copies(part):
                copy.wait()

    def store(self, tile, turn, start, value):
        rows, wide = self.refs[0].shape[2:]
        ref = self.refs[turn & 1]
        width = value.shape[1]
        for group in range(self.cube.groups):
            offset = (group * self.cube.tensors + tile) ^ self.me
            done = 0
            while done < width:
                part, place = divmod(start + done, wide)
                count = min(width - done, wide - place)
                slot = self.cube.slot(offset, self.orders[part][::-1])
                ref[part, slot, :, place : place + count] = value[
                    group * rows : (group + 1) * rows, done : done + count
                ]
                done += count


class Layer:
    def __init__(self, weights, base, hidden):
        self.weights = weights
        self.base = base
        self.hidden = hidden

    def out(self, place):
        return self.weights.block(place, self.base, self.base + LANES)

    def up(self, place):
        start = self.base + LANES
        return self.weights.block(place, start, start + self.hidden)

    def down(self, place):
        start = self.base + LANES + self.hidden
        return self.weights.block(place, start, start + self.hidden)


def tile_lanes(tile):
    if isinstance(tile, int):
        return pl.ds(tile * LANES, LANES)
    return pl.ds(pl.multiple_of(tile * LANES, LANES), LANES)


def add_up(parts):
    total = None
    for part in parts:
        total = part if total is None else total + part
    return total


def whole_spec(shape):
    return pl.BlockSpec(shape, lambda at: (0,) * len(shape))


def columns_spec(weights, columns, at_block):
    groups, tiles, rows, _ = weights.shape
    return pl.BlockSpec((groups, tiles, rows, columns), lambda at: (0, 0, 0, at_block))


def scalar_spec():
    return pl.BlockSpec(memory_space=pltpu.SMEM)


def follow(kernel, first, after):
    count = len(after)
    if not count:
        return kernel

    def late(*refs):
        return kernel(*refs[:first], *refs[first + count :])

    return late


def after_specs(after):
    return [pl.BlockSpec(memory_space=pl.ANY)] * len(after)


def place_of(at):
    return (at, at)


def call(kernel, name, ins, in_specs, outs, scratch=(), after=(), unblocked=0):
    kernel = follow(kernel, len(ins), after)
    ins = (*ins, *after)
    in_specs = [*in_specs, *after_specs(after)]
    return pl.pallas_call(
        kernel,
        grid=(1,),
        in_specs=in_specs,
        out_specs=[
            *after_specs(outs[:unblocked]), *[whole_spec(out.shape) for out in outs[unblocked:]]
        ],
        out_shape=outs,
        scratch_shapes=list(scratch),
        compiler_params=params(),
        name=name,
    )(*ins)


def embed_kernel(
    table_ref, ids_ref, vocab_ref, cos_ref, sin_ref, q_ref, own_ref, other_ref, resid_ref
):
    own = q_ref.shape[0]
    length = ids_ref.shape[1]
    tiles = table_ref.shape[0]
    hot = lax.broadcasted_iota(jnp.int32, (64, length), 0) == ids_ref[...]
    hot = hot.astype(single).T.astype(brain)
    resid_ref[...] = dot(hot[:own], vocab_ref[...])
    hot = hot[:, :TABLE_ROWS]
    cosine = cos_ref[...]
    sine = sin_ref[...]
    for at in range(tiles):
        lanes = slice(at * LANES, (at + 1) * LANES)
        rows = dot_exact(hot, table_ref[at])
        q_ref[:, lanes] = rotate(rows[:own, :LANES], cosine[:own], sine[:own]).astype(brain)
        keys = rotate(rows[:, LANES : 2 * LANES], cosine, sine).astype(brain)
        values = rows[:, 2 * LANES :].astype(brain)
        own_ref[0, :, lanes] = keys[:own]
        own_ref[1, :, lanes] = values[:own]
        other_ref[0, :, lanes] = keys[own:]
        other_ref[1, :, lanes] = values[own:]


def embed(table, ids, vocab, cosine, sine, after):
    tiles = table.shape[0]
    own = ids.shape[1] // 2
    wide = tiles * LANES
    ins = (table, ids, vocab, cosine, sine)
    outs = [
        jax.ShapeDtypeStruct((own, wide), brain),
        jax.ShapeDtypeStruct((2, own, wide), brain),
        jax.ShapeDtypeStruct((2, own, wide), brain),
        jax.ShapeDtypeStruct((own, vocab.shape[1]), single),
    ]
    specs = [whole_spec(x.shape) for x in ins]
    return call(embed_kernel, "embed", ins, specs, outs, (), after)


def attend_kernel(heads, q_ref, own_ref, other_ref, out_ref, logsum_ref):
    own = q_ref.shape[0]
    q_turned = q_ref[...].T
    keys = jnp.concatenate([own_ref[0], other_ref[0]], 0)
    v_turned = jnp.concatenate([own_ref[1], other_ref[1]], 0).T
    rows = lax.broadcasted_iota(jnp.int32, (LANES, own), 0)

    def scores_of(head):
        mine = (rows >= head * HEAD) & (rows < (head + 1) * HEAD)
        return mine, dot(keys, jnp.where(mine, q_turned, jnp.zeros_like(q_turned)))

    mixed = jnp.zeros((LANES, own), single)
    ahead = scores_of(0)
    for head in range(heads):
        mine, scores = ahead
        if head + 1 < heads:
            ahead = scores_of(head + 1)
        peak = column_max(scores) * scale_two
        weights = jnp.exp2(scores * scale_two - peak)
        total = column_sum(weights)
        probs = (weights * (1.0 / total)).astype(brain)
        mixed = jnp.where(mine, dot(v_turned, probs), mixed)
        logsum_ref[0, head : head + 1, :] = peak + jnp.log2(total)
    out_ref[...] = mixed.T.astype(brain)


def attend(q, kv_own, kv_other, heads, after=()):
    own, wide = q.shape
    tiles = wide // LANES
    own_spec = pl.BlockSpec((own, LANES), lambda at: (0, at))
    pair_spec = pl.BlockSpec((2, own, LANES), lambda at: (0, 0, at))
    return pl.pallas_call(
        follow(functools.partial(attend_kernel, heads), 3, after),
        grid=(tiles,),
        in_specs=[own_spec, pair_spec, pair_spec, *after_specs(after)],
        out_specs=[own_spec, pl.BlockSpec((1, 8, own), lambda at: (at, 0, 0))],
        out_shape=[
            jax.ShapeDtypeStruct((own, wide), brain),
            jax.ShapeDtypeStruct((tiles, 8, own), single),
        ],
        compiler_params=params(),
        name="attend",
    )(q, kv_own, kv_other, *after)


def attend_back_kernel(
    heads, chunk, count, me_ref, q_ref, kv_own_ref, kv_other_ref, g_ref, logsum_ref, *refs
):
    dq_ref, own_ref, other_ref = refs[count:]
    own = q_ref.shape[0]
    q = q_ref[...]
    grad = g_ref[...]
    q_turned = q.T
    g_turned = grad.T
    keys = jnp.concatenate([kv_own_ref[0], kv_other_ref[0]], 0)
    values = jnp.concatenate([kv_own_ref[1], kv_other_ref[1]], 0)
    k_turned = keys.T
    rows = lax.broadcasted_iota(jnp.int32, (LANES, chunk), 0)
    lanes = lax.broadcasted_iota(jnp.int32, (chunk, LANES), 1)
    none = jnp.zeros((LANES, chunk), brain)
    none_low = jnp.zeros((chunk, LANES), brain)
    for start in range(0, own, chunk):
        part = slice(start, start + chunk)
        dq = jnp.zeros((LANES, chunk), single)
        for head in range(heads):
            mine = (rows >= head * HEAD) & (rows < (head + 1) * HEAD)
            mine_low = (lanes >= head * HEAD) & (lanes < (head + 1) * HEAD)
            scores = dot(keys, jnp.where(mine, q_turned[:, part], none))
            probs = jnp.exp2(scores * scale_two - logsum_ref[0, head : head + 1, part])
            g_probs = dot(values, jnp.where(mine, g_turned[:, part], none))
            product = probs * g_probs
            inner = column_sum(product)
            g_scores = (product - probs * inner).astype(brain)
            dv = dot(probs.astype(brain), jnp.where(mine_low, grad[part, :], none_low))
            dk = dot(g_scores, jnp.where(mine_low, q[part, :], none_low))
            if start == 0 and head == 0:
                own_ref[0] = dk[:own]
                own_ref[1] = dv[:own]
                other_ref[0] = dk[own:]
                other_ref[1] = dv[own:]
            else:
                own_ref[0] += dk[:own]
                own_ref[1] += dv[:own]
                other_ref[0] += dk[own:]
                other_ref[1] += dv[own:]
            dq = jnp.where(mine, dot(k_turned, g_scores), dq)
        dq_ref[part, :] = (dq * scale).T
    own_ref[0] = own_ref[0] * scale
    other_ref[0] = other_ref[0] * scale


def attend_back(q, kv_own, kv_other, grad, logsum, heads, me, turns, tensors, after=()):
    own, wide = q.shape
    first = turns[0]
    count = len(turns)

    def tile(at, me):
        return (at + first) ^ (me[0] & (tensors - 1))

    own_spec = pl.BlockSpec((own, LANES), lambda at, me: (0, tile(at, me)))
    pair_spec = pl.BlockSpec((2, own, LANES), lambda at, me: (0, 0, tile(at, me)))
    one_shape = jax.ShapeDtypeStruct((own, count * LANES), single)
    one_out = pl.BlockSpec((own, LANES), lambda at, me: (0, at))
    pair_shape = jax.ShapeDtypeStruct((2, own, count * LANES), single)
    pair_out = pl.BlockSpec((2, own, LANES), lambda at, me: (0, 0, at))
    return pl.pallas_call(
        functools.partial(attend_back_kernel, heads, own, len(after)),
        grid_spec=pltpu.PrefetchScalarGridSpec(
            num_scalar_prefetch=1,
            grid=(count,),
            in_specs=[
                own_spec,
                pair_spec,
                pair_spec,
                own_spec,
                pl.BlockSpec((1, 8, own), lambda at, me: (tile(at, me), 0, 0)),
                *after_specs(after),
            ],
            out_specs=[one_out, pair_out, pair_out],
        ),
        out_shape=[one_shape, pair_shape, pair_shape],
        compiler_params=params(),
        name="attend_back",
    )(me, q, kv_own, kv_other, grad, logsum, *after)


def attention_out(mixed, resid, layer, places):
    parts = [
        dot(mixed[:, tile_lanes(place[1])], layer.out(place), 1, 1) for place in places
    ]
    return resid + add_up(parts)


def middle_kernel(
    feats, mixed_ref, resid_ref, w_ref, w_next_ref, norms_ref, cos_ref, sin_ref,
    mid_ref, next_ref, q_ref, kv_ref, w_held, w_semaphores,
):
    tiles = w_ref.shape[1]
    columns = w_held.shape[3]
    copies = [
        pltpu.make_async_copy(
            w_ref.at[:, :, :, first:last], w_held.at[:, :, :, first:last], w_semaphores.at[at]
        )
        for at, (first, last) in enumerate(((0, LANES), (LANES, columns)))
    ]
    for copy in copies:
        copy.start()
    copies[0].wait()
    layer = Layer(Gathered(w_held), 0, (columns - LANES) // 2)
    mid = attention_out(mixed_ref, resid_ref[...], layer, [place_of(at) for at in range(tiles)])
    mid_ref[...] = mid
    normed = feats.norm(mid, norms_ref[2:3], norms_ref[3:4])
    copies[1].wait()
    parts = []
    for at in range(tiles):
        act = gelu(dot(normed, layer.up(place_of(at)))).astype(brain)
        parts.append(dot(act, layer.down(place_of(at)), 1, 1))
    total = mid + add_up(parts)
    next_ref[...] = total
    normed = feats.norm(total, norms_ref[4:5], norms_ref[5:6])
    weights = Gathered(w_next_ref)
    cosine = cos_ref[...]
    sine = sin_ref[...]
    for at in range(tiles):
        lanes = slice(at * LANES, (at + 1) * LANES)
        rows = dot(normed, weights.block(place_of(at), 0, 3 * LANES))
        q_ref[:, lanes] = rotate(rows[:, :LANES], cosine, sine).astype(brain)
        kv_ref[0, :, lanes] = rotate(rows[:, LANES : 2 * LANES], cosine, sine).astype(brain)
        kv_ref[1, :, lanes] = rows[:, 2 * LANES :].astype(brain)


def middle(feats, mixed, resid, weights, columns, at_heads, norms, cosine, sine, after):
    own, wide = mixed.shape
    plain = jax.ShapeDtypeStruct(resid.shape, single)
    in_specs = [
        whole_spec(mixed.shape),
        whole_spec(resid.shape),
        *after_specs((weights,)),
        columns_spec(weights, 3 * LANES, at_heads),
        whole_spec(norms.shape),
        whole_spec(cosine.shape),
        whole_spec(sine.shape),
    ]
    outs = [
        plain,
        plain,
        jax.ShapeDtypeStruct((own, wide), brain),
        jax.ShapeDtypeStruct((2, own, wide), brain),
    ]
    ins = (mixed, resid, weights, weights, norms, cosine, sine)
    scratch = [
        pltpu.VMEM(weights.shape[:3] + (columns,), brain), pltpu.SemaphoreType.DMA((2,))
    ]
    kernel = functools.partial(middle_kernel, feats)
    return call(kernel, "middle", ins, in_specs, outs, scratch, after)


def feed_back(
    feats, turns, g_resid, mid, normed, mixed_ref, layer, gain, act_ref, slope_ref,
    grads, base, g_mid_ref, g_mixed_ref,
):
    hidden = layer.hidden
    g_low = g_resid.astype(brain)
    g_turned = g_low.T
    normed_turned = normed.T
    parts = []
    for turn, tile in turns:
        g_hidden = (dot(g_low, layer.down((turn, tile))) * slope_ref[turn]).astype(brain)
        grads.store(tile, turn, base + LANES + hidden, dot(g_turned, act_ref[turn]))
        grads.store(tile, turn, base + LANES, dot(normed_turned, g_hidden))
        parts.append(dot(g_hidden, layer.up((turn, tile)), 1, 1))
    grads.flush(range(1, len(grads.orders)))
    g_normed = add_up(parts)
    unit, inverse = feats.centred(mid)
    g_gain = jnp.sum(g_normed * unit, 0, keepdims=True)
    g_shift = jnp.sum(g_normed, 0, keepdims=True)
    g_mid = g_resid + feats.norm_back(unit, inverse, gain, g_normed)
    g_mid_ref[...] = g_mid
    g_low = g_mid.astype(brain)
    g_turned = g_low.T
    for turn, tile in turns:
        lanes = tile_lanes(tile)
        g_mixed_ref[:, lanes] = dot(g_low, layer.out((turn, tile))).astype(brain)
        grads.store(tile, turn, base, dot(g_turned, mixed_ref[:, lanes]))
    grads.flush([0])
    return g_gain, g_shift


def top_kernel(
    feats, cube, vocab_count, orders, grad_orders, me_ref, mixed_ref, resid_ref, w_own_ref,
    w_other_ref, norms_ref, vocab_ref, marks_ref, table_ref, keep_ref, send_ref, g_mid_ref, g_mixed_ref,
    g_norms_ref, g_vocab_ref, act_ref, slope_ref, keep_held, send_held, grad_semaphores,
    w_own_held, w_other_held, w_semaphores,
):
    me = me_ref[0]
    tiles = cube.tensors
    turns = [(turn, turn ^ (me & (tiles - 1))) for turn in range(tiles)]
    grads = Scattered(
        cube, me, (keep_held, send_held), (keep_ref, send_ref), grad_semaphores, grad_orders
    )
    copies = [
        [
            pltpu.make_async_copy(ref.at[part], held.at[part], w_semaphores.at[part, at])
            for at, (ref, held) in enumerate(((w_own_ref, w_own_held), (w_other_ref, w_other_held)))
        ]
        for part in range(len(orders))
    ]
    for part in copies:
        for copy in part:
            copy.start()
    for copy in copies[0]:
        copy.wait()
    layer = Layer(Relative(cube, me, (w_own_held, w_other_held), orders), 0, act_ref.shape[2])
    mid = attention_out(mixed_ref, resid_ref[...], layer, turns)
    normed = feats.norm(mid, norms_ref[6:7], norms_ref[7:8])
    for part in copies[1:]:
        for copy in part:
            copy.wait()
    parts = []
    for turn, tile in turns:
        hidden = dot(normed, layer.up((turn, tile)))
        share, bell = normal_share(hidden)
        act = (hidden * share).astype(brain)
        act_ref[turn] = act
        slope_ref[turn] = gelu_slope(hidden, share, bell)
        parts.append(dot(act, layer.down((turn, tile)), 1, 1))
    total = mid + add_up(parts)
    unit, inverse = feats.centred(total)
    gain = norms_ref[8:9]
    final = (unit * gain + norms_ref[9:10]).astype(brain)
    own = total.shape[0]
    marks = marks_ref[...].T.astype(jnp.int32)
    slots = marks.shape[0]
    slot = marks[:, 0:1]
    target = marks[:, 1:2]
    vocab = vocab_ref[...]
    where_hot = (lax.broadcasted_iota(jnp.int32, (slots, own), 1) == slot).astype(single)
    where_hot = where_hot.astype(brain)
    present = (slot >= 0).astype(single)
    picked = dot(where_hot, final).astype(brain)
    logits = dot(picked, vocab, 1, 1)
    lane = lax.broadcasted_iota(jnp.int32, logits.shape, 1)
    logits = jnp.where(lane < vocab_count, logits, -1e30)
    peak = jnp.max(logits, 1, keepdims=True)
    logsum = peak + jnp.log(jnp.sum(jnp.exp(logits - peak), 1, keepdims=True))
    target_hot = (lane == target).astype(single)
    target_logit = jnp.sum(
        jnp.where(lane < vocab_count, logits * target_hot, 0.0), 1, keepdims=True
    )
    loss = jnp.sum((logsum - target_logit) * present, 0, keepdims=True)
    share = present / table_ref[0, vocab_count : vocab_count + 1, 0:1]
    g_logits = ((jnp.exp(logits - logsum) - target_hot) * share).astype(brain)
    g_vocab_ref[...] = dot(g_logits, picked, 0, 0)[:TABLE_ROWS]
    g_picked = dot(g_logits, vocab)
    g_final = dot_exact(where_hot, g_picked, 0, 0)
    g_norms_ref[...] = jnp.zeros_like(g_norms_ref)
    g_norms_ref[8:9] = jnp.sum(g_final * unit, 0, keepdims=True)
    g_norms_ref[9:10] = jnp.sum(g_final, 0, keepdims=True)
    g_norms_ref[LOSS_ROW : LOSS_ROW + 1] = jnp.broadcast_to(loss, (1, g_norms_ref.shape[1]))
    g_resid = feats.norm_back(unit, inverse, gain, g_final)
    g_gain, g_shift = feed_back(
        feats, turns, g_resid, mid, normed, mixed_ref, layer, norms_ref[6:7], act_ref, slope_ref,
        grads, 0, g_mid_ref, g_mixed_ref,
    )
    g_norms_ref[6:7] = g_gain
    g_norms_ref[7:8] = g_shift
    grads.wait()


def top(
    feats, cube, orders, grad_orders, me, mixed, resid, w_own, w_other, norms, vocab,
    vocab_count, marks, table,
):
    own, wide = mixed.shape
    tiles = cube.tensors
    rows = w_own.shape[2]
    columns = w_own.shape[0] * w_own.shape[3] - 3 * LANES
    hidden = (columns - LANES) // 2
    pieces = len(grad_orders)
    grads = (pieces, cube.devices // 2, rows, columns // pieces)
    outs = [
        jax.ShapeDtypeStruct(grads, single),
        jax.ShapeDtypeStruct(grads, single),
        jax.ShapeDtypeStruct(resid.shape, single),
        jax.ShapeDtypeStruct(mixed.shape, brain),
        jax.ShapeDtypeStruct(norms.shape, single),
        jax.ShapeDtypeStruct((TABLE_ROWS, resid.shape[1]), single),
    ]
    in_specs = [
        scalar_spec(),
        whole_spec(mixed.shape),
        whole_spec(resid.shape),
        *after_specs((w_own, w_other)),
        whole_spec(norms.shape),
        whole_spec(vocab.shape),
        whole_spec(marks.shape),
        whole_spec(table.shape),
    ]
    scratch = [
        pltpu.VMEM((tiles, own, hidden), brain),
        pltpu.VMEM((tiles, own, hidden), single),
        pltpu.VMEM(grads, single),
        pltpu.VMEM(grads, single),
        pltpu.SemaphoreType.DMA((pieces, 2)),
        pltpu.VMEM(w_own.shape, brain),
        pltpu.VMEM(w_other.shape, brain),
        pltpu.SemaphoreType.DMA((w_own.shape[0], 2)),
    ]
    ins = (me, mixed, resid, w_own, w_other, norms, vocab, marks, table)
    kernel = functools.partial(top_kernel, feats, cube, vocab_count, orders, grad_orders)
    return call(kernel, "top", ins, in_specs, outs, scratch, (), 2)


def head_grads(turn, heads_refs, cosine, sine):
    dq_ref, own_ref, other_ref = heads_refs[3 * (turn // 2) : 3 * (turn // 2) + 3]
    lanes = tile_lanes(turn % 2)
    other = tile_lanes(1 - turn % 2)
    g_q = unrotate(dq_ref[:, lanes], cosine, sine)
    g_k = unrotate(own_ref[0, :, lanes] + other_ref[0, :, other], cosine, sine)
    g_v = own_ref[1, :, lanes] + other_ref[1, :, other]
    return jnp.concatenate([g_q, g_k, g_v], 1).astype(brain)


def lower_kernel(feats, cube, grad_orders, me_ref, *refs):
    heads_refs = refs[:6]
    (
        g_mid_in_ref, resid_ref, mid_ref, mixed_ref, w_in_ref, w_ref, norms_ref, cos_ref, sin_ref,
        g_norms_in_ref, keep_ref, send_ref, g_mid_ref, g_mixed_ref, g_norms_ref,
        act_ref, slope_ref, keep_held, send_held, grad_semaphores, w_held, w_semaphore,
    ) = refs[6:]
    copy = pltpu.make_async_copy(w_ref.at[:, :, :, : w_held.shape[3]], w_held, w_semaphore)
    copy.start()
    me = me_ref[0]
    tiles = cube.tensors
    turns = [(turn, turn ^ (me & (tiles - 1))) for turn in range(tiles)]
    layer = Layer(Gathered(w_held), 0, act_ref.shape[2])
    weights = Gathered(w_in_ref)
    grads = Scattered(
        cube, me, (keep_held, send_held), (keep_ref, send_ref), grad_semaphores, grad_orders
    )
    unit, inverse = feats.centred(resid_ref[...])
    gain = norms_ref[4:5]
    normed_turned = (unit * gain + norms_ref[5:6]).astype(brain).T
    cosine = cos_ref[...]
    sine = sin_ref[...]
    parts = []
    for turn, tile in turns:
        g_heads = head_grads(turn, heads_refs, cosine, sine)
        grads.store(tile, turn, 0, dot(normed_turned, g_heads))
        parts.append(dot(g_heads, weights.block((turn, tile), 0, 3 * LANES), 1, 1))
    g_normed = add_up(parts)
    g_norms_ref[...] = g_norms_in_ref[...]
    g_norms_ref[4:5] = jnp.sum(g_normed * unit, 0, keepdims=True)
    g_norms_ref[5:6] = jnp.sum(g_normed, 0, keepdims=True)
    g_resid = g_mid_in_ref[...] + feats.norm_back(unit, inverse, gain, g_normed)
    mid = mid_ref[...]
    normed = feats.norm(mid, norms_ref[2:3], norms_ref[3:4])
    copy.wait()
    for turn, tile in turns:
        hidden = dot(normed, layer.up((turn, tile)))
        share, bell = normal_share(hidden)
        act_ref[turn] = (hidden * share).astype(brain)
        slope_ref[turn] = gelu_slope(hidden, share, bell)
    g_gain, g_shift = feed_back(
        feats, turns, g_resid, mid, normed, mixed_ref, layer, norms_ref[2:3], act_ref, slope_ref,
        grads, 3 * LANES, g_mid_ref, g_mixed_ref,
    )
    g_norms_ref[2:3] = g_gain
    g_norms_ref[3:4] = g_shift
    grads.wait()


def lower(
    feats, cube, grad_orders, me, head_parts, g_mid, resid, mid, mixed, weights, at_heads,
    feed_columns, norms, cosine, sine, g_norms, after,
):
    own, wide = mixed.shape
    tiles = cube.tensors
    rows = weights.shape[2]
    hidden = (feed_columns - LANES) // 2
    columns = feed_columns + 3 * LANES
    count = len(grad_orders)
    grads = (count, cube.devices // 2, rows, columns // count)
    outs = [
        jax.ShapeDtypeStruct(grads, single),
        jax.ShapeDtypeStruct(grads, single),
        jax.ShapeDtypeStruct(resid.shape, single),
        jax.ShapeDtypeStruct(mixed.shape, brain),
        jax.ShapeDtypeStruct(norms.shape, single),
    ]
    before = (*head_parts, g_mid, resid, mid, mixed)
    rest = (norms, cosine, sine, g_norms)
    in_specs = [
        scalar_spec(),
        *[whole_spec(x.shape) for x in before],
        columns_spec(weights, 3 * LANES, at_heads),
        *after_specs((weights,)),
        *[whole_spec(x.shape) for x in rest],
    ]
    scratch = [
        pltpu.VMEM((tiles, own, hidden), brain),
        pltpu.VMEM((tiles, own, hidden), single),
        pltpu.VMEM(grads, single),
        pltpu.VMEM(grads, single),
        pltpu.SemaphoreType.DMA((count, 2)),
        pltpu.VMEM(weights.shape[:3] + (feed_columns,), brain),
        pltpu.SemaphoreType.DMA,
    ]
    ins = (me, *before, weights, weights, *rest)
    kernel = functools.partial(lower_kernel, feats, cube, grad_orders)
    return call(kernel, "lower", ins, in_specs, outs, scratch, after, 2)


def stacked_lanes(ref, row, value):
    rows = value.shape[0]
    for at in range(value.shape[1] // LANES):
        ref[row : row + rows, :] = value[:, at * LANES : (at + 1) * LANES]
        row += rows
    return row


def side_by_side(x, rows):
    return jnp.concatenate([x[at : at + rows] for at in range(0, x.shape[0], rows)], 1)


def bottom_kernel(
    feats, cube, orders, me_ref, *refs
):
    heads_refs = refs[:6]
    (
        g_mid_ref, ids_ref, w_own_ref, w_other_ref, norms_ref, vocab_ref, g_vocab_in_ref, g_norms_in_ref, cos_ref,
        sin_ref, keep_ref, send_ref, norms_out_ref,
    ) = refs[6:]
    tiles = cube.tensors
    own = g_mid_ref.shape[0]
    mine = me_ref[0] & (tiles - 1)
    hot = lax.broadcasted_iota(jnp.int32, (TABLE_ROWS, own), 0) == ids_ref[...]
    hot = hot.astype(single).astype(brain)
    cosine = cos_ref[...]
    sine = sin_ref[...]
    weights = Relative(cube, me_ref[0], (w_own_ref, w_other_ref), orders)
    first = w_own_ref.shape[-1] - 3 * LANES
    refs = (keep_ref, send_ref)
    rows = [0, 0]
    parts = []
    for turn in range(tiles):
        tile = turn ^ mine
        g_table = dot(hot, head_grads(turn, heads_refs, cosine, sine))
        rows[turn & 1] = stacked_lanes(refs[turn & 1], rows[turn & 1], g_table)
        weight = weights.block((turn, tile), first, first + 3 * LANES)
        high, middle_part, low = split_three(g_table)
        parts.append(dot(high, weight, 1, 1))
        parts.append(dot(middle_part, weight, 1, 1))
        parts.append(dot(low, weight, 1, 1))
    g_normed = add_up(parts)
    unit, inverse = feats.centred(vocab_ref[...].astype(single)[:TABLE_ROWS])
    norms_out_ref[...] = g_norms_in_ref[...]
    norms_out_ref[0:1] = jnp.sum(g_normed * unit, 0, keepdims=True)
    norms_out_ref[1:2] = jnp.sum(g_normed, 0, keepdims=True)
    g_norms = norms_out_ref[...]
    g_rows = feats.norm_back(unit, inverse, norms_ref[0:1], g_normed)
    g_vocab = g_vocab_in_ref[...] + (dot_exact(hot, g_mid_ref[...]) + g_rows)
    for ref, row in zip(refs, rows):
        row = stacked_lanes(ref, row, g_vocab)
        stacked_lanes(ref, row, g_norms)


def last_part(weights):
    parts = weights.shape[0]
    return pl.BlockSpec((1,) + weights.shape[1:], lambda at: (parts - 1, 0, 0, 0))


def bottom(
    feats, cube, orders, me, head_parts, g_mid, ids, w_own, w_other, norms, vocab, g_vocab,
    g_norms, cosine, sine, after,
):
    tiles = cube.tensors
    table_rows = 3 * TABLE_ROWS * tiles // 2
    vector_rows = (g_vocab.shape[0] + g_norms.shape[0]) * g_vocab.shape[1] // LANES
    out = jax.ShapeDtypeStruct((table_rows + vector_rows, LANES), single)
    before = (*head_parts, g_mid, ids)
    rest = (norms, vocab, g_vocab, g_norms, cosine, sine)
    in_specs = [
        scalar_spec(),
        *[whole_spec(x.shape) for x in before],
        last_part(w_own),
        last_part(w_other),
        *[whole_spec(x.shape) for x in rest],
    ]
    outs = [out, out, jax.ShapeDtypeStruct(norms.shape, single)]
    ins = (me, *before, w_own, w_other, *rest)
    kernel = functools.partial(bottom_kernel, feats, cube, orders[-1:])
    return call(kernel, "bottom", ins, in_specs, outs, (), after)[:2]


def send_kernel(count, skip, keep_ref, got_ref, *refs):
    outs = refs[skip:]
    for part in range(count):
        outs[part][...] = keep_ref[part] + got_ref[part]


def send_upper(keep, got, through, after):
    count, size, rows, wide = keep.shape
    half = size // 2
    step = rows // 2
    upper = pl.BlockSpec((count, half, step, wide), lambda at: (0, 1, at, 0))
    out = jax.ShapeDtypeStruct((half, rows, wide), single)
    results = pl.pallas_call(
        functools.partial(send_kernel, count, len(through) + len(after)),
        grid=(rows // step,),
        in_specs=[upper, upper, *after_specs(through), *after_specs(after)],
        out_specs=[
            *[pl.BlockSpec((half, step, wide), lambda at: (0, at, 0))] * count,
            *after_specs(through),
        ],
        out_shape=[
            *[out] * count,
            *[jax.ShapeDtypeStruct(x.shape, x.dtype) for x in through],
        ],
        input_output_aliases={2 + at: count + at for at in range(len(through))},
        compiler_params=params(),
        name="send_upper",
    )(keep, got, *through, *after)
    return results[:count], results[count:]


def halve_kernel(count, together, stacked, keeps, skip, *refs):
    held = refs[:keeps]
    got_count = 1 if together else count
    got = refs[keeps : keeps + got_count]
    outs = refs[keeps + got_count + skip :]
    size = held[0].shape[1]
    half = size // 2
    for part in range(count):
        arrived = got[0].at[part] if together else got[part]

        def total(rows):
            return add_up([x[part, rows] for x in held]) + arrived[rows]

        if size == 1:
            outs[0][part] = total(slice(0, 1))
        else:
            outs[0][part] = total(slice(0, half))
            send = outs[1].at[part] if stacked else outs[1 + part]
            send[...] = total(slice(half, size))


def halve(keeps, got, through=(), after=(), stacked=False):
    together = not isinstance(got, list)
    got = [got] if together else got
    count, _, rows, wide = keeps[0].shape
    size = got[0].shape[-3]
    step = rows // 2 if size >= 8 else rows
    half = max(size // 2, 1)

    def spec(*lead):
        return pl.BlockSpec((*lead, step, wide), lambda at: (*([0] * len(lead)), at, 0))

    outs = [jax.ShapeDtypeStruct((count, half, rows, wide), single)]
    out_specs = [spec(count, half)]
    if size > 1 and stacked:
        outs += outs
        out_specs += out_specs
    elif size > 1:
        outs += [jax.ShapeDtypeStruct((half, rows, wide), single)] * count
        out_specs += [spec(half)] * count
    sends = len(outs) - 1
    got_specs = [spec(count, size)] if together else [spec(size)] * count
    ins = (*keeps, *got)
    aliases = {len(ins) + at: len(outs) + at for at in range(len(through))}
    outs += [jax.ShapeDtypeStruct(x.shape, x.dtype) for x in through]
    skip = len(through) + len(after)
    results = pl.pallas_call(
        functools.partial(halve_kernel, count, together, stacked, len(keeps), skip),
        grid=(rows // step,),
        in_specs=[
            *[spec(count, size)] * len(keeps),
            *got_specs,
            *after_specs(through),
            *after_specs(after),
        ],
        out_specs=[*out_specs, *after_specs(through)],
        out_shape=outs,
        input_output_aliases=aliases,
        compiler_params=params(),
        name="halve",
    )(*ins, *through, *after)
    going = results[1] if stacked and sends else results[1 : 1 + sends]
    return results[0], going, results[1 + sends :]


def join_kernel(count, together, stacked, skip, *refs):
    ins = 1 if together else count
    helds, gots = refs[:ins], refs[ins : 2 * ins]
    outs = refs[2 * ins + skip :]
    for part in range(count):
        held = helds[0].at[part] if together else helds[part]
        got = gots[0].at[part] if together else gots[part]
        out = outs[0].at[part] if stacked else outs[part]
        size = held.shape[0]
        out[:size] = held[...]
        out[size:] = got[...]


def join(held, got, count, stacked, through=(), after=()):
    together = not isinstance(held, list)
    ins = (held, got) if together else (*held, *got)
    size, rows, wide = ins[0].shape[-3:]
    shape = (2 * size, rows, wide)
    if stacked:
        outs = [jax.ShapeDtypeStruct((count,) + shape, ins[0].dtype)]
    else:
        outs = [jax.ShapeDtypeStruct(shape, ins[0].dtype)] * count
    aliases = {len(ins) + at: len(outs) + at for at in range(len(through))}
    skip = len(through) + len(after)
    results = pl.pallas_call(
        functools.partial(join_kernel, count, together, stacked, skip),
        grid=(1,),
        in_specs=[
            *[whole_spec(x.shape) for x in ins], *after_specs(through), *after_specs(after)
        ],
        out_specs=[*[whole_spec(out.shape) for out in outs], *after_specs(through)],
        out_shape=[*outs, *[jax.ShapeDtypeStruct(x.shape, x.dtype) for x in through]],
        input_output_aliases=aliases,
        compiler_params=params(),
        name="join",
    )(*ins, *through, *after)
    joined = results[0] if stacked else list(results[:count])
    return joined, results[len(outs) :]


def wait_kernel(*refs):
    pass


def wait_for(x, after):
    return pl.pallas_call(
        wait_kernel,
        in_specs=after_specs((x, *after)),
        out_specs=after_specs((x,))[0],
        out_shape=jax.ShapeDtypeStruct(x.shape, x.dtype),
        input_output_aliases={0: 0},
        compiler_params=params(),
        name="wait_for",
    )(x, *after)


class Gather:
    def __init__(self, cube, parts):
        count = len(parts)
        self.cube = cube
        self.count = count
        turning = [cube.outer(turn)[:-1] for turn in range(count)]
        self.orders = [[cube.size - 1] + turns for turns in turning]
        self.held = jnp.stack(parts)[:, None]
        self.got = cube.swap(self.held, cube.size - 1)
        self.at = 1

    def step(self, through=(), after=()):
        last = self.at == len(self.orders[0])
        self.held, through = join(self.held, self.got, self.count, last, through, after)
        if not last:
            self.got = [
                self.cube.swap(x, order[self.at]) for x, order in zip(self.held, self.orders)
            ]
        self.at += 1
        return through

    def finish(self, after):
        self.held = wait_for(self.held, after)
        self.got = self.cube.swap(self.held, 0)


def normalize_features(resid, gain, shift):
    centre = resid - jnp.mean(resid, -1, keepdims=True)
    spread = jnp.mean(centre * centre, -1, keepdims=True)
    return centre * lax.rsqrt(spread + norm_eps) * gain + shift


def adamw(master, first, second, grad, step_rate):
    mean = beta_first * first + (1.0 - beta_first) * grad
    square = beta_second * second + (1.0 - beta_second) * grad * grad
    corrected = mean / (1.0 - beta_first**STEP)
    rescaled_values = square / (1.0 - beta_second**STEP)
    fresh = master - step_rate * (
        corrected / (jnp.sqrt(rescaled_values) + adam_eps) + weight_decay * master
    )
    return (fresh, mean, square)


def pad_lanes(x, lanes):
    return jnp.pad(x, [(0, 0)] * (x.ndim - 1) + [(0, lanes - x.shape[-1])])


def make_shards(groups, tensors):
    axes = ("dp", "tensor")
    cube = Cube(groups, tensors)

    def shards(
        token_ids,
        mask_pos,
        mask_target,
        mask_count,
        weight_in,
        weight_out,
        weight_up,
        weight_down,
        norm_params,
        vocab_table,
        first_in,
        first_out,
        first_up,
        first_down,
        first_norm,
        first_vocab,
        second_in,
        second_out,
        second_up,
        second_down,
        second_norm,
        second_vocab,
    ):
        layers, block, in_wide = weight_in.shape
        heads = in_wide // (3 * HEAD)
        per_heads = heads * HEAD
        hidden = weight_up.shape[2]
        hidden_padded = -(-hidden // LANES) * LANES
        vocab_count, width = vocab_table.shape
        feats = Features(width, groups)
        local_len = token_ids.shape[1]
        length = local_len * tensors
        own = length // 2
        here = lax.axis_index("tensor")
        group_at = lax.axis_index("dp")
        me = (group_at * tensors + here).astype(jnp.int32).reshape(1)
        sequence = here // 2
        quarters = jnp.stack([here, here ^ 2, here ^ 1, here ^ 3])

        heads_in = weight_in.astype(brain).transpose(1, 0, 2)
        heads_in = heads_in.reshape(block, layers, heads, 3, HEAD).transpose(0, 1, 3, 2, 4)
        heads_in = pad_lanes(heads_in.reshape(block, layers, 3, per_heads), LANES)
        heads_in = heads_in.reshape(block, layers, 3 * LANES)
        feed = jnp.concatenate(
            [
                pad_lanes(weight_out.astype(brain).transpose(2, 0, 1), LANES),
                pad_lanes(weight_up.astype(brain).transpose(1, 0, 2), hidden_padded),
                pad_lanes(weight_down.astype(brain).transpose(2, 0, 1), hidden_padded),
            ],
            2,
        )
        feed_columns = feed.shape[2]

        def pad_rows(x):
            return jnp.pad(x, ((0, feats.padded - block), (0, 0)))

        vocab_low = vocab_table.astype(brain)
        vocab_padded = jnp.pad(feats.pad(vocab_low), ((0, 64 - vocab_count), (0, 0)))
        norms = jnp.pad(feats.pad(norm_params), ((0, 16 - norm_params.shape[0]), (0, 0)))

        def gather_all(x):
            x = lax.all_gather(x, axes, axis=0, tiled=False)
            return x.reshape((groups, tensors) + x.shape[1:])

        weights = gather_all(pad_rows(jnp.concatenate([feed[:, 0], heads_in[:, 1]], 1)))
        at_heads = feed_columns // (3 * LANES)
        later = pad_rows(jnp.concatenate([feed[:, 1], heads_in[:, 0]], 1))
        third = later.shape[1] // 3
        gather = Gather(cube, [later[:, at : at + third] for at in range(0, 3 * third, third)])

        table_low = normalize_features(
            lax.reduce_precision(vocab_table, 8, 7), norm_params[0], norm_params[1]
        ).astype(brain)
        table_own = lax.dynamic_slice_in_dim(
            table_low.reshape(vocab_count, groups, block), group_at, 1, 1
        )[:, 0]
        table = dot(table_own, heads_in[:, 0])
        extra = jnp.zeros((TABLE_ROWS - vocab_count, 3 * LANES), single)
        extra = extra.at[0, 0].set(jnp.sum(mask_count).astype(single))
        table = jnp.concatenate([table, extra], 0)
        for at in range(2, cube.size):
            table = table + cube.swap(table, at)
        count_total = table[vocab_count, 0]
        ids_row = vocab_count + 1
        table = lax.dynamic_update_slice(
            table, pad_lanes(token_ids.astype(single), 3 * LANES), (ids_row, 0)
        )
        got = cube.swap(table, 1)
        upper = (here & 2) == 2
        pair = jnp.stack([jnp.where(upper, got, table), jnp.where(upper, table, got)])
        got = cube.swap(pair, 0)
        upper = (here & 1) == 1
        table = jnp.stack([jnp.where(upper, got, pair), jnp.where(upper, pair, got)], 1)
        table = table.reshape(tensors, TABLE_ROWS, 3 * LANES)
        ids = jnp.take(table[:, ids_row : ids_row + 2, :local_len], sequence, axis=1)
        ids = jnp.take(ids, quarters, axis=0).reshape(1, length).astype(jnp.int32)

        half = HEAD // 2
        freqs = 10000.0 ** (-jnp.arange(half, dtype=single) * 2.0 / HEAD)
        positions = (quarters[:, None] * local_len + jnp.arange(local_len)[None, :]).reshape(length)
        angles = positions.astype(single)[:, None] * freqs[None, :]
        cosine, sine = (jnp.cos(angles), jnp.sin(angles))
        cosine = pad_lanes(jnp.tile(jnp.concatenate([cosine, cosine], 1), (1, heads)), LANES)
        sine = pad_lanes(jnp.tile(jnp.concatenate([-sine, sine], 1), (1, heads)), LANES)
        cos_own, sin_own = (cosine[:own], sine[:own])

        slots = mask_pos.shape[1]
        my_pos = jnp.take(mask_pos, sequence, axis=0)
        my_count = jnp.take(mask_count, sequence, axis=0)
        quarter = my_pos // local_len
        inside = my_pos % local_len
        slot = jnp.where(
            quarter == here, inside, jnp.where(quarter == (here ^ 2), inside + local_len, -1)
        )
        slot = jnp.where(jnp.arange(slots) < my_count, slot, -1)
        target = jnp.take(mask_target, sequence, axis=0)
        marks = jnp.zeros((8, slots), jnp.int32).at[0].set(slot).at[1].set(target)
        marks = marks.astype(single)

        gather.step((), (table,))
        q_low, kv_low, kv_low_other, resid_low = embed(table, ids, vocab_padded, cosine, sine, ())
        while gather.at + 2 < cube.size:
            gather.step((), (q_low,))
        mixed_low, logsum_low = attend(q_low, kv_low, kv_low_other, heads)
        gather.step((), (logsum_low,))
        mid_low, resid, q, kv = middle(
            feats, mixed_low, resid_low, weights, feed_columns, at_heads, norms, cos_own, sin_own,
            (),
        )
        (kv,) = gather.step((kv,), (resid,))
        kv_other = cube.swap(kv, 0)
        gather.finish((kv_other,))
        mixed, logsum = attend(q, kv, kv_other, heads)
        grad_orders = [cube.outer(turn) for turn in range(3)]

        last_step = cube.size - 2

        class Sums:
            def __init__(self, keep, send):
                self.keeps = (keep,)
                self.got = cube.swap(send, 0)
                self.at = 0

            def step(self, through=(), after=()):
                stacked = self.at == last_step
                if self.at == 0:
                    sends, through = send_upper(*self.keeps, self.got, through, after)
                    self.keeps = (*self.keeps, self.got)
                    self.done = sends[0]
                else:
                    keep, sends, through = halve(self.keeps, self.got, through, after, stacked)
                    self.keeps = (keep,)
                    self.done = keep
                if stacked:
                    self.got = cube.swap(sends, grad_orders[0][-1])
                else:
                    self.got = [
                        cube.swap(x, order[self.at]) for x, order in zip(sends, grad_orders)
                    ]
                self.at += 1
                return through

            def finish(self, through=(), after=()):
                keep, _, through = halve(self.keeps, self.got, through, after)
                return keep[:, 0], through

        def exchange(arrays):
            return [cube.swap(x, 0) for x in arrays]

        first_turns = list(range(tensors // 2))
        last_turns = list(range(tensors // 2, tensors))
        keep, send, g_mid, g_mixed, g_norms, g_vocab = top(
            feats, cube, gather.orders, grad_orders, me, mixed, resid, gather.held, gather.got,
            norms, vocab_padded, vocab_count, marks, table,
        )
        sums_top = Sums(keep, send)
        part = (q, kv, kv_other, g_mixed, logsum, heads, me)
        first = attend_back(*part, first_turns, tensors)
        got_first = exchange(sums_top.step(first[2:], (first[0],)))
        last = attend_back(*part, last_turns, tensors, (sums_top.done,))
        got_last = exchange(sums_top.step(last[2:], (last[0],)))
        head_parts = (*first[:2], *got_first, *last[:2], *got_last)
        keep, send, g_mid, g_mixed, g_norms = lower(
            feats, cube, grad_orders, me, head_parts, g_mid, resid, mid_low, mixed_low, weights,
            at_heads, feed_columns, norms, cos_own, sin_own, g_norms, (sums_top.done,),
        )
        (send,) = sums_top.step((send,), (g_mid,))
        sums_low = Sums(keep, send)
        part = (q_low, kv_low, kv_low_other, g_mixed, logsum_low, heads, me)
        first = attend_back(*part, first_turns, tensors, (sums_top.done,))
        got_first = exchange(sums_top.step(first[2:], (first[0],)))
        sums_low.step((), (sums_top.done,))
        last = attend_back(*part, last_turns, tensors, (sums_low.done,))
        got_last = exchange(sums_low.step(last[2:], (last[0],)))
        head_parts = (*first[:2], *got_first, *last[:2], *got_last)
        keep_table, send_table = bottom(
            feats, cube, gather.orders, me, head_parts, g_mid, ids[:, :own], gather.held,
            gather.got, norms, vocab_padded, g_vocab, g_norms, cos_own, sin_own, (sums_low.done,),
        )
        got = cube.swap(send_table, 0)
        (keep_table,) = sums_low.step((keep_table,))
        total = keep_table + got
        tile_rows = 3 * TABLE_ROWS
        got = cube.swap(total[tile_rows:], 1)
        (total,) = sums_low.step((total,))
        total = jnp.concatenate(
            [total[:tile_rows] + got[:tile_rows], total[2 * tile_rows :] + got[tile_rows:]], 0
        )
        done = 2
        if cube.size > 4:
            near, far, both = cube.swap(total, 2), cube.swap(total, 3), cube.swap(total, 2, 3)
            total = (total + near) + (far + both)
            done = 4
        for at in range(done, cube.size):
            total = total + cube.swap(total, at)
        while sums_low.at <= last_step:
            sums_low.step()
        while sums_top.at <= last_step:
            sums_top.step((), (keep_table,))
        grads_low, _ = sums_low.finish()
        grads_top, _ = sums_top.finish((), (sums_low.done,))
        grads_top = jnp.concatenate(list(grads_top), 1)
        grads_low = jnp.concatenate(list(grads_low), 1)
        g_table = side_by_side(total[:tile_rows], TABLE_ROWS)[:vocab_count]
        vocab_rows = TABLE_ROWS * feats.total // LANES
        g_vocab = side_by_side(total[tile_rows : tile_rows + vocab_rows], TABLE_ROWS)
        g_vocab = feats.unpad(g_vocab[:vocab_count])
        g_norms = side_by_side(total[tile_rows + vocab_rows :], norms.shape[0])
        loss_total = g_norms[LOSS_ROW, 0]
        g_norms = feats.unpad(g_norms[: norm_params.shape[0]])
        grads_in_low = lax.dot_general(
            table_own.astype(single),
            g_table,
            (((0,), (0,)), ((), ())),
            precision=highest,
            preferred_element_type=single,
        )

        def unpack_in(grad):
            grad = grad[:block].reshape(block, 3, LANES)[:, :, :per_heads]
            return grad.reshape(block, 3, heads, HEAD).transpose(0, 2, 1, 3).reshape(block, in_wide)

        low_start = 3 * LANES
        start = LANES + hidden_padded
        grad_in = jnp.stack([unpack_in(grads_in_low), unpack_in(grads_low[:, :low_start])], 1)
        both = jnp.stack([grads_low[:block, low_start:], grads_top[:block]], 1)
        grads = (
            grad_in,
            both[:, :, :per_heads],
            both[:, :, LANES : LANES + hidden],
            both[:, :, start : start + hidden],
            g_norms,
            g_vocab,
        )
        by_rows = Layout(major_to_minor=(0, 1, 2))
        grads = [with_layout_constraint(x, by_rows) for x in grads[:4]] + list(grads[4:])
        turned = [(1, 0, 2), (2, 0, 1), (1, 0, 2), (2, 0, 1), None, None]
        turned_back = [(1, 0, 2), (1, 2, 0), (1, 0, 2), (1, 2, 0), None, None]

        def turn_all(arrays, orders):
            return [x if order is None else x.transpose(order) for x, order in zip(arrays, orders)]

        masters = (weight_in, weight_out, weight_up, weight_down, norm_params, vocab_table)
        firsts = (first_in, first_out, first_up, first_down, first_norm, first_vocab)
        seconds = (second_in, second_out, second_up, second_down, second_norm, second_vocab)
        masters, firsts, seconds = [turn_all(x, turned) for x in (masters, firsts, seconds)]
        results = [
            adamw(masters[which], firsts[which], seconds[which], grads[which], step_rates[which])
            for which in range(6)
        ]
        news, means, squares = [
            turn_all([entry[which] for entry in results], turned_back) for which in range(3)
        ]
        copies = [news[which].astype(brain) for which in (0, 1, 2, 3, 5)]
        return (loss_total, count_total, *news, *means, *squares, *copies)

    return shards


def solution(mesh):
    rows_in = P(None, "dp", "tensor")
    rows_out = P(None, "tensor", "dp")
    six = (rows_in, rows_out, rows_in, rows_out, P(), P())
    five = (rows_in, rows_out, rows_in, rows_out, P())
    return jax.shard_map(
        make_shards(mesh.shape["dp"], mesh.shape["tensor"]),
        mesh=mesh,
        in_specs=(P("dp", "tensor"), P("dp", None), P("dp", None), P("dp"), *six, *six, *six),
        out_specs=(P(), P(), *six, *six, *six, *five),
        check_vma=False,
    )
```
